32 devices in a mesh: dp: 4 (over y, core), fsdp: 8 (over z, x).
Axes of the slice: x: 2, y: 2, z: 4, core: 2. Of those that a mesh axis runs over, the one named last changes fastest.
Arguments:
- images: bfloat16 [256, 14, 14, 512], P(('dp', 'fsdp')), may hold values from -6 to 6
- input_gain: bfloat16 [512], P('fsdp'), may hold values from 0.099609375 to 1.8984375
- input_shift: bfloat16 [512], P('fsdp'), may hold values from -4 to 4
- attend_weight: bfloat16 [512, 1536], P('fsdp'), may hold values from -0.25 to 0.25
- attend_bias: bfloat16 [1536], P('fsdp'), may hold values from -4 to 4
- output_weight: bfloat16 [512, 512], P('fsdp'), may hold values from -2 to 2
- output_bias: bfloat16 [512], P('fsdp'), may hold values from -4 to 4
- second_gain: bfloat16 [512], P('fsdp'), may hold values from 0.099609375 to 1.8984375
- second_shift: bfloat16 [512], P('fsdp'), may hold values from -4 to 4
- expand_weight: bfloat16 [512, 2048], P('fsdp'), may hold values from -0.25 to 0.25
- expand_bias: bfloat16 [2048], P('fsdp'), may hold values from -4 to 4
- reduce_weight: bfloat16 [2048, 512], P('fsdp'), may hold values from -0.125 to 0.125
- reduce_bias: bfloat16 [512], P('fsdp'), may hold values from -4 to 4
- position_table: bfloat16 [169, 16], replicated, may hold values from -4 to 4
- region_labels: int32 [14, 14], replicated, may hold values from 0 to 3
- position_index: int32 [49, 49], replicated, may hold values from 0 to 168
- cotangent: bfloat16 [256, 14, 14, 512], P(('dp', 'fsdp')), may hold values from -6 to 6
Outputs:
- block_out: bfloat16 [256, 14, 14, 512], P(('dp', 'fsdp'))
- images_grad: bfloat16 [256, 14, 14, 512], P(('dp', 'fsdp'))
- input_gain_grad: float32 [512], P('fsdp')
- input_shift_grad: float32 [512], P('fsdp')
- attend_weight_grad: float32 [512, 1536], P('fsdp')
- attend_bias_grad: float32 [1536], P('fsdp')
- output_weight_grad: float32 [512, 512], P('fsdp')
- output_bias_grad: float32 [512], P('fsdp')
- second_gain_grad: float32 [512], P('fsdp')
- second_shift_grad: float32 [512], P('fsdp')
- expand_weight_grad: float32 [512, 2048], P('fsdp')
- expand_bias_grad: float32 [2048], P('fsdp')
- reduce_weight_grad: float32 [2048, 512], P('fsdp')
- reduce_bias_grad: float32 [512], P('fsdp')
- position_table_grad: float32 [169, 16], replicated
The draws below stay inside these ranges and needn't reach their ends.
All inputs are finite; a program needn't handle non-finite values.
Results may differ from the reference program's by a relative error of at most 0.017.
Values may be sent and summed in bfloat16 or wider, within the bound.
No kernel may reach another device: no remote copies, remote signals or barrier semaphores. Data moves between devices by JAX's collectives and lax.ppermute only.
A program may use at most 192 MiB of HBM per device.

```python
import jax
import jax.numpy as jnp
from jax import lax

D = 512
HEADS = 16
HEAD_DIM = 32
FF = 2048
WIN = 7
RES = 14
SHIFT = 3
WIN2 = 49
RELS = 169
IMAGES = 256


def set_ends(values, stream_key, low, largest):
    longest = values.shape.index(max(values.shape))
    spots = []
    for shift in (0, 1):
        where = [jax.random.randint(jax.random.fold_in(stream_key, axis), (), 0, length) for axis, length in enumerate(values.shape)]
        where[longest] = (where[longest] + shift) % values.shape[longest]
        spots.append(tuple(where))
    return values.at[spots[0]].set(low).at[spots[1]].set(largest)


def block_scale(rng, shape, cuts, least, largest):
    level, own = 1.0, jax.random.fold_in(rng, 6)
    for axis_at, shards_of in cuts:
        heights = jnp.exp(jax.random.uniform(jax.random.fold_in(own, axis_at), (shards_of,), jnp.float32, least / len(cuts), largest / len(cuts)))
        level = level * jnp.repeat(heights, shape[axis_at] // shards_of).reshape([-1 if axis == axis_at else 1 for axis in range(len(shape))])
    return level


def bell_draw(own_key, shape, scale, most, pieces=(), kind=jnp.bfloat16):
    factor_of = block_scale(own_key, shape, pieces, -0.22, 0.18) if pieces else 1.0
    entries = jax.random.normal(own_key, shape, jnp.float32) * scale * factor_of
    return jnp.minimum(jnp.maximum(entries, -most), most).astype(kind)


def setup_inputs(seed: int = 0) -> dict:
    keys = jax.random.split(jax.random.key(seed), 18)
    return {
        "images": bell_draw(keys[0], (IMAGES, RES, RES, D), 1.0, 6.0, ((0, 32),)),
        "input_gain": jnp.clip(1.0 + 0.18 * jax.random.normal(keys[1], (D,), jnp.float32), 0.099609375, 1.8984375).astype(jnp.bfloat16),
        "input_shift": bell_draw(keys[2], (D,), 0.3, 4.0, ((0, 8),)),
        "attend_weight": bell_draw(keys[3], (D, 3 * D), D ** -0.5, 0.25, ((0, 8),)),
        "attend_bias": bell_draw(keys[4], (3 * D,), 0.3, 4.0, ((0, 8),)),
        "output_weight": bell_draw(keys[5], (D, D), (max(D // WIN2, 1)) ** -0.5, 2.0, ((0, 8),)),
        "output_bias": bell_draw(keys[6], (D,), 0.3, 4.0, ((0, 8),)),
        "second_gain": jnp.clip(1.0 + 0.18 * jax.random.normal(keys[7], (D,), jnp.float32), 0.099609375, 1.8984375).astype(jnp.bfloat16),
        "second_shift": bell_draw(keys[8], (D,), 0.3, 4.0, ((0, 8),)),
        "expand_weight": bell_draw(keys[9], (D, FF), D ** -0.5, 0.25, ((0, 8),)),
        "expand_bias": bell_draw(keys[10], (FF,), 0.3, 4.0, ((0, 8),)),
        "reduce_weight": bell_draw(keys[11], (FF, D), FF ** -0.5, 0.125, ((0, 8),)),
        "reduce_bias": bell_draw(keys[12], (D,), 0.3, 4.0, ((0, 8),)),
        "position_table": bell_draw(keys[13], (RELS, HEADS), 1.0, 4.0),
        "region_labels": set_ends(jax.random.randint(keys[14], (RES, RES), 0, 4), jax.random.fold_in(keys[14], 1), 0, 3).astype(jnp.int32),
        "position_index": set_ends(jax.random.randint(keys[15], (WIN2, WIN2), 0, RELS), jax.random.fold_in(keys[15], 1), 0, RELS - 1).astype(jnp.int32),
        "cotangent": bell_draw(keys[16], (IMAGES, RES, RES, D), 1.0, 6.0, ((0, 32),)),
    }


@jax.custom_vjp
def low(v):
    return lax.optimization_barrier(v.astype(jnp.bfloat16)).astype(jnp.float32)

@jax.custom_vjp
def low_back(v):
    return v

def low_keep(v):
    return (low(v), None)

def low_pass(kept, grad):
    return (grad,)

def back_keep(v):
    return (v, None)

def back_low(kept, grad):
    return (low(grad),)
low.defvjp(low_keep, low_pass)
low_back.defvjp(back_keep, back_low)
EPSILON = 1e-05
HIGHEST = lax.Precision.HIGHEST

def norm_rows(values, gain, offset):
    center = values - lax.optimization_barrier(jnp.mean(values, axis=-1, keepdims=True))
    spread = lax.optimization_barrier(jnp.mean(center * center, axis=-1, keepdims=True))
    return center * lax.rsqrt(spread + EPSILON) * gain + offset

def to_windows(field):
    count = field.shape[0]
    across = RES // WIN
    tiles = field.reshape(count, across, WIN, across, WIN, field.shape[-1]).transpose(0, 1, 3, 2, 4, 5)
    return tiles.reshape(count * across * across, WIN * WIN, field.shape[-1])

def from_windows(tiles, count):
    across = RES // WIN
    field = tiles.reshape(count, across, across, WIN, WIN, tiles.shape[-1]).transpose(0, 1, 3, 2, 4, 5)
    return field.reshape(count, RES, RES, tiles.shape[-1])

def apply_matrix(left, matrix):
    return jnp.einsum('...c,ce->...e', left, low(matrix), precision=HIGHEST)

def block(images, params, region_labels, position_index):
    input_gain, input_shift, attend_weight, attend_bias, output_weight, output_bias, second_gain, second_shift, expand_weight, expand_bias, reduce_weight, reduce_bias, position_table = params
    count = images.shape[0]
    across = RES // WIN
    normed = norm_rows(images, input_gain, input_shift)
    tiles = low(to_windows(jnp.roll(normed, (-SHIFT, -SHIFT), (1, 2))))
    triple = low_back(apply_matrix(tiles, attend_weight) + attend_bias)
    queries = low(triple[..., :D] * HEAD_DIM ** (-0.5)).reshape(-1, WIN2, HEADS, HEAD_DIM)
    key_rows = low(triple[..., D:2 * D]).reshape(-1, WIN2, HEADS, HEAD_DIM)
    value_rows = low(triple[..., 2 * D:]).reshape(-1, WIN2, HEADS, HEAD_DIM)
    labels = region_labels.reshape(across, WIN, across, WIN).transpose(0, 2, 1, 3).reshape(across * across, WIN2)
    masking = jnp.where(labels[:, :, None] == labels[:, None, :], 0.0, -100.0)
    rel_bias = position_table[position_index].transpose(2, 0, 1)
    scores = jnp.einsum('aqhd,akhd->ahqk', queries, key_rows, precision=HIGHEST)
    scores = scores.reshape(count, across * across, HEADS, WIN2, WIN2) + rel_bias[None, None] + masking[None, :, None]
    scores = low_back(scores)
    mixing = low(jax.nn.softmax(scores, axis=-1)).reshape(-1, HEADS, WIN2, WIN2)
    context = jnp.einsum('ahqk,akhd->aqhd', mixing, value_rows, precision=HIGHEST).reshape(-1, WIN2, D)
    merged = low(low_back(jnp.roll(from_windows(context, count), (SHIFT, SHIFT), (1, 2))))
    middle = images + low_back(apply_matrix(merged, output_weight) + output_bias)
    normed_two = low(norm_rows(middle, second_gain, second_shift))
    hidden = low_back(apply_matrix(normed_two, expand_weight) + expand_bias)
    activated = low(jax.nn.gelu(hidden, approximate=False))
    return middle + low_back(apply_matrix(activated, reduce_weight) + reduce_bias)

def reference(images, input_gain, input_shift, attend_weight, attend_bias, output_weight, output_bias, second_gain, second_shift, expand_weight, expand_bias, reduce_weight, reduce_bias, position_table, region_labels, position_index, cotangent):
    params = tuple((weight.astype(jnp.float32) for weight in (input_gain, input_shift, attend_weight, attend_bias, output_weight, output_bias, second_gain, second_shift, expand_weight, expand_bias, reduce_weight, reduce_bias, position_table)))
    group = 16
    inputs = images.astype(jnp.float32).reshape(IMAGES // group, group, RES, RES, D)
    cotans = cotangent.astype(jnp.float32).reshape(IMAGES // group, group, RES, RES, D)

    def one_group(totals, item):
        batch_in, batch_cot = item
        result, pullback = jax.vjp(lambda inner, weights: block(inner, weights, region_labels, position_index), batch_in, params)
        batch_grad, weight_grads = pullback(batch_cot)
        totals = tuple((running + addend for running, addend in zip(totals, weight_grads)))
        return (totals, (result.astype(jnp.bfloat16), batch_grad.astype(jnp.bfloat16)))
    zeros = tuple((jnp.zeros(weight.shape, jnp.float32) for weight in params))
    sums, (results, input_grads) = lax.scan(one_group, zeros, (inputs, cotans))
    return (results.reshape(IMAGES, RES, RES, D), input_grads.reshape(IMAGES, RES, RES, D), sums[0], sums[1], sums[2], sums[3], sums[4], sums[5], sums[6], sums[7], sums[8], sums[9], sums[10], sums[11], sums[12])
```

```python
import functools

import jax
import jax.numpy as jnp
import numpy as np
from jax import lax
from jax.experimental import pallas as pl
from jax.experimental.pallas import tpu as pltpu
from jax.sharding import PartitionSpec as P

HEADS = 16
HEAD_DIM = 32
WIN = 7
RES = 14
SHIFT = 3
WIN2 = 49
TOKENS = RES * RES
EPSILON = 1e-05
GROUP = 4
SLOT = 64
KEYS = 56
SPAN = 208
STEP = 192
BLOCKS = 4
LANES = 128
ROWS = 224
CHUNK = 512
VMEM = 60 * 1024 * 1024
F32 = jnp.float32
BF16 = jnp.bfloat16


def window_order():
    select = np.zeros((GROUP, 4 * SLOT, SPAN), np.float32)
    for image in range(GROUP):
        for wi in range(2):
            for wj in range(2):
                for ti in range(WIN):
                    for tj in range(WIN):
                        row = (wi * 2 + wj) * SLOT + ti * WIN + tj
                        si = (wi * WIN + ti + SHIFT) % RES
                        sj = (wj * WIN + tj + SHIFT) % RES
                        select[image, row, si * RES + sj + image * (TOKENS - STEP)] = 1.0
    return select


def dot(left, right, contract):
    return lax.dot_general(left, right, (contract, ((), ())), preferred_element_type=F32)


def nn(left, right):
    return dot(left, right, ((1,), (0,)))


def nt(left, right):
    return dot(left, right, ((1,), (1,)))


def tn(left, right):
    return dot(left, right, ((0,), (0,)))


def norm(rows):
    center = rows - jnp.mean(rows, axis=-1, keepdims=True)
    spread = jnp.mean(center * center, axis=-1, keepdims=True)
    scale = lax.rsqrt(spread + EPSILON)
    return center * scale, scale


def norm_back(z, scale, gain, grad):
    g = grad * gain
    return scale * (
        g - jnp.mean(g, axis=-1, keepdims=True) - z * jnp.mean(g * z, axis=-1, keepdims=True)
    )


def head_masks():
    lane = lax.broadcasted_iota(jnp.int32, (SLOT, LANES), 1)
    return [(lane // HEAD_DIM) == j for j in range(4)]


def spread_heads(rows, masks):
    zero = jnp.zeros_like(rows)
    return jnp.concatenate([jnp.where(mask, rows, zero) for mask in masks], axis=0)


def pick_heads(wide, masks):
    total = jnp.where(masks[0], wide[:SLOT], 0.0)
    for j in range(1, 4):
        total = jnp.where(masks[j], wide[j * SLOT : (j + 1) * SLOT], total)
    return total


def pad_keys(rows):
    return jnp.concatenate([rows, jnp.zeros((SLOT - KEYS, rows.shape[1]), F32)], axis=0).astype(
        BF16
    )


def mix(keys, spread_q, bias):
    scores = nt(keys, spread_q)[:KEYS] + bias
    top = jnp.max(scores, axis=0, keepdims=True)
    raised = jnp.exp(scores - top)
    return raised * (1.0 / jnp.sum(raised, axis=0, keepdims=True))


def put_span(ref, start, value, columns=slice(None)):
    head = pl.ds(start, 16)
    tail = pl.ds(pl.multiple_of(start + 16, 16), SPAN - 16)
    ref[head, columns] = ref[head, columns] + value[:16]
    ref[tail, columns] = value[16:]


def attend_kernel(
    images, gain, shift, weight, attend_bias, bias, select, select_t, normed, windows, merged, flat
):
    width = images.shape[1]
    z, _ = norm(images[...].astype(F32))
    low = (z * gain[...].astype(F32) + shift[...].astype(F32)).astype(BF16)
    normed[...] = low
    for part in range(3):
        cols = slice(part * width, (part + 1) * width)
        value = nn(low, weight[:, cols]) + attend_bias[:, cols].astype(F32)
        if part == 0:
            value = value * HEAD_DIM**-0.5
        flat[:, cols] = value.astype(BF16)
    merged[:16, :] = jnp.zeros((16, width), BF16)

    def one_image(image, carry):
        start = pl.multiple_of(image * STEP, 16)
        span = flat[pl.ds(start, SPAN), :]
        chosen = select[image]
        windows[image] = nn(chosen, span).astype(BF16)
        masks = head_masks()
        rows = []
        for w in range(4):
            at = slice(w * SLOT, (w + 1) * SLOT)
            parts = []
            for g in range(BLOCKS):
                q, k, v = (
                    windows[image, at, part * width + g * LANES : part * width + (g + 1) * LANES]
                    for part in range(3)
                )
                mixing = mix(k, spread_heads(q, masks), bias[w, g])
                parts.append(pick_heads(tn(pad_keys(mixing), v), masks).astype(BF16))
            rows.append(jnp.concatenate(parts, axis=1))
        context = jnp.concatenate(rows, axis=0)
        put_span(merged, start, nn(select_t[image], context).astype(BF16))
        return carry

    lax.fori_loop(0, GROUP, one_image, 0)


def gelu_parts(t):
    k = 1.0 / (1.0 + (0.3275911 * 0.5**0.5) * jnp.abs(t))
    bell = jnp.exp(-0.5 * (t * t))
    poly = 0.5 * 1.061405429 * k - 0.5 * 1.453152027
    poly = poly * k + 0.5 * 1.421413741
    poly = poly * k - 0.5 * 0.284496736
    poly = poly * k + 0.5 * 0.254829592
    tail = poly * k * bell
    below = jnp.where(t >= 0, 1.0 - tail, tail)
    return t * below, below + t * (bell * 0.3989422804014327)


def feed_kernel(
    images,
    merged,
    cot,
    out_w,
    out_b,
    gain,
    shift,
    exp_w,
    exp_b,
    red_w,
    red_b,
    block_out,
    grad_mid,
    act,
    grad_hid,
    normed_two,
    narrow,
    wide,
):
    @pl.when(pl.program_id(0) == 0)
    def _():
        narrow[...] = jnp.zeros_like(narrow)
        wide[...] = jnp.zeros_like(wide)

    middle = images[...].astype(F32) + nn(merged[...], out_w[...]) + out_b[...].astype(F32)
    z, scale = norm(middle)
    scaled = gain[...].astype(F32)
    low = (z * scaled + shift[...].astype(F32)).astype(BF16)
    normed_two[...] = low
    grad = cot[...]
    result = middle + red_b[...].astype(F32)
    grad_y = jnp.zeros_like(middle)
    for c in range(exp_w.shape[1] // CHUNK):
        at = slice(c * CHUNK, (c + 1) * CHUNK)
        hidden = nn(low, exp_w[:, at]) + exp_b[:, at].astype(F32)
        grad_act = nt(grad, red_w[at, :])
        active, slope = gelu_parts(hidden)
        active = active.astype(BF16)
        act[:, at] = active
        grad_h = (grad_act * slope).astype(BF16)
        grad_hid[:, at] = grad_h
        wide[:, at] += jnp.sum(grad_h.astype(F32), axis=0, keepdims=True)
        result = result + nn(active, red_w[at, :])
        grad_y = grad_y + nt(grad_h, exp_w[:, at])
    block_out[...] = result.astype(BF16)
    wide_cot = grad.astype(F32)
    grad_middle = wide_cot + norm_back(z, scale, scaled, grad_y)
    grad_mid[...] = grad_middle
    narrow[0:1] += jnp.sum(grad_y * z, axis=0, keepdims=True)
    narrow[1:2] += jnp.sum(grad_y, axis=0, keepdims=True)
    narrow[2:3] += jnp.sum(wide_cot, axis=0, keepdims=True)
    narrow[3:4] += jnp.sum(grad_middle.astype(BF16).astype(F32), axis=0, keepdims=True)


def attend_back_kernel(
    grad_mid, out_w, windows, bias, select, select_t, branch, triple, scores, sums, flat, tiles
):
    width = grad_mid.shape[1]

    @pl.when(pl.program_id(0) == 0)
    def _():
        scores[...] = jnp.zeros_like(scores)
        sums[...] = jnp.zeros_like(sums)

    low = grad_mid[...].astype(BF16)
    branch[...] = low
    flat[...] = nt(low, out_w[...]).astype(BF16)
    triple[:16, :] = jnp.zeros((16, 3 * width), BF16)

    def one_image(image, carry):
        start = pl.multiple_of(image * STEP, 16)
        context = nn(select[image], flat[pl.ds(start, SPAN), :]).astype(BF16)
        masks = head_masks()
        for w in range(4):
            at = slice(w * SLOT, (w + 1) * SLOT)
            for g in range(BLOCKS):
                cols = [
                    slice(part * width + g * LANES, part * width + (g + 1) * LANES)
                    for part in range(3)
                ]
                q, k, v = (windows[image, at, c] for c in cols)
                grad_c = context[at, g * LANES : (g + 1) * LANES]
                spread_q = spread_heads(q, masks)
                spread_g = spread_heads(grad_c, masks)
                mixing = mix(k, spread_q, bias[w, g])
                grad_v = nn(pad_keys(mixing), spread_g)
                grad_m = nt(v, spread_g)[:KEYS]
                inner = jnp.sum(grad_m * mixing, axis=0, keepdims=True)
                grad_s = pad_keys(mixing * (grad_m - inner))
                scores[g] += grad_s.astype(F32)[:KEYS]
                grad_k = nn(grad_s, spread_q)
                grad_q = pick_heads(tn(grad_s, k), masks) * HEAD_DIM**-0.5
                for c, value in zip(cols, (grad_q, grad_k, grad_v)):
                    tiles[at, c] = value.astype(BF16)
        sums[...] += jnp.sum(tiles[...].astype(F32), axis=0, keepdims=True)
        put_span(triple, start, nn(select_t[image], tiles[...]).astype(BF16))
        return carry

    lax.fori_loop(0, GROUP, one_image, 0)


def input_back_kernel(triple, weight, images, gain, grad_mid, images_grad, narrow):
    @pl.when(pl.program_id(0) == 0)
    def _():
        narrow[...] = jnp.zeros_like(narrow)

    grad_n = nt(triple[...], weight[...])
    z, scale = norm(images[...].astype(F32))
    back = norm_back(z, scale, gain[...].astype(F32), grad_n)
    images_grad[...] = (grad_mid[...] + back).astype(BF16)
    narrow[0:1] += jnp.sum(grad_n * z, axis=0, keepdims=True)
    narrow[1:2] += jnp.sum(grad_n, axis=0, keepdims=True)


def whole(array):
    return pl.BlockSpec(array.shape, lambda i: (0,) * array.ndim)


def rows_of(count, width):
    return pl.BlockSpec((count, width), lambda i: (i, 0))


def call(kernel, steps, args, specs, outs, out_specs, scratch=(), flops=0):
    moved = sum(a.size * a.dtype.itemsize for a in args) + sum(
        o.size * o.dtype.itemsize for o in outs
    )
    return pl.pallas_call(
        kernel,
        grid=(steps,),
        in_specs=specs,
        out_specs=out_specs,
        out_shape=outs,
        scratch_shapes=list(scratch),
        compiler_params=pltpu.CompilerParams(vmem_limit_bytes=VMEM),
        cost_estimate=pl.CostEstimate(flops=flops, bytes_accessed=moved, transcendentals=0),
    )(*args)


def shape(dims, kind):
    return jax.ShapeDtypeStruct(dims, kind)


def window_bias(region_labels, position_index, position_table):
    across = RES // WIN
    labels = (
        region_labels.reshape(across, WIN, across, WIN).transpose(0, 2, 1, 3).reshape(-1, WIN2)
    )
    masking = jnp.where(labels[:, :, None] == labels[:, None, :], 0.0, -100.0).astype(F32)
    index = jnp.pad(
        position_index.T, ((0, KEYS - WIN2), (0, SLOT - WIN2)), constant_values=-1
    ).reshape(-1)
    onehot = (jnp.arange(position_table.shape[0], dtype=jnp.int32)[:, None] == index[None]).astype(
        BF16
    )
    looked = dot(position_table, onehot, ((0,), (0,)))
    looked = looked.reshape(BLOCKS, 4, KEYS, SLOT).transpose(0, 2, 1, 3)
    masking = jnp.pad(masking, ((0, 0), (0, KEYS - WIN2), (0, SLOT - WIN2)))
    bias = looked[None] + masking[:, None, :, None, :]
    real = lax.broadcasted_iota(jnp.int32, bias.shape, 2) < WIN2
    bias = jnp.where(real, bias, -1e30).reshape(4, BLOCKS, KEYS, 4 * SLOT)
    return bias, onehot


def bits_of(size):
    return [1 << b for b in range(size.bit_length() - 1)]


def swap(value, axis, size, bit):
    return lax.ppermute(value, axis, [(i, i ^ bit) for i in range(size)])


def gather(shard, fsdp, dp):
    rows, columns = shard.shape
    half = columns // 2
    core = lax.axis_index("dp") % 2
    me = lax.axis_index("fsdp")
    bits = bits_of(fsdp)
    value = lax.dynamic_slice_in_dim(shard, core * half, half, 1)
    value = value.reshape((1,) * len(bits) + (rows, half))
    for at, bit in enumerate(reversed(bits)):
        other = swap(value, "fsdp", fsdp, bit)
        up = (me & bit) != 0
        value = jnp.concatenate(
            [jnp.where(up, other, value), jnp.where(up, value, other)], axis=at
        )
    value = value.reshape(fsdp * rows, half)
    other = swap(value, "dp", dp, 1)
    return jnp.concatenate(
        [jnp.where(core == 0, value, other), jnp.where(core == 0, other, value)], axis=1
    ).reshape(fsdp, rows, columns)


def keep_and_send(value, upper, axis):
    half = value.shape[axis] // 2
    low = lax.slice_in_dim(value, 0, half, axis=axis)
    high = lax.slice_in_dim(value, half, 2 * half, axis=axis)
    return jnp.where(upper, high, low), jnp.where(upper, low, high)


def reduce_to_shard(total, fsdp, dp):
    columns = total.shape[1]
    core = lax.axis_index("dp") % 2
    me = lax.axis_index("fsdp")
    bits = bits_of(fsdp)
    kept, sent = keep_and_send(total, core == 1, 1)
    kept = kept.astype(F32) + swap(sent.astype(BF16), "dp", dp, 1).astype(F32)
    kept = kept.reshape((2,) * len(bits) + (total.shape[0] // fsdp, columns // 2))
    for bit in bits:
        axis = len(bits) - bit.bit_length()
        kept, sent = keep_and_send(kept, (me & bit) != 0, axis)
        kept = kept + swap(sent.astype(BF16), "fsdp", fsdp, bit).astype(F32)
    kept = kept.reshape(total.shape[0] // fsdp, columns // 2)
    for bit in bits_of(dp)[1:]:
        kept = kept.astype(BF16)
        kept = kept.astype(F32) + swap(kept, "dp", dp, bit).astype(F32)
    low = kept.astype(BF16)
    other = swap(low, "dp", dp, 1)
    return jnp.concatenate(
        [jnp.where(core == 0, low, other), jnp.where(core == 0, other, low)], axis=1
    ).astype(F32)


def body(fsdp, dp, *args):
    (
        images,
        input_gain,
        input_shift,
        attend_weight,
        attend_bias,
        output_weight,
        output_bias,
        second_gain,
        second_shift,
        expand_weight,
        expand_bias,
        reduce_weight,
        reduce_bias,
        position_table,
        region_labels,
        position_index,
        cotangent,
    ) = args
    count = images.shape[0]
    width = images.shape[-1]
    rows = attend_weight.shape[0]
    hidden = expand_weight.shape[1]
    tokens = count * TOKENS
    vectors = (
        input_gain,
        input_shift,
        attend_bias,
        output_bias,
        second_gain,
        second_shift,
        expand_bias,
        reduce_bias,
    )
    small = jnp.concatenate(vectors)
    small = jnp.pad(small, (0, 3 * width - small.shape[0])).reshape(1, 3 * width)
    front = gather(
        jnp.concatenate([attend_weight, jnp.pad(small, ((0, 15), (0, 0)))], axis=0), fsdp, dp
    )
    ratio = hidden // width
    rest = gather(
        jnp.concatenate(
            [output_weight, expand_weight]
            + [reduce_weight[i * rows : (i + 1) * rows] for i in range(ratio)],
            axis=1,
        ),
        fsdp,
        dp,
    )
    attend_w = front[:, :rows].reshape(width, 3 * width)
    line = front[:, rows]
    full = []
    at = 0
    for vector in vectors:
        size = vector.shape[0]
        full.append(line[:, at : at + size].reshape(1, fsdp * size))
        at += size
    gain_1, shift_1, attend_b, out_b, gain_2, shift_2, exp_b, red_b = full
    out_w = rest[:, :, :width].reshape(width, width)
    exp_w = rest[:, :, width : width + hidden].reshape(width, hidden)
    red_w = (
        rest[:, :, width + hidden :]
        .reshape(fsdp, rows, ratio, width)
        .transpose(0, 2, 1, 3)
        .reshape(hidden, width)
    )
    bias, onehot = window_bias(region_labels, position_index, position_table)
    order = window_order()
    select = jnp.asarray(order, BF16)
    select_t = jnp.asarray(order.transpose(0, 2, 1), BF16)
    flat_in = images.reshape(tokens, width)
    flat_cot = cotangent.reshape(tokens, width)

    group_rows = GROUP * TOKENS
    groups = count // GROUP
    win_spec = pl.BlockSpec((GROUP, 4 * SLOT, 3 * width), lambda i: (i, 0, 0))
    normed, windows, merged = call(
        attend_kernel,
        groups,
        (flat_in, gain_1, shift_1, attend_w, attend_b, bias, select, select_t),
        [rows_of(group_rows, width)]
        + [whole(a) for a in (gain_1, shift_1, attend_w, attend_b, bias, select, select_t)],
        (
            shape((tokens, width), BF16),
            shape((count, 4 * SLOT, 3 * width), BF16),
            shape((tokens, width), BF16),
        ),
        (rows_of(group_rows, width), win_spec, rows_of(group_rows, width)),
        (pltpu.VMEM((group_rows, 3 * width), BF16),),
        flops=12 * 10**9,
    )
    by_rows = rows_of(ROWS, width)
    by_hidden = rows_of(ROWS, hidden)
    fixed = (out_w, out_b, gain_2, shift_2, exp_w, exp_b, red_w, red_b)
    block_out, grad_mid, act, grad_hid, normed_two, narrow_2, wide_2 = call(
        feed_kernel,
        tokens // ROWS,
        (flat_in, merged, flat_cot) + fixed,
        [by_rows] * 3 + [whole(a) for a in fixed],
        (
            shape((tokens, width), BF16),
            shape((tokens, width), F32),
            shape((tokens, hidden), BF16),
            shape((tokens, hidden), BF16),
            shape((tokens, width), BF16),
            shape((8, width), F32),
            shape((1, hidden), F32),
        ),
        (
            by_rows,
            by_rows,
            by_hidden,
            by_hidden,
            by_rows,
            pl.BlockSpec((8, width), lambda i: (0, 0)),
            pl.BlockSpec((1, hidden), lambda i: (0, 0)),
        ),
        flops=20 * 10**9,
    )
    red_grad = tn(act, flat_cot).astype(BF16)
    exp_grad = tn(normed_two, grad_hid).astype(BF16)
    feed_grad = reduce_to_shard(
        jnp.concatenate(
            [
                exp_grad,
                red_grad.reshape(fsdp, ratio, rows, width)
                .transpose(0, 2, 1, 3)
                .reshape(width, hidden),
            ],
            axis=1,
        ),
        fsdp,
        dp,
    )
    branch, triple, scores, sums = call(
        attend_back_kernel,
        groups,
        (grad_mid, out_w, windows, bias, select, select_t),
        [rows_of(group_rows, width), whole(out_w), win_spec]
        + [whole(a) for a in (bias, select, select_t)],
        (
            shape((tokens, width), BF16),
            shape((tokens, 3 * width), BF16),
            shape((BLOCKS, KEYS, 4 * SLOT), F32),
            shape((1, 3 * width), F32),
        ),
        (
            rows_of(group_rows, width),
            rows_of(group_rows, 3 * width),
            pl.BlockSpec((BLOCKS, KEYS, 4 * SLOT), lambda i: (0, 0, 0)),
            pl.BlockSpec((1, 3 * width), lambda i: (0, 0)),
        ),
        (
            pltpu.VMEM((group_rows, width), BF16),
            pltpu.VMEM((4 * SLOT, 3 * width), BF16),
        ),
        flops=16 * 10**9,
    )
    attend_total = reduce_to_shard(
        jnp.concatenate([tn(normed, triple).astype(BF16), tn(merged, branch).astype(BF16)], axis=1),
        fsdp,
        dp,
    )
    images_grad, narrow_1 = call(
        input_back_kernel,
        tokens // ROWS,
        (triple, attend_w, flat_in, gain_1, grad_mid),
        [rows_of(ROWS, 3 * width), whole(attend_w), by_rows, whole(gain_1), by_rows],
        (shape((tokens, width), BF16), shape((8, width), F32)),
        (by_rows, pl.BlockSpec((8, width), lambda i: (0, 0))),
        flops=3 * 10**9,
    )
    score_rows = scores.reshape(BLOCKS, KEYS, 4, SLOT).transpose(0, 2, 1, 3).reshape(HEADS, -1)
    table_grad = lax.dot_general(
        onehot.astype(F32), score_rows, (((1,), (1,)), ((), ())), precision=lax.Precision.HIGHEST
    )
    bundle = (
        narrow_1[0],
        narrow_1[1],
        sums[0],
        narrow_2[3],
        narrow_2[0],
        narrow_2[1],
        wide_2[0],
        narrow_2[2],
    )
    sizes = [b.shape[0] for b in bundle]
    total = lax.psum(jnp.concatenate(list(bundle) + [table_grad.reshape(-1)]), ("dp", "fsdp"))
    me = lax.axis_index("fsdp")
    vector_grads = []
    at = 0
    for size in sizes:
        part = size // fsdp
        vector_grads.append(lax.dynamic_slice_in_dim(total[at : at + size], me * part, part, 0))
        at += size
    table_grad = total[at:].reshape(table_grad.shape)
    red_shard = (
        feed_grad[:, hidden:]
        .reshape(rows, ratio, width)
        .transpose(1, 0, 2)
        .reshape(ratio * rows, width)
    )
    return (
        block_out.reshape(images.shape),
        images_grad.reshape(images.shape),
        vector_grads[0],
        vector_grads[1],
        attend_total[:, : 3 * width],
        vector_grads[2],
        attend_total[:, 3 * width :],
        vector_grads[3],
        vector_grads[4],
        vector_grads[5],
        feed_grad[:, :hidden],
        vector_grads[6],
        red_shard,
        vector_grads[7],
        table_grad,
    )


def solution(mesh):
    tokens = P(("dp", "fsdp"), None, None, None)
    line, matrix = P("fsdp"), P("fsdp", None)
    weights = (line, line, matrix, line, matrix, line, line, line, matrix, line, matrix, line)
    return jax.shard_map(
        functools.partial(body, mesh.shape["fsdp"], mesh.shape["dp"]),
        mesh=mesh,
        in_specs=(tokens,) + weights + (P(), P(), P(), tokens),
        out_specs=(tokens, tokens) + weights + (P(),),
        check_vma=False,
    )
```

```python
import functools

import jax
import jax.numpy as jnp
import numpy as np
from jax import lax
from jax.experimental import pallas as pl
from jax.experimental.pallas import tpu as pltpu
from jax.sharding import PartitionSpec as P

HEADS = 16
HEAD_DIM = 32
WIN = 7
RES = 14
SHIFT = 3
WIN2 = 49
TOKENS = RES * RES
EPSILON = 1e-05
GROUP = 4
SLOT = 64
KEYS = 56
SPAN = 208
STEP = 192
BLOCKS = 4
LANES = 128
ROWS = 224
CHUNK = 512
VMEM = 60 * 1024 * 1024
F32 = jnp.float32
BF16 = jnp.bfloat16


def window_order():
    select = np.zeros((GROUP, 4 * SLOT, SPAN), np.float32)
    for image in range(GROUP):
        for wi in range(2):
            for wj in range(2):
                for ti in range(WIN):
                    for tj in range(WIN):
                        row = (wi * 2 + wj) * SLOT + ti * WIN + tj
                        si = (wi * WIN + ti + SHIFT) % RES
                        sj = (wj * WIN + tj + SHIFT) % RES
                        select[image, row, si * RES + sj + image * (TOKENS - STEP)] = 1.0
    return select


def dot(left, right, contract):
    return lax.dot_general(left, right, (contract, ((), ())), preferred_element_type=F32)


def nn(left, right):
    return dot(left, right, ((1,), (0,)))


def nt(left, right):
    return dot(left, right, ((1,), (1,)))


def tn(left, right):
    return dot(left, right, ((0,), (0,)))


def norm(rows):
    center = rows - jnp.mean(rows, axis=-1, keepdims=True)
    spread = jnp.mean(center * center, axis=-1, keepdims=True)
    scale = lax.rsqrt(spread + EPSILON)
    return center * scale, scale


def norm_back(z, scale, gain, grad):
    g = grad * gain
    return scale * (
        g - jnp.mean(g, axis=-1, keepdims=True) - z * jnp.mean(g * z, axis=-1, keepdims=True)
    )


def head_masks():
    lane = lax.broadcasted_iota(jnp.int32, (SLOT, LANES), 1)
    return [(lane // HEAD_DIM) == j for j in range(4)]


def spread_heads(rows, masks):
    zero = jnp.zeros_like(rows)
    return jnp.concatenate([jnp.where(mask, rows, zero) for mask in masks], axis=0)


def pick_heads(wide, masks):
    total = jnp.where(masks[0], wide[:SLOT], 0.0)
    for j in range(1, 4):
        total = jnp.where(masks[j], wide[j * SLOT : (j + 1) * SLOT], total)
    return total


def pad_keys(rows):
    return jnp.concatenate([rows, jnp.zeros((SLOT - KEYS, rows.shape[1]), F32)], axis=0).astype(
        BF16
    )


def mix(keys, spread_q, bias):
    scores = nt(keys, spread_q)[:KEYS] + bias
    top = jnp.max(scores, axis=0, keepdims=True)
    raised = jnp.exp(scores - top)
    return raised * (1.0 / jnp.sum(raised, axis=0, keepdims=True))


def put_span(ref, start, value, columns=slice(None)):
    head = pl.ds(start, 16)
    tail = pl.ds(pl.multiple_of(start + 16, 16), SPAN - 16)
    ref[head, columns] = ref[head, columns] + value[:16]
    ref[tail, columns] = value[16:]


def attend_kernel(
    images, gain, shift, weight, attend_bias, bias, select, select_t, normed, windows, merged, flat
):
    width = images.shape[1]
    z, _ = norm(images[...].astype(F32))
    low = (z * gain[...].astype(F32) + shift[...].astype(F32)).astype(BF16)
    normed[...] = low
    for part in range(3):
        cols = slice(part * width, (part + 1) * width)
        value = nn(low, weight[:, cols]) + attend_bias[:, cols].astype(F32)
        if part == 0:
            value = value * HEAD_DIM**-0.5
        flat[:, cols] = value.astype(BF16)
    merged[:16, :] = jnp.zeros((16, width), BF16)

    def one_image(image, carry):
        start = pl.multiple_of(image * STEP, 16)
        span = flat[pl.ds(start, SPAN), :]
        chosen = select[image]
        windows[image] = nn(chosen, span).astype(BF16)
        masks = head_masks()
        rows = []
        for w in range(4):
            at = slice(w * SLOT, (w + 1) * SLOT)
            parts = []
            for g in range(BLOCKS):
                q, k, v = (
                    windows[image, at, part * width + g * LANES : part * width + (g + 1) * LANES]
                    for part in range(3)
                )
                mixing = mix(k, spread_heads(q, masks), bias[w, g])
                parts.append(pick_heads(tn(pad_keys(mixing), v), masks).astype(BF16))
            rows.append(jnp.concatenate(parts, axis=1))
        context = jnp.concatenate(rows, axis=0)
        put_span(merged, start, nn(select_t[image], context).astype(BF16))
        return carry

    lax.fori_loop(0, GROUP, one_image, 0)


def gelu_parts(t):
    k = 1.0 / (1.0 + (0.3275911 * 0.5**0.5) * jnp.abs(t))
    bell = jnp.exp(-0.5 * (t * t))
    poly = 0.5 * 1.061405429 * k - 0.5 * 1.453152027
    poly = poly * k + 0.5 * 1.421413741
    poly = poly * k - 0.5 * 0.284496736
    poly = poly * k + 0.5 * 0.254829592
    tail = poly * k * bell
    below = jnp.where(t >= 0, 1.0 - tail, tail)
    return t * below, below + t * (bell * 0.3989422804014327)


def feed_kernel(
    images,
    merged,
    cot,
    out_w,
    out_b,
    gain,
    shift,
    exp_w,
    exp_b,
    red_w,
    red_b,
    place,
    place_t,
    block_out,
    grad_mid,
    act,
    grad_hid,
    normed_two,
    narrow,
    wide,
):
    @pl.when(pl.program_id(0) == 0)
    def _():
        narrow[...] = jnp.zeros_like(narrow)
        wide[...] = jnp.zeros_like(wide)

    middle = images[...].astype(F32) + nn(merged[...], out_w[...]) + out_b[...].astype(F32)
    z, scale = norm(middle)
    scaled = gain[...].astype(F32)
    low = (z * scaled + shift[...].astype(F32)).astype(BF16)
    normed_two[...] = low
    grad = from_grid(cot[...], place_t[...])
    result = middle + red_b[...].astype(F32)
    grad_y = jnp.zeros_like(middle)
    for c in range(exp_w.shape[1] // CHUNK):
        at = slice(c * CHUNK, (c + 1) * CHUNK)
        hidden = nn(low, exp_w[:, at]) + exp_b[:, at].astype(F32)
        grad_act = nt(grad, red_w[at, :])
        active, slope = gelu_parts(hidden)
        active = active.astype(BF16)
        act[:, at] = active
        grad_h = (grad_act * slope).astype(BF16)
        grad_hid[:, at] = grad_h
        wide[:, at] += jnp.sum(grad_h.astype(F32), axis=0, keepdims=True)
        result = result + nn(active, red_w[at, :])
        grad_y = grad_y + nt(grad_h, exp_w[:, at])
    block_out[...] = to_grid(result.astype(BF16), place[...])
    wide_cot = grad.astype(F32)
    grad_middle = wide_cot + norm_back(z, scale, scaled, grad_y)
    grad_mid[...] = grad_middle
    narrow[0:1] += jnp.sum(grad_y * z, axis=0, keepdims=True)
    narrow[1:2] += jnp.sum(grad_y, axis=0, keepdims=True)
    narrow[2:3] += jnp.sum(wide_cot, axis=0, keepdims=True)
    narrow[3:4] += jnp.sum(grad_middle.astype(BF16).astype(F32), axis=0, keepdims=True)


def attend_back_kernel(
    grad_mid, out_w, windows, bias, select, select_t, branch, triple, scores, sums, flat, tiles
):
    width = grad_mid.shape[1]

    @pl.when(pl.program_id(0) == 0)
    def _():
        scores[...] = jnp.zeros_like(scores)
        sums[...] = jnp.zeros_like(sums)

    low = grad_mid[...].astype(BF16)
    branch[...] = low
    flat[...] = nt(low, out_w[...]).astype(BF16)
    triple[:16, :] = jnp.zeros((16, 3 * width), BF16)

    def one_image(image, carry):
        start = pl.multiple_of(image * STEP, 16)
        context = nn(select[image], flat[pl.ds(start, SPAN), :]).astype(BF16)
        masks = head_masks()
        for w in range(4):
            at = slice(w * SLOT, (w + 1) * SLOT)
            for g in range(BLOCKS):
                cols = [
                    slice(part * width + g * LANES, part * width + (g + 1) * LANES)
                    for part in range(3)
                ]
                q, k, v = (windows[image, at, c] for c in cols)
                grad_c = context[at, g * LANES : (g + 1) * LANES]
                spread_q = spread_heads(q, masks)
                spread_g = spread_heads(grad_c, masks)
                mixing = mix(k, spread_q, bias[w, g])
                grad_v = nn(pad_keys(mixing), spread_g)
                grad_m = nt(v, spread_g)[:KEYS]
                inner = jnp.sum(grad_m * mixing, axis=0, keepdims=True)
                grad_s = pad_keys(mixing * (grad_m - inner))
                scores[g] += grad_s.astype(F32)[:KEYS]
                grad_k = nn(grad_s, spread_q)
                grad_q = pick_heads(tn(grad_s, k), masks) * HEAD_DIM**-0.5
                for c, value in zip(cols, (grad_q, grad_k, grad_v)):
                    tiles[at, c] = value.astype(BF16)
        sums[...] += jnp.sum(tiles[...].astype(F32), axis=0, keepdims=True)
        put_span(triple, start, nn(select_t[image], tiles[...]).astype(BF16))
        return carry

    lax.fori_loop(0, GROUP, one_image, 0)


def input_back_kernel(triple, weight, images, gain, grad_mid, place, images_grad, narrow):
    @pl.when(pl.program_id(0) == 0)
    def _():
        narrow[...] = jnp.zeros_like(narrow)

    grad_n = nt(triple[...], weight[...])
    z, scale = norm(images[...].astype(F32))
    back = norm_back(z, scale, gain[...].astype(F32), grad_n)
    images_grad[...] = to_grid((grad_mid[...] + back).astype(BF16), place[...])
    narrow[0:1] += jnp.sum(grad_n * z, axis=0, keepdims=True)
    narrow[1:2] += jnp.sum(grad_n, axis=0, keepdims=True)


def grid_rows():
    place = np.zeros((ROWS // RES * 16, ROWS), np.float32)
    for token in range(ROWS):
        place[token // RES * 16 + token % RES, token] = 1.0
    return place


def from_grid(block, place_t):
    lines = block.shape[0]
    padded = jnp.concatenate([block, jnp.zeros((lines, 16 - RES, block.shape[2]), BF16)], axis=1)
    return nn(place_t, padded.reshape(lines * 16, block.shape[2])).astype(BF16)


def to_grid(rows, place):
    padded = nn(place, rows).astype(BF16)
    return padded.reshape(-1, 16, rows.shape[1])[:, :RES]


def whole(array):
    return pl.BlockSpec(array.shape, lambda i: (0,) * array.ndim)


def rows_of(count, width):
    return pl.BlockSpec((count, width), lambda i: (i, 0))


def call(kernel, steps, args, specs, outs, out_specs, scratch=(), flops=0):
    moved = sum(a.size * a.dtype.itemsize for a in args) + sum(
        o.size * o.dtype.itemsize for o in outs
    )
    return pl.pallas_call(
        kernel,
        grid=(steps,),
        in_specs=specs,
        out_specs=out_specs,
        out_shape=outs,
        scratch_shapes=list(scratch),
        compiler_params=pltpu.CompilerParams(vmem_limit_bytes=VMEM),
        cost_estimate=pl.CostEstimate(flops=flops, bytes_accessed=moved, transcendentals=0),
    )(*args)


def shape(dims, kind):
    return jax.ShapeDtypeStruct(dims, kind)


def window_bias(region_labels, position_index, position_table):
    across = RES // WIN
    labels = (
        region_labels.reshape(across, WIN, across, WIN).transpose(0, 2, 1, 3).reshape(-1, WIN2)
    )
    masking = jnp.where(labels[:, :, None] == labels[:, None, :], 0.0, -100.0).astype(F32)
    index = jnp.pad(
        position_index.T, ((0, KEYS - WIN2), (0, SLOT - WIN2)), constant_values=-1
    ).reshape(-1)
    onehot = (jnp.arange(position_table.shape[0], dtype=jnp.int32)[:, None] == index[None]).astype(
        BF16
    )
    looked = dot(position_table, onehot, ((0,), (0,)))
    looked = looked.reshape(BLOCKS, 4, KEYS, SLOT).transpose(0, 2, 1, 3)
    masking = jnp.pad(masking, ((0, 0), (0, KEYS - WIN2), (0, SLOT - WIN2)))
    bias = looked[None] + masking[:, None, :, None, :]
    real = lax.broadcasted_iota(jnp.int32, bias.shape, 2) < WIN2
    bias = jnp.where(real, bias, -1e30).reshape(4, BLOCKS, KEYS, 4 * SLOT)
    return bias, onehot


def bits_of(size):
    return [1 << b for b in range(size.bit_length() - 1)]


def swap(value, axis, size, bit):
    return lax.ppermute(value, axis, [(i, i ^ bit) for i in range(size)])


def after(value, *others):
    return lax.optimization_barrier((value,) + others)[0]


def cut_for_core(shard):
    half = shard.shape[1] // 2
    return lax.dynamic_slice_in_dim(shard, (lax.axis_index("dp") % 2) * half, half, 1)


def join_bit(value, other, up, axis):
    return jnp.concatenate([jnp.where(up, other, value), jnp.where(up, value, other)], axis=axis)


def gather_bit(value, fsdp, bit):
    axis = fsdp.bit_length() - 1 - bit.bit_length()
    up = (lax.axis_index("fsdp") & bit) != 0
    return join_bit(value, swap(value, "fsdp", fsdp, bit), up, axis)


def gather_core(value, dp):
    return join_bit(value, swap(value, "dp", dp, 1), lax.axis_index("dp") % 2 == 1, 1)


def keep_and_send(value, upper, axis):
    half = value.shape[axis] // 2
    low = lax.slice_in_dim(value, 0, half, axis=axis)
    high = lax.slice_in_dim(value, half, 2 * half, axis=axis)
    return jnp.where(upper, high, low), jnp.where(upper, low, high).astype(BF16)


def add_up(kept, arrived):
    total = kept.astype(F32)
    for value in arrived:
        total = total + value.astype(F32)
    return total


def fold_bit(value, fsdp, bit, left):
    upper = (lax.axis_index("fsdp") & bit) != 0
    axis = sorted(left, reverse=True).index(bit)
    kept, sent = keep_and_send(value, upper, axis)
    shape_left = kept.shape[:axis] + kept.shape[axis + 1 :]
    return kept.reshape(shape_left), sent.reshape(shape_left), [b for b in left if b != bit]


def stack_rows(*values):
    return jnp.concatenate([v.reshape(-1, v.shape[-1]).astype(BF16) for v in values], axis=0)


def split_rows(stacked, *like):
    out, at = [], 0
    for value in like:
        size = value.size // value.shape[-1]
        out.append(stacked[at : at + size].reshape(value.shape))
        at += size
    return out


def body(fsdp, dp, *args):
    (
        images,
        input_gain,
        input_shift,
        attend_weight,
        attend_bias,
        output_weight,
        output_bias,
        second_gain,
        second_shift,
        expand_weight,
        expand_bias,
        reduce_weight,
        reduce_bias,
        position_table,
        region_labels,
        position_index,
        cotangent,
    ) = args
    count = images.shape[0]
    width = images.shape[-1]
    rows = attend_weight.shape[0]
    hidden = expand_weight.shape[1]
    tokens = count * TOKENS
    vectors = (
        input_gain,
        input_shift,
        attend_bias,
        output_bias,
        second_gain,
        second_shift,
        expand_bias,
        reduce_bias,
    )
    small = jnp.concatenate(vectors)
    small = jnp.pad(small, (0, 3 * width - small.shape[0])).reshape(1, 3 * width)
    ratio = hidden // width
    bits = bits_of(fsdp)
    lead = (1,) * len(bits)
    front = cut_for_core(
        jnp.concatenate([attend_weight, jnp.pad(small, ((0, 15), (0, 0)))], axis=0)
    )
    rest = jnp.concatenate(
        [after(output_weight, front), expand_weight]
        + [reduce_weight[i * rows : (i + 1) * rows] for i in range(ratio)],
        axis=1,
    )
    front = front.reshape(lead + front.shape)
    rest = cut_for_core(rest)
    rest = rest.reshape(lead + rest.shape)
    for bit in reversed(bits):
        front = gather_bit(front, fsdp, bit)
        if bit != 1:
            rest = gather_bit(after(rest, front), fsdp, bit)
    front = gather_core(front.reshape(-1, front.shape[-1]), dp).reshape(fsdp, -1, 3 * width)
    front = after(front, rest)
    rest_low = swap(rest, "fsdp", fsdp, 1)
    attend_w = front[:, :rows].reshape(width, 3 * width)
    line = front[:, rows]
    full = []
    at = 0
    for vector in vectors:
        size = vector.shape[0]
        full.append(line[:, at : at + size].reshape(1, fsdp * size))
        at += size
    gain_1, shift_1, attend_b, out_b, gain_2, shift_2, exp_b, red_b = full
    bias, onehot = window_bias(region_labels, position_index, position_table)
    order = window_order()
    select = jnp.asarray(order, BF16)
    select_t = jnp.asarray(order.transpose(0, 2, 1), BF16)
    flat_in = images.reshape(tokens, width)
    flat_cot = cotangent.reshape(tokens, width)
    grid_cot = cotangent.reshape(tokens // RES, RES, width)
    place = jnp.asarray(grid_rows(), BF16)
    place_t = jnp.asarray(grid_rows().T, BF16)
    by_lines = pl.BlockSpec((ROWS // RES, RES, width), lambda i: (i, 0, 0))

    group_rows = GROUP * TOKENS
    groups = count // GROUP
    win_spec = pl.BlockSpec((GROUP, 4 * SLOT, 3 * width), lambda i: (i, 0, 0))
    normed, windows, merged = call(
        attend_kernel,
        groups,
        (flat_in, gain_1, shift_1, attend_w, attend_b, bias, select, select_t),
        [rows_of(group_rows, width)]
        + [whole(a) for a in (gain_1, shift_1, attend_w, attend_b, bias, select, select_t)],
        (
            shape((tokens, width), BF16),
            shape((count, 4 * SLOT, 3 * width), BF16),
            shape((tokens, width), BF16),
        ),
        (rows_of(group_rows, width), win_spec, rows_of(group_rows, width)),
        (pltpu.VMEM((group_rows, 3 * width), BF16),),
        flops=12 * 10**9,
    )
    rest_low = after(rest_low, merged)
    rest = join_bit(rest, rest_low, (lax.axis_index("fsdp") & 1) != 0, len(bits) - 1)
    rest = gather_core(rest.reshape(width, -1), dp).reshape(fsdp, rows, -1)
    out_w = rest[:, :, :width].reshape(width, width)
    exp_w = rest[:, :, width : width + hidden].reshape(width, hidden)
    red_w = (
        rest[:, :, width + hidden :]
        .reshape(fsdp, rows, ratio, width)
        .transpose(0, 2, 1, 3)
        .reshape(hidden, width)
    )
    by_rows = rows_of(ROWS, width)
    by_hidden = rows_of(ROWS, hidden)
    fixed = (out_w, out_b, gain_2, shift_2, exp_w, exp_b, red_w, red_b, place, place_t)
    block_out, grad_mid, act, grad_hid, normed_two, narrow_2, wide_2 = call(
        feed_kernel,
        tokens // ROWS,
        (flat_in, merged, grid_cot) + fixed,
        [by_rows, by_rows, by_lines] + [whole(a) for a in fixed],
        (
            shape(grid_cot.shape, BF16),
            shape((tokens, width), F32),
            shape((tokens, hidden), BF16),
            shape((tokens, hidden), BF16),
            shape((tokens, width), BF16),
            shape((8, width), F32),
            shape((1, hidden), F32),
        ),
        (
            by_lines,
            by_rows,
            by_hidden,
            by_hidden,
            by_rows,
            pl.BlockSpec((8, width), lambda i: (0, 0)),
            pl.BlockSpec((1, hidden), lambda i: (0, 0)),
        ),
        flops=20 * 10**9,
    )
    red_grad = tn(act, flat_cot).astype(BF16)
    exp_grad = tn(normed_two, grad_hid).astype(BF16)
    core = lax.axis_index("dp") % 2
    me = lax.axis_index("fsdp")
    feed = jnp.concatenate(
        [
            exp_grad,
            red_grad.reshape(fsdp, ratio, rows, width)
            .transpose(0, 2, 1, 3)
            .reshape(width, hidden),
        ],
        axis=1,
    )
    kept, sent = keep_and_send(feed, core == 1, 1)
    feed = add_up(kept, [swap(sent, "dp", dp, 1)])
    kept, sent = keep_and_send(feed, (lax.axis_index("dp") & 2) != 0, 1)
    grad_mid = after(grad_mid, sent)
    feed, feed_new = kept, swap(sent, "dp", dp, 2)
    branch, triple, scores, sums = call(
        attend_back_kernel,
        groups,
        (grad_mid, out_w, windows, bias, select, select_t),
        [rows_of(group_rows, width), whole(out_w), win_spec]
        + [whole(a) for a in (bias, select, select_t)],
        (
            shape((tokens, width), BF16),
            shape((tokens, 3 * width), BF16),
            shape((BLOCKS, KEYS, 4 * SLOT), F32),
            shape((1, 3 * width), F32),
        ),
        (
            rows_of(group_rows, width),
            rows_of(group_rows, 3 * width),
            pl.BlockSpec((BLOCKS, KEYS, 4 * SLOT), lambda i: (0, 0, 0)),
            pl.BlockSpec((1, 3 * width), lambda i: (0, 0)),
        ),
        (
            pltpu.VMEM((group_rows, width), BF16),
            pltpu.VMEM((4 * SLOT, 3 * width), BF16),
        ),
        flops=16 * 10**9,
    )
    feed_new = after(feed_new, triple)
    feed = add_up(feed, [feed_new]).reshape((2,) * len(bits) + (rows, -1))
    feed, sent_1, feed_bits = fold_bit(feed, fsdp, 1, bits)
    attend = jnp.concatenate(
        [tn(normed, triple).astype(BF16), tn(merged, branch).astype(BF16)], axis=1
    )
    vectors = (
        sums[0],
        narrow_2[3],
        narrow_2[0],
        narrow_2[1],
        wide_2[0],
        narrow_2[2],
    )
    line = jnp.concatenate([v.reshape(fsdp, -1) for v in vectors], axis=1).astype(BF16)
    line = jnp.pad(line, ((0, 0), (0, attend.shape[1] - line.shape[1])))
    line = jnp.pad(line[:, None], ((0, 0), (0, 15), (0, 0)))
    attend = jnp.concatenate([attend.reshape(fsdp, rows, -1), line], axis=1)
    attend_kept, attend_sent = keep_and_send(attend, core == 1, 2)
    attend = add_up(attend_kept, [swap(attend_sent, "dp", dp, 1)])
    attend = attend.reshape((2,) * len(bits) + attend.shape[1:])
    attend, sent_2, attend_bits = fold_bit(attend, fsdp, 2, bits)
    feed_new = swap(sent_1, "fsdp", fsdp, 1)
    attend_new = swap(sent_2, "fsdp", fsdp, 2)
    triple = after(triple, sent_1, sent_2)
    score_rows = scores.reshape(BLOCKS, KEYS, 4, SLOT).transpose(0, 2, 1, 3).reshape(HEADS, -1)
    table_grad = lax.dot_general(
        onehot.astype(F32), score_rows, (((1,), (1,)), ((), ())), precision=lax.Precision.HIGHEST
    )
    images_grad, narrow_1 = call(
        input_back_kernel,
        tokens // ROWS,
        (triple, attend_w, flat_in, gain_1, grad_mid, place),
        [rows_of(ROWS, 3 * width), whole(attend_w), by_rows, whole(gain_1), by_rows, whole(place)],
        (shape(grid_cot.shape, BF16), shape((8, width), F32)),
        (by_lines, pl.BlockSpec((8, width), lambda i: (0, 0))),
        flops=3 * 10**9,
    )
    feed = add_up(feed, [after(feed_new, images_grad)])
    attend = add_up(attend, [after(attend_new, images_grad)])
    columns = attend.shape[-1]
    shared = jnp.concatenate([narrow_1[:2].reshape(-1), table_grad.reshape(-1)])
    shared_size = shared.shape[0]
    shared = jnp.pad(shared, (0, 16 * columns - shared_size)).reshape(16, columns)

    feed, sent_1, feed_bits = fold_bit(feed, fsdp, 2, feed_bits)
    attend, sent_2, attend_bits = fold_bit(attend, fsdp, 1, attend_bits)
    attend_new, shared_new = split_rows(
        swap(stack_rows(sent_2, shared), "fsdp", fsdp, 1), sent_2, shared
    )
    feed = add_up(feed, [swap(sent_1, "fsdp", fsdp, 2)])
    attend = add_up(attend, [attend_new])
    shared = add_up(shared, [shared_new])
    for bit in bits[2:]:
        feed, sent_1, feed_bits = fold_bit(feed, fsdp, bit, feed_bits)
        attend, sent_2, attend_bits = fold_bit(attend, fsdp, bit, attend_bits)
        feed_new, attend_new, shared_new = split_rows(
            swap(stack_rows(sent_1, sent_2, shared), "fsdp", fsdp, bit), sent_1, sent_2, shared
        )
        feed = add_up(feed, [feed_new])
        attend = add_up(attend, [attend_new])
        shared = add_up(shared, [shared_new])
    for bit in bits_of(dp)[:0:-1]:
        feed_new, attend_new, shared_new = split_rows(
            swap(stack_rows(feed, attend, shared), "dp", dp, bit), feed, attend, shared
        )
        feed = feed.astype(BF16)
        if bit == 2:
            feed = join_bit(feed, feed_new, (lax.axis_index("dp") & bit) != 0, 1)
        else:
            feed = add_up(feed, [feed_new])
        attend = add_up(attend.astype(BF16), [attend_new])
        shared = add_up(shared.astype(BF16), [shared_new])
    shared = shared.astype(BF16)
    attend = attend.astype(BF16)
    feed = feed.astype(BF16)
    feed_parts = jnp.split(feed, feed.shape[1] // columns, axis=1)
    arrived = split_rows(
        swap(stack_rows(*feed_parts, attend, shared), "dp", dp, 1), *feed_parts, attend, shared
    )
    far = lax.ppermute(
        shared,
        ("dp", "fsdp"),
        [
            (d * fsdp + f, (d ^ 1) * fsdp + (f ^ 2))
            for d in range(dp)
            for f in range(fsdp)
        ],
    )
    shared = add_up(shared, [arrived[-1], swap(shared, "fsdp", fsdp, 2), far])
    attend = join_bit(attend, arrived[-2], core == 1, 1).astype(F32)
    feed = join_bit(feed, jnp.concatenate(arrived[:-2], axis=1), core == 1, 1).astype(F32)
    shared = shared.reshape(-1)
    table_grad = shared[2 * width : shared_size].reshape(table_grad.shape)
    vector_grads = [
        lax.dynamic_slice_in_dim(shared, i * width + me * rows, rows, 0) for i in range(2)
    ]
    at = 0
    for vector in vectors:
        size = vector.shape[0] // fsdp
        vector_grads.append(attend[rows, at : at + size])
        at += size
    attend_total = attend[:rows]
    red_shard = (
        feed[:, hidden:]
        .reshape(rows, ratio, width)
        .transpose(1, 0, 2)
        .reshape(ratio * rows, width)
    )
    return (
        block_out.reshape(images.shape),
        images_grad.reshape(images.shape),
        vector_grads[0],
        vector_grads[1],
        attend_total[:, : 3 * width],
        vector_grads[2],
        attend_total[:, 3 * width :],
        vector_grads[3],
        vector_grads[4],
        vector_grads[5],
        feed[:, :hidden],
        vector_grads[6],
        red_shard,
        vector_grads[7],
        table_grad,
    )


def solution(mesh):
    tokens = P(("dp", "fsdp"), None, None, None)
    line, matrix = P("fsdp"), P("fsdp", None)
    weights = (line, line, matrix, line, matrix, line, line, line, matrix, line, matrix, line)
    return jax.shard_map(
        functools.partial(body, mesh.shape["fsdp"], mesh.shape["dp"]),
        mesh=mesh,
        in_specs=(tokens,) + weights + (P(), P(), P(), tokens),
        out_specs=(tokens, tokens) + weights + (P(),),
        check_vma=False,
    )
```

```python
import functools

import jax
import jax.numpy as jnp
import numpy as np
from jax import lax
from jax.experimental import pallas as pl
from jax.experimental.pallas import tpu as pltpu
from jax.sharding import PartitionSpec as P

HEADS = 16
HEAD_DIM = 32
WIN = 7
RES = 14
SHIFT = 3
WIN2 = 49
TOKENS = RES * RES
EPSILON = 1e-05
GROUP = 4
SLOT = 64
KEYS = 56
SPAN = 208
STEP = 192
BLOCKS = 4
LANES = 128
ROWS = 224
CHUNK = 512
VMEM = 60 * 1024 * 1024
F32 = jnp.float32
BF16 = jnp.bfloat16


def window_order():
    select = np.zeros((GROUP, 4 * SLOT, SPAN), np.float32)
    for image in range(GROUP):
        for wi in range(2):
            for wj in range(2):
                for ti in range(WIN):
                    for tj in range(WIN):
                        row = (wi * 2 + wj) * SLOT + ti * WIN + tj
                        si = (wi * WIN + ti + SHIFT) % RES
                        sj = (wj * WIN + tj + SHIFT) % RES
                        select[image, row, si * RES + sj + image * (TOKENS - STEP)] = 1.0
    return select


def dot(left, right, contract):
    return lax.dot_general(left, right, (contract, ((), ())), preferred_element_type=F32)


def nn(left, right):
    return dot(left, right, ((1,), (0,)))


def nt(left, right):
    return dot(left, right, ((1,), (1,)))


def tn(left, right):
    return dot(left, right, ((0,), (0,)))


def norm(rows):
    center = rows - jnp.mean(rows, axis=-1, keepdims=True)
    spread = jnp.mean(center * center, axis=-1, keepdims=True)
    scale = lax.rsqrt(spread + EPSILON)
    return center * scale, scale


def norm_back(z, scale, gain, grad):
    g = grad * gain
    return scale * (
        g - jnp.mean(g, axis=-1, keepdims=True) - z * jnp.mean(g * z, axis=-1, keepdims=True)
    )


def head_masks():
    lane = lax.broadcasted_iota(jnp.int32, (SLOT, LANES), 1)
    return [(lane // HEAD_DIM) == j for j in range(4)]


def spread_heads(rows, masks):
    zero = jnp.zeros_like(rows)
    return jnp.concatenate([jnp.where(mask, rows, zero) for mask in masks], axis=0)


def pick_heads(wide, masks):
    total = jnp.where(masks[0], wide[:SLOT], 0.0)
    for j in range(1, 4):
        total = jnp.where(masks[j], wide[j * SLOT : (j + 1) * SLOT], total)
    return total


def pad_keys(rows):
    return jnp.concatenate([rows, jnp.zeros((SLOT - KEYS, rows.shape[1]), F32)], axis=0).astype(
        BF16
    )


def mix(keys, spread_q, bias):
    scores = nt(keys, spread_q)[:KEYS] + bias
    top = jnp.max(scores, axis=0, keepdims=True)
    raised = jnp.exp(scores - top)
    return raised * (1.0 / jnp.sum(raised, axis=0, keepdims=True))


def put_span(ref, start, value, columns=slice(None)):
    head = pl.ds(start, 16)
    tail = pl.ds(pl.multiple_of(start + 16, 16), SPAN - 16)
    ref[head, columns] = ref[head, columns] + value[:16]
    ref[tail, columns] = value[16:]


def pack_kernel(
    ids, attend, vectors, output, expand, reduce, front, rest
):
    rows = attend.shape[0]
    half = attend.shape[1] // 2
    width = output.shape[1]
    front[rows:, :] = jnp.zeros((16, half), BF16)
    front[rows:, : vectors.shape[1]] = vectors[...]
    for core in range(2):

        @pl.when(ids[1] == core)
        def _():
            front[:rows, :] = attend[:, core * half : (core + 1) * half]
            if core == 0:
                for i in range(4):
                    rest[i * rows : (i + 1) * rows] = expand[:, i * width : (i + 1) * width]
            else:
                rest[: 4 * rows] = reduce[...]
            rest[4 * rows :] = output[core * (rows // 2) : (core + 1) * (rows // 2)]


def spread_line(lines, index, size, me):
    members = lines.shape[1]
    bits = members.bit_length() - 1
    piece = lines[index][:, :size]
    column = lax.broadcasted_iota(jnp.int32, (size, members * size), 1)
    inside = lax.broadcasted_iota(jnp.int32, (size, members * size), 0)
    wide = nn(piece, (column % size == inside).astype(BF16))
    place = lax.broadcasted_iota(jnp.int32, wide.shape, 0)
    flipped = sum(((place >> b) & 1) << (bits - 1 - b) for b in range(bits))
    owner = lax.broadcasted_iota(jnp.int32, wide.shape, 1) // size
    return jnp.sum(jnp.where(owner == (flipped ^ me), wide, 0.0), axis=0, keepdims=True)


def flip(place, bits):
    return sum(((place >> b) & 1) << (bits - 1 - b) for b in range(bits))


def attend_kernel(
    ids, images, mine, other, lines, bias, select, select_t, normed, windows, merged, weight, flat
):
    width = images.shape[1]
    me, core = ids[0], ids[1]
    members = mine.shape[0]
    rows = width // members

    @pl.when(pl.program_id(0) == 0)
    def _():
        half = mine.shape[2]
        for own in range(2):

            @pl.when(core == own)
            def _():
                for side, part in ((own, mine), (1 - own, other)):
                    for place in range(members):
                        member = flip(place, members.bit_length() - 1) ^ me
                        at = pl.ds(pl.multiple_of(member * rows, rows), rows)
                        weight[at, side * half : (side + 1) * half] = part[place, :rows, :]

    z, _ = norm(images[...].astype(F32))
    gain = spread_line(lines, 0, rows, me)
    shift = spread_line(lines, 1, rows, me)
    attend_bias = spread_line(lines, 2, 3 * rows, me)
    low = (z * gain + shift).astype(BF16)
    normed[...] = low
    for part in range(3):
        cols = slice(part * width, (part + 1) * width)
        value = nn(low, weight[:, cols]) + attend_bias[:, cols]
        if part == 0:
            value = value * HEAD_DIM**-0.5
        flat[:, cols] = value.astype(BF16)
    merged[:16, :] = jnp.zeros((16, width), BF16)

    def one_image(image, carry):
        start = pl.multiple_of(image * STEP, 16)
        span = flat[pl.ds(start, SPAN), :]
        chosen = select[image]
        windows[image] = nn(chosen, span).astype(BF16)
        masks = head_masks()
        rows = []
        for w in range(4):
            at = slice(w * SLOT, (w + 1) * SLOT)
            parts = []
            for g in range(BLOCKS):
                q, k, v = (
                    windows[image, at, part * width + g * LANES : part * width + (g + 1) * LANES]
                    for part in range(3)
                )
                mixing = mix(k, spread_heads(q, masks), bias[w, g])
                parts.append(pick_heads(tn(pad_keys(mixing), v), masks).astype(BF16))
            rows.append(jnp.concatenate(parts, axis=1))
        context = jnp.concatenate(rows, axis=0)
        put_span(merged, start, nn(select_t[image], context).astype(BF16))
        return carry

    lax.fori_loop(0, GROUP, one_image, 0)


def gelu_parts(t):
    k = 1.0 / (1.0 + (0.3275911 * 0.5**0.5) * jnp.abs(t))
    bell = jnp.exp(-0.5 * (t * t))
    poly = 0.5 * 1.061405429 * k - 0.5 * 1.453152027
    poly = poly * k + 0.5 * 1.421413741
    poly = poly * k - 0.5 * 0.284496736
    poly = poly * k + 0.5 * 0.254829592
    tail = poly * k * bell
    below = jnp.where(t >= 0, 1.0 - tail, tail)
    return t * below, below + t * (bell * 0.3989422804014327)


def feed_kernel(
    ids,
    images,
    merged,
    cot,
    lines,
    near,
    far,
    near_core,
    far_core,
    place,
    place_t,
    block_out,
    flat_cot,
    grad_mid,
    act,
    grad_hid,
    normed_two,
    narrow,
    wide,
    out_w,
    exp_w,
    red_w,
    vectors,
):
    me, core = ids[0], ids[1]
    width = images.shape[1]
    held = near.shape[0]
    rows = width // (2 * held)

    @pl.when(pl.program_id(0) == 0)
    def _():
        narrow[...] = jnp.zeros_like(narrow)
        wide[...] = jnp.zeros_like(wide)
        for i, index in enumerate((3, 4, 5, 7)):
            vectors[i : i + 1, :width] = spread_line(lines, index, rows, me)
        vectors[4:5, :] = spread_line(lines, 6, 4 * rows, me)
        for own in range(2):

            @pl.when(core == own)
            def _():
                for side, parts in ((own, (near, far)), (1 - own, (near_core, far_core))):
                    for odd, part in enumerate(parts):
                        for at in range(held):
                            member = ((flip(at, held.bit_length() - 1) << 1) | odd) ^ me
                            if side == 0:
                                to = pl.ds(pl.multiple_of(member * rows, rows), rows)
                                for i in range(4):
                                    exp_w[to, i * width : (i + 1) * width] = part[
                                        at, i * rows : (i + 1) * rows, :
                                    ]
                            else:
                                to = pl.ds(pl.multiple_of(member * 4 * rows, 4 * rows), 4 * rows)
                                red_w[to, :] = part[at, : 4 * rows, :]
                            half = rows // 2
                            to = pl.ds(pl.multiple_of(member * rows + side * half, half), half)
                            out_w[to, :] = part[at, 4 * rows :, :]

    middle = images[...].astype(F32) + nn(merged[...], out_w[...]) + vectors[0:1, :width]
    z, scale = norm(middle)
    scaled = vectors[1:2, :width]
    low = (z * scaled + vectors[2:3, :width]).astype(BF16)
    normed_two[...] = low
    grad = from_grid(cot[...], place_t[...])
    flat_cot[...] = grad
    result = middle + vectors[3:4, :width]
    grad_y = jnp.zeros_like(middle)
    for c in range(exp_w.shape[1] // CHUNK):
        at = slice(c * CHUNK, (c + 1) * CHUNK)
        hidden = nn(low, exp_w[:, at]) + vectors[4:5, at]
        grad_act = nt(grad, red_w[at, :])
        active, slope = gelu_parts(hidden)
        active = active.astype(BF16)
        act[:, at] = active
        grad_h = (grad_act * slope).astype(BF16)
        grad_hid[:, at] = grad_h
        wide[:, at] += jnp.sum(grad_h.astype(F32), axis=0, keepdims=True)
        result = result + nn(active, red_w[at, :])
        grad_y = grad_y + nt(grad_h, exp_w[:, at])
    block_out[...] = to_grid(result.astype(BF16), place[...])
    wide_cot = grad.astype(F32)
    grad_middle = wide_cot + norm_back(z, scale, scaled, grad_y)
    grad_mid[...] = grad_middle
    narrow[0:1] += jnp.sum(grad_y * z, axis=0, keepdims=True)
    narrow[1:2] += jnp.sum(grad_y, axis=0, keepdims=True)
    narrow[2:3] += jnp.sum(wide_cot, axis=0, keepdims=True)
    narrow[3:4] += jnp.sum(grad_middle.astype(BF16).astype(F32), axis=0, keepdims=True)


def feed_grad_kernel(ids, act, grad_hid, cot, normed_two, out):
    me, core, second = ids[0], ids[1], ids[2]
    step = pl.program_id(0)
    members, half = out.shape[2], out.shape[3]
    rows = half // 2
    grad = tn(act[...], cot[...]).astype(BF16)
    count = grad.shape[0] // (2 * half)
    for i in range(count):
        for h in range(2):
            at = (2 * i + h) * half
            out[core, h ^ second, (step * count + i) ^ me] = grad[at : at + half]
    grad = tn(normed_two[...], grad_hid[...]).astype(BF16)
    to = pl.ds(pl.multiple_of((step % 2) * rows, rows), rows)
    for member in range(members):
        out[1 - core, (step // 2) ^ second, member ^ me, to, :] = grad[
            member * rows : (member + 1) * rows
        ]


def attend_grad_kernel(ids, normed, triple, merged, branch, out):
    me, core = ids[0], ids[1]
    step = pl.program_id(0)
    members = out.shape[1]
    rows = out.shape[2] // 2

    def store(grad):
        low = grad.astype(BF16)
        to = pl.ds(pl.multiple_of((step % 2) * rows, rows), rows)
        for member in range(members):
            out[(step // 2) ^ core, member ^ me, to, :] = low[member * rows : (member + 1) * rows]

    @pl.when(step < 3)
    def _():
        store(tn(normed[...], triple[...]))

    @pl.when(step == 3)
    def _():
        store(tn(merged[...], branch[...]))


def unpack_kernel(ids, attend, feed_0, feed_1, arrived, attend_w, out_w, exp_w, red_w):
    core, second = ids[1], ids[2]
    size = attend.shape[0]
    rows = size // 2
    width = attend.shape[1]

    def place(side, attend_part, feeds):
        if side == 0:
            attend_w[:, :width] = attend_part[:rows].astype(F32)
            attend_w[:, width : 2 * width] = attend_part[rows:].astype(F32)
        else:
            attend_w[:, 2 * width :] = attend_part[:rows].astype(F32)
            out_w[...] = attend_part[rows:].astype(F32)
        for h, part in enumerate(feeds):
            if side == 0:
                red_w[h * size : (h + 1) * size] = part.astype(F32)
            else:
                at = 2 * h * width
                exp_w[:, at : at + width] = part[:rows].astype(F32)
                exp_w[:, at + width : at + 2 * width] = part[rows:].astype(F32)

    for own in range(2):
        for y in range(2):

            @pl.when((core == own) & (second == y))
            def _():
                place(own, attend[...], (feed_0[...], feed_1[...])[:: 1 - 2 * y])
                parts = [arrived[i * size : (i + 1) * size, :] for i in range(3)]
                place(1 - own, parts[2], parts[:2][:: 1 - 2 * y])


def attend_back_kernel(
    ids, grad_mid, out_w, windows, bias, select, select_t, branch, triple, scores, sums, flat, tiles
):
    width = grad_mid.shape[1]

    @pl.when(pl.program_id(0) == 0)
    def _():
        scores[...] = jnp.zeros_like(scores)
        sums[...] = jnp.zeros_like(sums)

    low = grad_mid[...].astype(BF16)
    branch[...] = low
    flat[...] = nt(low, out_w[...]).astype(BF16)
    triple[:16, :] = jnp.zeros((16, 3 * width), BF16)

    def one_image(image, carry):
        start = pl.multiple_of(image * STEP, 16)
        context = nn(select[image], flat[pl.ds(start, SPAN), :]).astype(BF16)
        masks = head_masks()
        for w in range(4):
            at = slice(w * SLOT, (w + 1) * SLOT)
            for g in range(BLOCKS):
                cols = [
                    slice(part * width + g * LANES, part * width + (g + 1) * LANES)
                    for part in range(3)
                ]
                q, k, v = (windows[image, at, c] for c in cols)
                grad_c = context[at, g * LANES : (g + 1) * LANES]
                spread_q = spread_heads(q, masks)
                spread_g = spread_heads(grad_c, masks)
                mixing = mix(k, spread_q, bias[w, g])
                grad_v = nn(pad_keys(mixing), spread_g)
                grad_m = nt(v, spread_g)[:KEYS]
                inner = jnp.sum(grad_m * mixing, axis=0, keepdims=True)
                grad_s = pad_keys(mixing * (grad_m - inner))
                scores[g] += grad_s.astype(F32)[:KEYS]
                grad_k = nn(grad_s, spread_q)
                grad_q = pick_heads(tn(grad_s, k), masks) * HEAD_DIM**-0.5
                for c, value in zip(cols, (grad_q, grad_k, grad_v)):
                    tiles[at, c] = value.astype(BF16)
        sums[...] += jnp.sum(tiles[...].astype(F32), axis=0, keepdims=True)
        put_span(triple, start, nn(select_t[image], tiles[...]).astype(BF16))
        return carry

    lax.fori_loop(0, GROUP, one_image, 0)


def input_back_kernel(
    ids, triple, weight, images, lines, grad_mid, place, images_grad, narrow
):
    @pl.when(pl.program_id(0) == 0)
    def _():
        narrow[...] = jnp.zeros_like(narrow)

    grad_n = nt(triple[...], weight[...])
    z, scale = norm(images[...].astype(F32))
    gain = spread_line(lines, 0, lines.shape[2] // 4, ids[0])
    back = norm_back(z, scale, gain, grad_n)
    images_grad[...] = to_grid((grad_mid[...] + back).astype(BF16), place[...])
    narrow[0:1] += jnp.sum(grad_n * z, axis=0, keepdims=True)
    narrow[1:2] += jnp.sum(grad_n, axis=0, keepdims=True)


def grid_rows():
    place = np.zeros((ROWS // RES * 16, ROWS), np.float32)
    for token in range(ROWS):
        place[token // RES * 16 + token % RES, token] = 1.0
    return place


def from_grid(block, place_t):
    lines = block.shape[0]
    padded = jnp.concatenate([block, jnp.zeros((lines, 16 - RES, block.shape[2]), BF16)], axis=1)
    return nn(place_t, padded.reshape(lines * 16, block.shape[2])).astype(BF16)


def to_grid(rows, place):
    padded = nn(place, rows).astype(BF16)
    return padded.reshape(-1, 16, rows.shape[1])[:, :RES]


def whole(array):
    return pl.BlockSpec(array.shape, lambda i, ids: (0,) * array.ndim)


def rows_of(count, width):
    return pl.BlockSpec((count, width), lambda i, ids: (i, 0))


def call(kernel, steps, ids, args, specs, outs, out_specs, scratch=(), flops=0):
    moved = sum(a.size * a.dtype.itemsize for a in args) + sum(
        o.size * o.dtype.itemsize for o in outs
    )
    return pl.pallas_call(
        kernel,
        grid_spec=pltpu.PrefetchScalarGridSpec(
            num_scalar_prefetch=1,
            grid=(steps,),
            in_specs=specs,
            out_specs=out_specs,
            scratch_shapes=list(scratch),
        ),
        out_shape=outs,
        compiler_params=pltpu.CompilerParams(vmem_limit_bytes=VMEM),
        cost_estimate=pl.CostEstimate(flops=flops, bytes_accessed=moved, transcendentals=0),
    )(ids, *args)


def shape(dims, kind):
    return jax.ShapeDtypeStruct(dims, kind)


def window_bias(region_labels, position_index, position_table):
    across = RES // WIN
    labels = (
        region_labels.reshape(across, WIN, across, WIN).transpose(0, 2, 1, 3).reshape(-1, WIN2)
    )
    masking = jnp.where(labels[:, :, None] == labels[:, None, :], 0.0, -100.0).astype(F32)
    index = jnp.pad(
        position_index.T, ((0, KEYS - WIN2), (0, SLOT - WIN2)), constant_values=-1
    ).reshape(-1)
    onehot = (jnp.arange(position_table.shape[0], dtype=jnp.int32)[:, None] == index[None]).astype(
        BF16
    )
    looked = dot(position_table, onehot, ((0,), (0,)))
    looked = looked.reshape(BLOCKS, 4, KEYS, SLOT).transpose(0, 2, 1, 3)
    masking = jnp.pad(masking, ((0, 0), (0, KEYS - WIN2), (0, SLOT - WIN2)))
    bias = looked[None] + masking[:, None, :, None, :]
    real = lax.broadcasted_iota(jnp.int32, bias.shape, 2) < WIN2
    bias = jnp.where(real, bias, -1e30).reshape(4, BLOCKS, KEYS, 4 * SLOT)
    return bias, onehot


def bits_of(size):
    return [1 << b for b in range(size.bit_length() - 1)]


def swap(value, axis, size, bit):
    return lax.ppermute(value, axis, [(i, i ^ bit) for i in range(size)])


def after(value, *others):
    return lax.optimization_barrier((value,) + others)[0]


def take(value, axis, side):
    return lax.index_in_dim(value, side, axis, keepdims=False)


def add_up(kept, arrived):
    total = kept.astype(F32)
    for value in arrived:
        total = total + value.astype(F32)
    return total


def stack_rows(*values):
    return jnp.concatenate([v.reshape(-1, v.shape[-1]).astype(BF16) for v in values], axis=0)


def split_rows(stacked, *like):
    out, at = [], 0
    for value in like:
        size = value.size // value.shape[-1]
        out.append(stacked[at : at + size].reshape(value.shape))
        at += size
    return out


def body(fsdp, dp, *args):
    (
        images,
        input_gain,
        input_shift,
        attend_weight,
        attend_bias,
        output_weight,
        output_bias,
        second_gain,
        second_shift,
        expand_weight,
        expand_bias,
        reduce_weight,
        reduce_bias,
        position_table,
        region_labels,
        position_index,
        cotangent,
    ) = args
    count = images.shape[0]
    width = images.shape[-1]
    rows = attend_weight.shape[0]
    hidden = expand_weight.shape[1]
    tokens = count * TOKENS
    me, dp_me = lax.axis_index("fsdp"), lax.axis_index("dp")
    ids = jnp.stack([me, dp_me % 2, (dp_me // 2) % 2]).astype(jnp.int32)
    bits = bits_of(fsdp)
    vectors = (
        input_gain,
        input_shift,
        attend_bias,
        output_bias,
        second_gain,
        second_shift,
        expand_bias,
        reduce_bias,
    )
    widest = expand_bias.shape[0]
    small = sum(
        jnp.pad(v[None], ((i, 15 - i), (0, widest - v.shape[0]))) for i, v in enumerate(vectors)
    )
    shards = (attend_weight, small, output_weight, expand_weight, reduce_weight)
    packed = (
        shape((rows + 16, 3 * width // 2), BF16),
        shape((4 * rows + rows // 2, width), BF16),
    )
    front, rest = call(
        pack_kernel,
        1,
        ids,
        shards,
        [whole(a) for a in shards],
        packed,
        [whole(a) for a in packed],
    )
    front, rest = front[None], rest[None]
    for bit in reversed(bits):
        front = jnp.concatenate([front, swap(front, "fsdp", fsdp, bit)], axis=0)
        if bit != 1:
            rest = jnp.concatenate(
                [rest, swap(after(rest, front), "fsdp", fsdp, bit)], axis=0
            )
    front_core = swap(front, "dp", dp, 1)
    lines = front[:, rows:, :widest].transpose(1, 0, 2)
    near = rest
    near_core = swap(near, "dp", dp, 1)
    far = swap(near, "fsdp", fsdp, 1)
    front = after(front, near)

    bias, onehot = window_bias(region_labels, position_index, position_table)
    order = window_order()
    select = jnp.asarray(order, BF16)
    select_t = jnp.asarray(order.transpose(0, 2, 1), BF16)
    flat_in = images.reshape(tokens, width)
    grid_cot = cotangent.reshape(tokens // RES, RES, width)
    place = jnp.asarray(grid_rows(), BF16)
    place_t = jnp.asarray(grid_rows().T, BF16)
    by_lines = pl.BlockSpec((ROWS // RES, RES, width), lambda i, ids: (i, 0, 0))

    group_rows = GROUP * TOKENS
    groups = count // GROUP
    by_group = rows_of(group_rows, width)
    win_spec = pl.BlockSpec((GROUP, 4 * SLOT, 3 * width), lambda i, ids: (i, 0, 0))
    fixed = (front, front_core, lines, bias, select, select_t)
    attend_w = shape((width, 3 * width), BF16)
    normed, windows, merged, attend_w = call(
        attend_kernel,
        groups,
        ids,
        (flat_in,) + fixed,
        [by_group] + [whole(a) for a in fixed],
        (
            shape((tokens, width), BF16),
            shape((count, 4 * SLOT, 3 * width), BF16),
            shape((tokens, width), BF16),
            attend_w,
        ),
        (by_group, win_spec, by_group, whole(attend_w)),
        (pltpu.VMEM((group_rows, 3 * width), BF16),),
        flops=12 * 10**9,
    )
    far = after(far, merged)
    far_core = swap(far, "dp", dp, 1)
    by_rows = rows_of(ROWS, width)
    by_hidden = rows_of(ROWS, hidden)
    fixed = (lines, near, far, near_core, far_core, place, place_t)
    sums_out = (shape((8, width), F32), shape((1, hidden), F32), shape((width, width), BF16))
    block_out, flat_cot, grad_mid, act, grad_hid, normed_two, narrow_2, wide_2, out_w = call(
        feed_kernel,
        tokens // ROWS,
        ids,
        (flat_in, merged, grid_cot) + fixed,
        [by_rows, by_rows, by_lines] + [whole(a) for a in fixed],
        (
            shape(grid_cot.shape, BF16),
            shape((tokens, width), BF16),
            shape((tokens, width), F32),
            shape((tokens, hidden), BF16),
            shape((tokens, hidden), BF16),
            shape((tokens, width), BF16),
        )
        + sums_out,
        [by_lines, by_rows, by_rows, by_hidden, by_hidden, by_rows]
        + [whole(a) for a in sums_out],
        (
            pltpu.VMEM((width, hidden), BF16),
            pltpu.VMEM((hidden, width), BF16),
            pltpu.VMEM((8, hidden), F32),
        ),
        flops=20 * 10**9,
    )
    feed = shape((2, 2, fsdp, 2 * rows, width), BF16)
    column = pl.BlockSpec((tokens, width), lambda i, ids: (0, i))
    feed = call(
        feed_grad_kernel,
        hidden // width,
        ids,
        (act, grad_hid, flat_cot, normed_two),
        [column, column, whole(flat_cot), whole(normed_two)],
        (feed,),
        [whole(feed)],
        flops=7 * 10**9,
    )[0]
    arrived = swap(feed[1], "dp", dp, 1)
    feed = add_up(feed[0], [arrived])
    sent = feed[1].astype(BF16)
    grad_mid = after(grad_mid, sent)
    feed = feed[0]
    feed_new = swap(sent, "dp", dp, 2)
    fixed = (bias, select, select_t)
    score_out = (shape((BLOCKS, KEYS, 4 * SLOT), F32), shape((1, 3 * width), F32))
    branch, triple, scores, sums = call(
        attend_back_kernel,
        groups,
        ids,
        (grad_mid, out_w, windows) + fixed,
        [by_group, whole(out_w), win_spec] + [whole(a) for a in fixed],
        (shape((tokens, width), BF16), shape((tokens, 3 * width), BF16)) + score_out,
        [by_group, rows_of(group_rows, 3 * width)] + [whole(a) for a in score_out],
        (
            pltpu.VMEM((group_rows, width), BF16),
            pltpu.VMEM((4 * SLOT, 3 * width), BF16),
        ),
        flops=16 * 10**9,
    )
    feed_new = after(feed_new, triple)
    feed = add_up(feed, [feed_new]).reshape((2,) * len(bits) + (2 * rows, width))
    first, second = len(bits) - 1, len(bits) - 2
    sent_1 = take(feed, first, 1).astype(BF16)
    feed = take(feed, first, 0)
    attend = shape((2, fsdp, 2 * rows, width), BF16)
    attend = call(
        attend_grad_kernel,
        4,
        ids,
        (normed, triple, merged, branch),
        [
            whole(normed),
            pl.BlockSpec((tokens, width), lambda i, ids: (0, jnp.minimum(i, 2))),
            whole(merged),
            whole(branch),
        ],
        (attend,),
        [whole(attend)],
        flops=3 * 10**9,
    )[0]
    attend = add_up(attend[0], [swap(attend[1], "dp", dp, 1)])
    attend = attend.reshape((2,) * len(bits) + attend.shape[1:])
    sent_2 = take(attend, second, 1).astype(BF16)
    attend = take(attend, second, 0)
    feed_new = swap(sent_1, "fsdp", fsdp, 1)
    attend_new = swap(sent_2, "fsdp", fsdp, 2)
    triple = after(triple, sent_1, sent_2)
    score_rows = scores.reshape(BLOCKS, KEYS, 4, SLOT).transpose(0, 2, 1, 3).reshape(HEADS, -1)
    table_grad = lax.dot_general(
        onehot.astype(F32), score_rows, (((1,), (1,)), ((), ())), precision=lax.Precision.HIGHEST
    )
    images_grad, narrow_1 = call(
        input_back_kernel,
        tokens // ROWS,
        ids,
        (triple, attend_w, flat_in, lines, grad_mid, place),
        [rows_of(ROWS, 3 * width), whole(attend_w), by_rows, whole(lines), by_rows, whole(place)],
        (shape(grid_cot.shape, BF16), sums_out[0]),
        [by_lines, whole(sums_out[0])],
        flops=3 * 10**9,
    )
    feed = add_up(feed, [after(feed_new, images_grad)])
    attend = add_up(attend, [after(attend_new, images_grad)])
    table_rows = -(-table_grad.size // width)
    table_part = jnp.pad(table_grad.reshape(-1), (0, table_rows * width - table_grad.size))
    shared = jnp.concatenate(
        [
            narrow_1[:2],
            sums.reshape(3, width),
            narrow_2[3:4],
            narrow_2[:2],
            wide_2.reshape(4, width),
            narrow_2[2:3],
            table_part.reshape(table_rows, width),
        ],
        axis=0,
    )
    shared = jnp.pad(shared, ((0, 32 - shared.shape[0]), (0, 0))).astype(BF16)

    first, second = first - 1, len(bits) - 2
    sent_1 = take(feed, first, 1)
    feed = take(feed, first, 0)
    sent_2 = take(attend, second, 1)
    attend = take(attend, second, 0)
    attend_new, shared_new = split_rows(
        swap(stack_rows(sent_2, shared), "fsdp", fsdp, 1), sent_2, shared
    )
    feed = add_up(feed, [swap(sent_1.astype(BF16), "fsdp", fsdp, 2)])
    attend = add_up(attend, [attend_new])
    shared = add_up(shared, [shared_new])
    for bit in bits[2:]:
        last = feed.ndim - 3
        sent_1, feed = take(feed, last, 1), take(feed, last, 0)
        sent_2, attend = take(attend, last, 1), take(attend, last, 0)
        feed_new, attend_new, shared_new = split_rows(
            swap(stack_rows(sent_1, sent_2, shared), "fsdp", fsdp, bit), sent_1, sent_2, shared
        )
        feed = add_up(feed, [feed_new])
        attend = add_up(attend, [attend_new])
        shared = add_up(shared, [shared_new])
    feed, attend, shared = feed.astype(BF16), attend.astype(BF16), shared.astype(BF16)
    for bit in bits_of(dp)[:0:-1]:
        feed_new, attend_new, shared_new = split_rows(
            swap(stack_rows(feed, attend, shared), "dp", dp, bit), feed, attend, shared
        )
        attend = add_up(attend, [attend_new]).astype(BF16)
        shared = add_up(shared, [shared_new]).astype(BF16)
        if bit != 2:
            feed = add_up(feed, [feed_new]).astype(BF16)
    arrived = swap(stack_rows(feed, feed_new, attend, shared), "dp", dp, 1)
    across = lax.ppermute(
        shared,
        ("dp", "fsdp"),
        [(d * fsdp + f, (d ^ 1) * fsdp + (f ^ 2)) for d in range(dp) for f in range(fsdp)],
    )
    near = swap(shared, "fsdp", fsdp, 2)
    shared = add_up(shared, [arrived[6 * rows :], near, across])
    grads = (
        shape((rows, 3 * width), F32),
        shape((rows, width), F32),
        shape((rows, hidden), F32),
        shape((4 * rows, width), F32),
    )
    operands = (attend, feed, feed_new, arrived)
    attend_grad, out_grad, exp_grad, red_grad = call(
        unpack_kernel,
        1,
        ids,
        operands,
        [whole(a) for a in operands],
        grads,
        [whole(a) for a in grads],
    )
    vector_grads = []
    at = 0
    for vector in vectors:
        size = vector.shape[0]
        count_rows = size * fsdp // width
        line = shared[at : at + count_rows].reshape(-1)
        vector_grads.append(lax.dynamic_slice_in_dim(line, me * size, size, 0))
        at += count_rows
    table_grad = shared[at : at + table_rows].reshape(-1)[: table_grad.size].reshape(
        table_grad.shape
    )
    return (
        block_out.reshape(images.shape),
        images_grad.reshape(images.shape),
        vector_grads[0],
        vector_grads[1],
        attend_grad,
        vector_grads[2],
        out_grad,
        vector_grads[3],
        vector_grads[4],
        vector_grads[5],
        exp_grad,
        vector_grads[6],
        red_grad,
        vector_grads[7],
        table_grad,
    )


def solution(mesh):
    tokens = P(("dp", "fsdp"), None, None, None)
    line, matrix = P("fsdp"), P("fsdp", None)
    weights = (line, line, matrix, line, matrix, line, line, line, matrix, line, matrix, line)
    return jax.shard_map(
        functools.partial(body, mesh.shape["fsdp"], mesh.shape["dp"]),
        mesh=mesh,
        in_specs=(tokens,) + weights + (P(), P(), P(), tokens),
        out_specs=(tokens, tokens) + weights + (P(),),
        check_vma=False,
    )
```

```python
import functools

import jax
import jax.numpy as jnp
import numpy as np
from jax import lax
from jax.experimental import pallas as pl
from jax.experimental.pallas import tpu as pltpu
from jax.sharding import PartitionSpec as P

HEADS = 16
HEAD_DIM = 32
WIN = 7
RES = 14
SHIFT = 3
WIN2 = 49
TOKENS = RES * RES
EPSILON = 1e-05
GROUP = 4
SLOT = 64
KEYS = 56
SPAN = 208
STEP = 192
BLOCKS = 4
LANES = 128
ROWS = 784
PIECE = 112
CHUNK = 1024
VMEM = 60 * 1024 * 1024
F32 = jnp.float32
BF16 = jnp.bfloat16


def window_order():
    select = np.zeros((GROUP, 4 * SLOT, SPAN), np.float32)
    for image in range(GROUP):
        for wi in range(2):
            for wj in range(2):
                for ti in range(WIN):
                    for tj in range(WIN):
                        row = (wi * 2 + wj) * SLOT + ti * WIN + tj
                        si = (wi * WIN + ti + SHIFT) % RES
                        sj = (wj * WIN + tj + SHIFT) % RES
                        select[image, row, si * RES + sj + image * (TOKENS - STEP)] = 1.0
    return select


def dot(left, right, contract):
    return lax.dot_general(left, right, (contract, ((), ())), preferred_element_type=F32)


def nn(left, right):
    return dot(left, right, ((1,), (0,)))


def nt(left, right):
    return dot(left, right, ((1,), (1,)))


def tn(left, right):
    return dot(left, right, ((0,), (0,)))


def norm(rows):
    center = rows - jnp.mean(rows, axis=-1, keepdims=True)
    spread = jnp.mean(center * center, axis=-1, keepdims=True)
    scale = lax.rsqrt(spread + EPSILON)
    return center * scale, scale


def norm_back(z, scale, gain, grad):
    g = grad * gain
    return scale * (
        g - jnp.mean(g, axis=-1, keepdims=True) - z * jnp.mean(g * z, axis=-1, keepdims=True)
    )


def head_masks():
    lane = lax.broadcasted_iota(jnp.int32, (SLOT, LANES), 1)
    return [(lane // HEAD_DIM) == j for j in range(4)]


def spread_heads(rows, masks):
    zero = jnp.zeros_like(rows)
    return jnp.concatenate([jnp.where(mask, rows, zero) for mask in masks], axis=0)


def pick_heads(wide, masks):
    total = jnp.where(masks[0], wide[:SLOT], 0.0)
    for j in range(1, 4):
        total = jnp.where(masks[j], wide[j * SLOT : (j + 1) * SLOT], total)
    return total


def pad_keys(rows):
    return jnp.concatenate([rows, jnp.zeros((SLOT - KEYS, rows.shape[1]), F32)], axis=0).astype(
        BF16
    )


def mix(keys, spread_q, bias):
    scores = nt(keys, spread_q)[:KEYS] + bias
    top = jnp.max(scores, axis=0, keepdims=True)
    raised = jnp.exp(scores - top)
    return raised * (1.0 / jnp.sum(raised, axis=0, keepdims=True))


def put_span(ref, start, value, columns=slice(None)):
    head = pl.ds(start, 16)
    tail = pl.ds(pl.multiple_of(start + 16, 16), SPAN - 16)
    ref[head, columns] = ref[head, columns] + value[:16]
    ref[tail, columns] = value[16:]


def pack_kernel(
    ids, attend, vectors, output, expand, reduce, front, rest
):
    rows = attend.shape[0]
    half = attend.shape[1] // 2
    width = output.shape[1]
    front[rows:, :] = jnp.zeros((16, half), BF16)
    front[rows:, : vectors.shape[1]] = vectors[...]
    for core in range(2):

        @pl.when(ids[1] == core)
        def _():
            front[:rows, :] = attend[:, core * half : (core + 1) * half]
            if core == 0:
                for i in range(4):
                    rest[i * rows : (i + 1) * rows] = expand[:, i * width : (i + 1) * width]
            else:
                rest[: 4 * rows] = reduce[...]
            rest[4 * rows :] = output[core * (rows // 2) : (core + 1) * (rows // 2)]


def spread_line(lines, index, size, me):
    members = lines.shape[1]
    bits = members.bit_length() - 1
    piece = lines[index][:, :size]
    column = lax.broadcasted_iota(jnp.int32, (size, members * size), 1)
    inside = lax.broadcasted_iota(jnp.int32, (size, members * size), 0)
    wide = nn(piece, (column % size == inside).astype(BF16))
    place = lax.broadcasted_iota(jnp.int32, wide.shape, 0)
    flipped = sum(((place >> b) & 1) << (bits - 1 - b) for b in range(bits))
    owner = lax.broadcasted_iota(jnp.int32, wide.shape, 1) // size
    return jnp.sum(jnp.where(owner == (flipped ^ me), wide, 0.0), axis=0, keepdims=True)


def flip(place, bits):
    return sum(((place >> b) & 1) << (bits - 1 - b) for b in range(bits))


def attend_kernel(
    ids, images, mine, other, lines, bias, select, select_t, normed, windows, merged, weight, flat
):
    width = images.shape[1]
    me, core = ids[0], ids[1]
    members = mine.shape[0]
    rows = width // members

    @pl.when(pl.program_id(0) == 0)
    def _():
        half = mine.shape[2]
        for own in range(2):

            @pl.when(core == own)
            def _():
                for side, part in ((own, mine), (1 - own, other)):
                    for place in range(members):
                        member = flip(place, members.bit_length() - 1) ^ me
                        at = pl.ds(pl.multiple_of(member * rows, rows), rows)
                        weight[at, side * half : (side + 1) * half] = part[place, :rows, :]

    z, _ = norm(images[...].astype(F32))
    gain = spread_line(lines, 0, rows, me)
    shift = spread_line(lines, 1, rows, me)
    attend_bias = spread_line(lines, 2, 3 * rows, me)
    low = (z * gain + shift).astype(BF16)
    normed[...] = low
    for part in range(3):
        cols = slice(part * width, (part + 1) * width)
        value = nn(low, weight[:, cols]) + attend_bias[:, cols]
        if part == 0:
            value = value * HEAD_DIM**-0.5
        flat[:, cols] = value.astype(BF16)
    merged[:16, :] = jnp.zeros((16, width), BF16)

    def one_image(image, carry):
        start = pl.multiple_of(image * STEP, 16)
        span = flat[pl.ds(start, SPAN), :]
        chosen = select[image]
        windows[image] = nn(chosen, span).astype(BF16)
        masks = head_masks()
        rows = []
        for w in range(4):
            at = slice(w * SLOT, (w + 1) * SLOT)
            parts = []
            for g in range(BLOCKS):
                q, k, v = (
                    windows[image, at, part * width + g * LANES : part * width + (g + 1) * LANES]
                    for part in range(3)
                )
                mixing = mix(k, spread_heads(q, masks), bias[w, g])
                parts.append(pick_heads(tn(pad_keys(mixing), v), masks).astype(BF16))
            rows.append(jnp.concatenate(parts, axis=1))
        context = jnp.concatenate(rows, axis=0)
        put_span(merged, start, nn(select_t[image], context).astype(BF16))
        return carry

    lax.fori_loop(0, GROUP, one_image, 0)


def gelu_parts(t):
    k = 1.0 / (1.0 + (0.3275911 * 0.5**0.5) * jnp.abs(t))
    bell = jnp.exp(-0.5 * (t * t))
    poly = 0.5 * 1.061405429 * k - 0.5 * 1.453152027
    poly = poly * k + 0.5 * 1.421413741
    poly = poly * k - 0.5 * 0.284496736
    poly = poly * k + 0.5 * 0.254829592
    tail = poly * k * bell
    below = jnp.where(t >= 0, 1.0 - tail, tail)
    return t * below, below + t * (bell * 0.3989422804014327)


def sum_tiles(left, right, columns, side):
    total = None
    for tile in range(left.shape[0]):
        cols = [slice(None), slice(None)]
        cols[side] = columns
        part = tn(left[tile, :, cols[0]], right[tile, :, cols[1]])
        total = part if total is None else total + part
    return total.astype(BF16)


def put_feed_grad(ids, step, act, grad_hid, cot, normed_two, out):
    me, core, second = ids[0], ids[1], ids[2]
    members, half = out.shape[2], out.shape[3]
    rows = half // 2
    width = cot.shape[2]
    columns = pl.ds(pl.multiple_of(step * width, width), width)
    grad = sum_tiles(act, cot, columns, 0)
    count = grad.shape[0] // (2 * half)
    for i in range(count):
        for h in range(2):
            at = (2 * i + h) * half
            out[core, h ^ second, (step * count + i) ^ me] = grad[at : at + half]
    grad = sum_tiles(normed_two, grad_hid, columns, 1)
    to = pl.ds(pl.multiple_of((step % 2) * rows, rows), rows)
    for member in range(members):
        out[1 - core, (step // 2) ^ second, member ^ me, to, :] = grad[
            member * rows : (member + 1) * rows
        ]


def feed_kernel(
    ids,
    images,
    merged,
    cot,
    lines,
    near,
    far,
    near_core,
    far_core,
    place,
    place_t,
    block_out,
    grad_mid,
    narrow,
    wide,
    out_w,
    feed_grad,
    exp_w,
    red_w,
    vectors,
    cot_all,
    normed_all,
    act_all,
    grad_all,
):
    me, core = ids[0], ids[1]
    step = pl.program_id(0)
    tiles = act_all.shape[0]
    width = images.shape[1]
    held = near.shape[0]
    rows = width // (2 * held)

    @pl.when(pl.program_id(0) == 0)
    def _():
        narrow[...] = jnp.zeros_like(narrow)
        wide[...] = jnp.zeros_like(wide)
        for i, index in enumerate((3, 4, 5, 7)):
            vectors[i : i + 1, :width] = spread_line(lines, index, rows, me)
        vectors[4:5, :] = spread_line(lines, 6, 4 * rows, me)
        for own in range(2):

            @pl.when(core == own)
            def _():
                for side, parts in ((own, (near, far)), (1 - own, (near_core, far_core))):
                    for odd, part in enumerate(parts):
                        for at in range(held):
                            member = ((flip(at, held.bit_length() - 1) << 1) | odd) ^ me
                            if side == 0:
                                to = pl.ds(pl.multiple_of(member * rows, rows), rows)
                                for i in range(4):
                                    exp_w[to, i * width : (i + 1) * width] = part[
                                        at, i * rows : (i + 1) * rows, :
                                    ]
                            else:
                                to = pl.ds(pl.multiple_of(member * 4 * rows, 4 * rows), 4 * rows)
                                red_w[to, :] = part[at, : 4 * rows, :]
                            half = rows // 2
                            to = pl.ds(pl.multiple_of(member * rows + side * half, half), half)
                            out_w[to, :] = part[at, 4 * rows :, :]

    @pl.when(step < tiles)
    def _():
        middle = images[...].astype(F32) + nn(merged[...], out_w[...]) + vectors[0:1, :width]
        z, scale = norm(middle)
        scaled = vectors[1:2, :width]
        low = (z * scaled + vectors[2:3, :width]).astype(BF16)
        normed_all[step] = low
        from_grid(cot, place_t, cot_all.at[step])
        grad = cot_all[step]
        result = middle + vectors[3:4, :width]
        grad_y = jnp.zeros_like(middle)
        for c in range(exp_w.shape[1] // CHUNK):
            at = slice(c * CHUNK, (c + 1) * CHUNK)
            hidden = nn(low, exp_w[:, at]) + vectors[4:5, at]
            grad_act = nt(grad, red_w[at, :])
            active, slope = gelu_parts(hidden)
            active = active.astype(BF16)
            act_all[step, :, at] = active
            grad_h = (grad_act * slope).astype(BF16)
            grad_all[step, :, at] = grad_h
            wide[:, at] += jnp.sum(grad_h.astype(F32), axis=0, keepdims=True)
            result = result + nn(active, red_w[at, :])
            grad_y = grad_y + nt(grad_h, exp_w[:, at])
        to_grid(result.astype(BF16), place, block_out)
        wide_cot = grad.astype(F32)
        grad_middle = wide_cot + norm_back(z, scale, scaled, grad_y)
        grad_mid[...] = grad_middle
        narrow[0:1] += jnp.sum(grad_y * z, axis=0, keepdims=True)
        narrow[1:2] += jnp.sum(grad_y, axis=0, keepdims=True)
        narrow[2:3] += jnp.sum(wide_cot, axis=0, keepdims=True)
        narrow[3:4] += jnp.sum(grad_middle.astype(BF16).astype(F32), axis=0, keepdims=True)

    @pl.when(step >= tiles)
    def _():
        put_feed_grad(
            ids, step - tiles, act_all, grad_all, cot_all, normed_all, feed_grad
        )


def unpack_kernel(ids, attend, feed_0, feed_1, arrived, attend_w, out_w, exp_w, red_w):
    core, second = ids[1], ids[2]
    size = attend.shape[0]
    rows = size // 2
    width = attend.shape[1]

    def place(side, attend_part, feeds):
        if side == 0:
            attend_w[:, :width] = attend_part[:rows].astype(F32)
            attend_w[:, width : 2 * width] = attend_part[rows:].astype(F32)
        else:
            attend_w[:, 2 * width :] = attend_part[:rows].astype(F32)
            out_w[...] = attend_part[rows:].astype(F32)
        for h, part in enumerate(feeds):
            if side == 0:
                red_w[h * size : (h + 1) * size] = part.astype(F32)
            else:
                at = 2 * h * width
                exp_w[:, at : at + width] = part[:rows].astype(F32)
                exp_w[:, at + width : at + 2 * width] = part[rows:].astype(F32)

    for own in range(2):
        for y in range(2):

            @pl.when((core == own) & (second == y))
            def _():
                place(own, attend[...], (feed_0[...], feed_1[...])[:: 1 - 2 * y])
                parts = [arrived[i * size : (i + 1) * size, :] for i in range(3)]
                place(1 - own, parts[2], parts[:2][:: 1 - 2 * y])


def attend_back_kernel(
    ids,
    grad_mid,
    out_w,
    windows,
    normed,
    merged,
    bias,
    select,
    select_t,
    triple,
    scores,
    sums,
    attend_grad,
    flat,
    tiles,
    total,
):
    width = grad_mid.shape[1]

    @pl.when(pl.program_id(0) == 0)
    def _():
        scores[...] = jnp.zeros_like(scores)
        sums[...] = jnp.zeros_like(sums)

    low = grad_mid[...].astype(BF16)
    flat[...] = nt(low, out_w[...]).astype(BF16)
    triple[:16, :] = jnp.zeros((16, 3 * width), BF16)

    def one_image(image, carry):
        start = pl.multiple_of(image * STEP, 16)
        context = nn(select[image], flat[pl.ds(start, SPAN), :]).astype(BF16)
        masks = head_masks()
        for w in range(4):
            at = slice(w * SLOT, (w + 1) * SLOT)
            for g in range(BLOCKS):
                cols = [
                    slice(part * width + g * LANES, part * width + (g + 1) * LANES)
                    for part in range(3)
                ]
                q, k, v = (windows[image, at, c] for c in cols)
                grad_c = context[at, g * LANES : (g + 1) * LANES]
                spread_q = spread_heads(q, masks)
                spread_g = spread_heads(grad_c, masks)
                mixing = mix(k, spread_q, bias[w, g])
                grad_v = nn(pad_keys(mixing), spread_g)
                grad_m = nt(v, spread_g)[:KEYS]
                inner = jnp.sum(grad_m * mixing, axis=0, keepdims=True)
                grad_s = pad_keys(mixing * (grad_m - inner))
                scores[g] += grad_s.astype(F32)[:KEYS]
                grad_k = nn(grad_s, spread_q)
                grad_q = pick_heads(tn(grad_s, k), masks) * HEAD_DIM**-0.5
                for c, value in zip(cols, (grad_q, grad_k, grad_v)):
                    tiles[at, c] = value.astype(BF16)
        sums[...] += jnp.sum(tiles[...].astype(F32), axis=0, keepdims=True)
        put_span(triple, start, nn(select_t[image], tiles[...]).astype(BF16))
        return carry

    lax.fori_loop(0, GROUP, one_image, 0)
    me, core = ids[0], ids[1]
    members = attend_grad.shape[1]
    rows = attend_grad.shape[2] // 2
    last = pl.num_programs(0) - 1
    for part in range(4):
        at = slice(part * width, (part + 1) * width)
        grad = tn(normed[...], triple[:, at]) if part < 3 else tn(merged[...], low)

        @pl.when(pl.program_id(0) == 0)
        def _():
            total[:, at] = grad

        @pl.when(pl.program_id(0) > 0)
        def _():
            total[:, at] += grad

    @pl.when(pl.program_id(0) == last)
    def _():
        for part in range(4):
            to = slice((part % 2) * rows, (part % 2 + 1) * rows)
            for member in range(members):
                attend_grad[(part // 2) ^ core, member ^ me, to, :] = total[
                    member * rows : (member + 1) * rows, part * width : (part + 1) * width
                ].astype(BF16)


def input_back_kernel(
    ids, triple, weight, images, lines, grad_mid, place, images_grad, narrow
):
    @pl.when(pl.program_id(0) == 0)
    def _():
        narrow[...] = jnp.zeros_like(narrow)

    grad_n = nt(triple[...], weight[...])
    z, scale = norm(images[...].astype(F32))
    gain = spread_line(lines, 0, lines.shape[2] // 4, ids[0])
    back = norm_back(z, scale, gain, grad_n)
    to_grid((grad_mid[...] + back).astype(BF16), place, images_grad)
    narrow[0:1] += jnp.sum(grad_n * z, axis=0, keepdims=True)
    narrow[1:2] += jnp.sum(grad_n, axis=0, keepdims=True)


def grid_rows():
    place = np.zeros((PIECE // RES * 16, PIECE), np.float32)
    for token in range(PIECE):
        place[token // RES * 16 + token % RES, token] = 1.0
    return place


def from_grid(ref, place_t, rows):
    lines = PIECE // RES
    gap = jnp.zeros((lines, 16 - RES, rows.shape[1]), BF16)
    for i in range(rows.shape[0] // PIECE):
        padded = jnp.concatenate([ref[i * lines : (i + 1) * lines], gap], axis=1)
        padded = padded.reshape(lines * 16, rows.shape[1])
        rows[i * PIECE : (i + 1) * PIECE] = nn(place_t[...], padded).astype(BF16)


def to_grid(rows, place, ref):
    lines = PIECE // RES
    for i in range(rows.shape[0] // PIECE):
        padded = nn(place[...], rows[i * PIECE : (i + 1) * PIECE]).astype(BF16)
        ref[i * lines : (i + 1) * lines] = padded.reshape(lines, 16, rows.shape[1])[:, :RES]


def whole(array):
    return pl.BlockSpec(array.shape, lambda i, ids: (0,) * array.ndim)


def once(array):
    return pl.BlockSpec(
        array.shape, lambda i, ids: (0,) * array.ndim, pipeline_mode=pl.Buffered(1)
    )


def rows_of(count, width):
    return pl.BlockSpec((count, width), lambda i, ids: (i, 0))


def call(kernel, steps, ids, args, specs, outs, out_specs, scratch=(), flops=0):
    moved = sum(a.size * a.dtype.itemsize for a in args) + sum(
        o.size * o.dtype.itemsize for o in outs
    )
    return pl.pallas_call(
        kernel,
        grid_spec=pltpu.PrefetchScalarGridSpec(
            num_scalar_prefetch=1,
            grid=(steps,),
            in_specs=specs,
            out_specs=out_specs,
            scratch_shapes=list(scratch),
        ),
        out_shape=outs,
        compiler_params=pltpu.CompilerParams(vmem_limit_bytes=VMEM),
        cost_estimate=pl.CostEstimate(flops=flops, bytes_accessed=moved, transcendentals=0),
    )(ids, *args)


def shape(dims, kind):
    return jax.ShapeDtypeStruct(dims, kind)


def window_bias(region_labels, position_index, position_table):
    across = RES // WIN
    labels = (
        region_labels.reshape(across, WIN, across, WIN).transpose(0, 2, 1, 3).reshape(-1, WIN2)
    )
    masking = jnp.where(labels[:, :, None] == labels[:, None, :], 0.0, -100.0).astype(F32)
    index = jnp.pad(
        position_index.T, ((0, KEYS - WIN2), (0, SLOT - WIN2)), constant_values=-1
    ).reshape(-1)
    onehot = (jnp.arange(position_table.shape[0], dtype=jnp.int32)[:, None] == index[None]).astype(
        BF16
    )
    looked = dot(position_table, onehot, ((0,), (0,)))
    looked = looked.reshape(BLOCKS, 4, KEYS, SLOT).transpose(0, 2, 1, 3)
    masking = jnp.pad(masking, ((0, 0), (0, KEYS - WIN2), (0, SLOT - WIN2)))
    bias = looked[None] + masking[:, None, :, None, :]
    real = lax.broadcasted_iota(jnp.int32, bias.shape, 2) < WIN2
    bias = jnp.where(real, bias, -1e30).reshape(4, BLOCKS, KEYS, 4 * SLOT)
    return bias, onehot


def bits_of(size):
    return [1 << b for b in range(size.bit_length() - 1)]


def swap(value, axis, size, bit):
    return lax.ppermute(value, axis, [(i, i ^ bit) for i in range(size)])


def after(value, *others):
    return lax.optimization_barrier((value,) + others)[0]


def take(value, axis, side):
    return lax.index_in_dim(value, side, axis, keepdims=False)


def add_up(kept, arrived):
    total = kept.astype(F32)
    for value in arrived:
        total = total + value.astype(F32)
    return total


def stack_rows(*values):
    return jnp.concatenate([v.reshape(-1, v.shape[-1]).astype(BF16) for v in values], axis=0)


def split_rows(stacked, *like):
    out, at = [], 0
    for value in like:
        size = value.size // value.shape[-1]
        out.append(stacked[at : at + size].reshape(value.shape))
        at += size
    return out


def body(fsdp, dp, *args):
    (
        images,
        input_gain,
        input_shift,
        attend_weight,
        attend_bias,
        output_weight,
        output_bias,
        second_gain,
        second_shift,
        expand_weight,
        expand_bias,
        reduce_weight,
        reduce_bias,
        position_table,
        region_labels,
        position_index,
        cotangent,
    ) = args
    count = images.shape[0]
    width = images.shape[-1]
    rows = attend_weight.shape[0]
    hidden = expand_weight.shape[1]
    tokens = count * TOKENS
    me, dp_me = lax.axis_index("fsdp"), lax.axis_index("dp")
    ids = jnp.stack([me, dp_me % 2, (dp_me // 2) % 2]).astype(jnp.int32)
    bits = bits_of(fsdp)
    vectors = (
        input_gain,
        input_shift,
        attend_bias,
        output_bias,
        second_gain,
        second_shift,
        expand_bias,
        reduce_bias,
    )
    widest = expand_bias.shape[0]
    small = sum(
        jnp.pad(v[None], ((i, 15 - i), (0, widest - v.shape[0]))) for i, v in enumerate(vectors)
    )
    shards = (attend_weight, small, output_weight, expand_weight, reduce_weight)
    packed = (
        shape((rows + 16, 3 * width // 2), BF16),
        shape((4 * rows + rows // 2, width), BF16),
    )
    front, rest = call(
        pack_kernel,
        1,
        ids,
        shards,
        [whole(a) for a in shards],
        packed,
        [whole(a) for a in packed],
    )
    front, rest = front[None], rest[None]
    for bit in reversed(bits):
        front = jnp.concatenate([front, swap(front, "fsdp", fsdp, bit)], axis=0)
        if bit != 1:
            rest = jnp.concatenate(
                [rest, swap(after(rest, front), "fsdp", fsdp, bit)], axis=0
            )
    front_core = swap(front, "dp", dp, 1)
    lines = front[:, rows:, :widest].transpose(1, 0, 2)
    near = rest
    near_core = swap(near, "dp", dp, 1)
    far = swap(near, "fsdp", fsdp, 1)
    front = after(front, near)

    bias, onehot = window_bias(region_labels, position_index, position_table)
    order = window_order()
    select = jnp.asarray(order, BF16)
    select_t = jnp.asarray(order.transpose(0, 2, 1), BF16)
    flat_in = images.reshape(tokens, width)
    grid_cot = cotangent.reshape(tokens // RES, RES, width)
    place = jnp.asarray(grid_rows(), BF16)
    place_t = jnp.asarray(grid_rows().T, BF16)
    by_lines = pl.BlockSpec((ROWS // RES, RES, width), lambda i, ids: (i, 0, 0))

    group_rows = GROUP * TOKENS
    groups = count // GROUP
    by_group = rows_of(group_rows, width)
    win_spec = pl.BlockSpec((GROUP, 4 * SLOT, 3 * width), lambda i, ids: (i, 0, 0))
    fixed = (front, front_core, lines, bias, select, select_t)
    attend_w = shape((width, 3 * width), BF16)
    normed, windows, merged, attend_w = call(
        attend_kernel,
        groups,
        ids,
        (flat_in,) + fixed,
        [by_group] + [whole(a) for a in fixed],
        (
            shape((tokens, width), BF16),
            shape((count, 4 * SLOT, 3 * width), BF16),
            shape((tokens, width), BF16),
            attend_w,
        ),
        (by_group, win_spec, by_group, whole(attend_w)),
        (pltpu.VMEM((group_rows, 3 * width), BF16),),
        flops=12 * 10**9,
    )
    far = after(far, merged)
    far_core = swap(far, "dp", dp, 1)
    by_rows = rows_of(ROWS, width)
    tiles = tokens // ROWS
    tile_rows = pl.BlockSpec((ROWS, width), lambda i, ids: (jnp.minimum(i, tiles - 1), 0))
    tile_lines = pl.BlockSpec(
        (ROWS // RES, RES, width), lambda i, ids: (jnp.minimum(i, tiles - 1), 0, 0)
    )
    fixed = (lines, near, far, near_core, far_core, place, place_t)
    sums_out = (
        shape((8, width), F32),
        shape((1, hidden), F32),
        shape((width, width), BF16),
        shape((2, 2, fsdp, 2 * rows, width), BF16),
    )
    block_out, grad_mid, narrow_2, wide_2, out_w, feed = call(
        feed_kernel,
        tiles + hidden // width,
        ids,
        (flat_in, merged, grid_cot) + fixed,
        [tile_rows, tile_rows, tile_lines] + [once(a) for a in fixed],
        (shape(grid_cot.shape, BF16), shape((tokens, width), F32)) + sums_out,
        [tile_lines, tile_rows] + [whole(a) for a in sums_out],
        (
            pltpu.VMEM((width, hidden), BF16),
            pltpu.VMEM((hidden, width), BF16),
            pltpu.VMEM((8, hidden), F32),
            pltpu.VMEM((tiles, ROWS, width), BF16),
            pltpu.VMEM((tiles, ROWS, width), BF16),
            pltpu.VMEM((tiles, ROWS, hidden), BF16),
            pltpu.VMEM((tiles, ROWS, hidden), BF16),
        ),
        flops=27 * 10**9,
    )
    arrived = swap(feed[1], "dp", dp, 1)
    feed = add_up(feed[0], [arrived])
    sent = feed[1].astype(BF16)
    grad_mid = after(grad_mid, sent)
    feed = feed[0]
    feed_new = swap(sent, "dp", dp, 2)
    fixed = (bias, select, select_t)
    score_out = (
        shape((BLOCKS, KEYS, 4 * SLOT), F32),
        shape((1, 3 * width), F32),
        shape((2, fsdp, 2 * rows, width), BF16),
    )
    triple, scores, sums, attend = call(
        attend_back_kernel,
        groups,
        ids,
        (grad_mid, out_w, windows, normed, merged) + fixed,
        [by_group, whole(out_w), win_spec, by_group, by_group] + [whole(a) for a in fixed],
        (shape((tokens, 3 * width), BF16),) + score_out,
        [rows_of(group_rows, 3 * width)] + [whole(a) for a in score_out],
        (
            pltpu.VMEM((group_rows, width), BF16),
            pltpu.VMEM((4 * SLOT, 3 * width), BF16),
            pltpu.VMEM((width, 4 * width), F32),
        ),
        flops=19 * 10**9,
    )
    feed_new = after(feed_new, triple)
    feed = add_up(feed, [feed_new]).reshape((2,) * len(bits) + (2 * rows, width))
    first, second = len(bits) - 1, len(bits) - 2
    sent_1 = take(feed, first, 1).astype(BF16)
    feed = take(feed, first, 0)
    attend = add_up(attend[0], [swap(after(attend[1], feed_new), "dp", dp, 1)])
    attend = attend.reshape((2,) * len(bits) + attend.shape[1:])
    sent_2 = take(attend, second, 1).astype(BF16)
    attend = take(attend, second, 0)
    feed_new = swap(sent_1, "fsdp", fsdp, 1)
    attend_new = swap(sent_2, "fsdp", fsdp, 2)
    triple = after(triple, sent_1, sent_2)
    score_rows = scores.reshape(BLOCKS, KEYS, 4, SLOT).transpose(0, 2, 1, 3).reshape(HEADS, -1)
    table_grad = lax.dot_general(
        onehot.astype(F32), score_rows, (((1,), (1,)), ((), ())), precision=lax.Precision.HIGHEST
    )
    images_grad, narrow_1 = call(
        input_back_kernel,
        tokens // ROWS,
        ids,
        (triple, attend_w, flat_in, lines, grad_mid, place),
        [rows_of(ROWS, 3 * width), whole(attend_w), by_rows, whole(lines), by_rows, whole(place)],
        (shape(grid_cot.shape, BF16), sums_out[0]),
        [by_lines, whole(sums_out[0])],
        flops=3 * 10**9,
    )
    feed = add_up(feed, [after(feed_new, images_grad)])
    attend = add_up(attend, [after(attend_new, images_grad)])
    table_rows = -(-table_grad.size // width)
    table_part = jnp.pad(table_grad.reshape(-1), (0, table_rows * width - table_grad.size))
    shared = jnp.concatenate(
        [
            narrow_1[:2],
            sums.reshape(3, width),
            narrow_2[3:4],
            narrow_2[:2],
            wide_2.reshape(4, width),
            narrow_2[2:3],
            table_part.reshape(table_rows, width),
        ],
        axis=0,
    )
    shared = jnp.pad(shared, ((0, 32 - shared.shape[0]), (0, 0))).astype(BF16)

    first, second = first - 1, len(bits) - 2
    sent_1 = take(feed, first, 1)
    feed = take(feed, first, 0)
    sent_2 = take(attend, second, 1)
    attend = take(attend, second, 0)
    attend_new, shared_new = split_rows(
        swap(stack_rows(sent_2, shared), "fsdp", fsdp, 1), sent_2, shared
    )
    feed = add_up(feed, [swap(sent_1.astype(BF16), "fsdp", fsdp, 2)])
    attend = add_up(attend, [attend_new])
    shared = add_up(shared, [shared_new])
    for bit in bits[2:]:
        last = feed.ndim - 3
        sent_1, feed = take(feed, last, 1), take(feed, last, 0)
        sent_2, attend = take(attend, last, 1), take(attend, last, 0)
        feed_new, attend_new, shared_new = split_rows(
            swap(stack_rows(sent_1, sent_2, shared), "fsdp", fsdp, bit), sent_1, sent_2, shared
        )
        feed = add_up(feed, [feed_new])
        attend = add_up(attend, [attend_new])
        shared = add_up(shared, [shared_new])
    feed, attend, shared = feed.astype(BF16), attend.astype(BF16), shared.astype(BF16)
    for bit in bits_of(dp)[:0:-1]:
        feed_new, attend_new, shared_new = split_rows(
            swap(stack_rows(feed, attend, shared), "dp", dp, bit), feed, attend, shared
        )
        attend = add_up(attend, [attend_new]).astype(BF16)
        shared = add_up(shared, [shared_new]).astype(BF16)
        if bit != 2:
            feed = add_up(feed, [feed_new]).astype(BF16)
    arrived = swap(stack_rows(feed, feed_new, attend, shared), "dp", dp, 1)
    across = lax.ppermute(
        shared,
        ("dp", "fsdp"),
        [(d * fsdp + f, (d ^ 1) * fsdp + (f ^ 2)) for d in range(dp) for f in range(fsdp)],
    )
    near = swap(shared, "fsdp", fsdp, 2)
    shared = add_up(shared, [arrived[6 * rows :], near, across])
    grads = (
        shape((rows, 3 * width), F32),
        shape((rows, width), F32),
        shape((rows, hidden), F32),
        shape((4 * rows, width), F32),
    )
    operands = (attend, feed, feed_new, arrived)
    attend_grad, out_grad, exp_grad, red_grad = call(
        unpack_kernel,
        1,
        ids,
        operands,
        [whole(a) for a in operands],
        grads,
        [whole(a) for a in grads],
    )
    vector_grads = []
    at = 0
    for vector in vectors:
        size = vector.shape[0]
        count_rows = size * fsdp // width
        line = shared[at : at + count_rows].reshape(-1)
        vector_grads.append(lax.dynamic_slice_in_dim(line, me * size, size, 0))
        at += count_rows
    table_grad = shared[at : at + table_rows].reshape(-1)[: table_grad.size].reshape(
        table_grad.shape
    )
    return (
        block_out.reshape(images.shape),
        images_grad.reshape(images.shape),
        vector_grads[0],
        vector_grads[1],
        attend_grad,
        vector_grads[2],
        out_grad,
        vector_grads[3],
        vector_grads[4],
        vector_grads[5],
        exp_grad,
        vector_grads[6],
        red_grad,
        vector_grads[7],
        table_grad,
    )


def solution(mesh):
    tokens = P(("dp", "fsdp"), None, None, None)
    line, matrix = P("fsdp"), P("fsdp", None)
    weights = (line, line, matrix, line, matrix, line, line, line, matrix, line, matrix, line)
    return jax.shard_map(
        functools.partial(body, mesh.shape["fsdp"], mesh.shape["dp"]),
        mesh=mesh,
        in_specs=(tokens,) + weights + (P(), P(), P(), tokens),
        out_specs=(tokens, tokens) + weights + (P(),),
        check_vma=False,
    )
```

```python
import functools

import jax
import jax.numpy as jnp
import numpy as np
from jax import lax
from jax.experimental import pallas as pl
from jax.experimental.pallas import tpu as pltpu
from jax.sharding import PartitionSpec as P

HEADS = 16
HEAD_DIM = 32
WIN = 7
RES = 14
SHIFT = 3
WIN2 = 49
TOKENS = RES * RES
EPSILON = 1e-05
GROUP = 4
SLOT = 64
KEYS = 56
SPAN = 208
STEP = 192
BLOCKS = 4
LANES = 128
ROWS = 784
PIECE = 112
CHUNK = 1024
VMEM = 60 * 1024 * 1024
F32 = jnp.float32
BF16 = jnp.bfloat16


def window_order():
    select = np.zeros((GROUP, 4 * SLOT, SPAN), np.float32)
    for image in range(GROUP):
        for wi in range(2):
            for wj in range(2):
                for ti in range(WIN):
                    for tj in range(WIN):
                        row = (wi * 2 + wj) * SLOT + ti * WIN + tj
                        si = (wi * WIN + ti + SHIFT) % RES
                        sj = (wj * WIN + tj + SHIFT) % RES
                        select[image, row, si * RES + sj + image * (TOKENS - STEP)] = 1.0
    return select


def dot(left, right, contract):
    return lax.dot_general(left, right, (contract, ((), ())), preferred_element_type=F32)


def nn(left, right):
    return dot(left, right, ((1,), (0,)))


def nt(left, right):
    return dot(left, right, ((1,), (1,)))


def tn(left, right):
    return dot(left, right, ((0,), (0,)))


def norm(rows):
    center = rows - jnp.mean(rows, axis=-1, keepdims=True)
    spread = jnp.mean(center * center, axis=-1, keepdims=True)
    scale = lax.rsqrt(spread + EPSILON)
    return center * scale, scale


def norm_back(z, scale, gain, grad):
    g = grad * gain
    return scale * (
        g - jnp.mean(g, axis=-1, keepdims=True) - z * jnp.mean(g * z, axis=-1, keepdims=True)
    )


def head_masks():
    lane = lax.broadcasted_iota(jnp.int32, (SLOT, LANES), 1)
    return [(lane // HEAD_DIM) == j for j in range(4)]


def spread_heads(rows, masks):
    zero = jnp.zeros_like(rows)
    return jnp.concatenate([jnp.where(mask, rows, zero) for mask in masks], axis=0)


def pick_heads(wide, masks):
    total = jnp.where(masks[0], wide[:SLOT], 0.0)
    for j in range(1, 4):
        total = jnp.where(masks[j], wide[j * SLOT : (j + 1) * SLOT], total)
    return total


def pad_keys(rows):
    return jnp.concatenate([rows, jnp.zeros((SLOT - KEYS, rows.shape[1]), F32)], axis=0).astype(
        BF16
    )


def mix(keys, spread_q, bias):
    scores = nt(keys, spread_q)[:KEYS] + bias
    top = jnp.max(scores, axis=0, keepdims=True)
    raised = jnp.exp(scores - top)
    return raised * (1.0 / jnp.sum(raised, axis=0, keepdims=True))


def put_span(ref, start, value, columns=slice(None)):
    head = pl.ds(start, 16)
    tail = pl.ds(pl.multiple_of(start + 16, 16), SPAN - 16)
    ref[head, columns] = ref[head, columns] + value[:16]
    ref[tail, columns] = value[16:]


def pack_front_kernel(ids, attend, vectors, front):
    rows = attend.shape[0]
    half = attend.shape[1] // 2
    front[0, rows:, :] = jnp.zeros((16, half), BF16)
    front[0, rows:, : vectors.shape[1]] = vectors[...]
    for core in range(2):

        @pl.when(ids[1] == core)
        def _():
            front[0, :rows, :] = attend[:, core * half : (core + 1) * half]


def pack_rest_kernel(ids, output, expand, reduce, rest):
    rows, width = output.shape
    for core in range(2):

        @pl.when(ids[1] == core)
        def _():
            if core == 0:
                for i in range(4):
                    rest[0, i * rows : (i + 1) * rows] = expand[:, i * width : (i + 1) * width]
            else:
                rest[0, : 4 * rows] = reduce[...]
            rest[0, 4 * rows :] = output[core * (rows // 2) : (core + 1) * (rows // 2)]


def spread_line(lines, index, size, me):
    members = lines.shape[1]
    bits = members.bit_length() - 1
    piece = lines[index][:, :size]
    column = lax.broadcasted_iota(jnp.int32, (size, members * size), 1)
    inside = lax.broadcasted_iota(jnp.int32, (size, members * size), 0)
    wide = nn(piece, (column % size == inside).astype(BF16))
    place = lax.broadcasted_iota(jnp.int32, wide.shape, 0)
    flipped = sum(((place >> b) & 1) << (bits - 1 - b) for b in range(bits))
    owner = lax.broadcasted_iota(jnp.int32, wide.shape, 1) // size
    return jnp.sum(jnp.where(owner == (flipped ^ me), wide, 0.0), axis=0, keepdims=True)


def flip(place, bits):
    return sum(((place >> b) & 1) << (bits - 1 - b) for b in range(bits))


def attend_kernel(
    ids, images, mine, other, lines, bias, select, select_t, normed, windows, merged, weight, flat
):
    width = images.shape[1]
    me, core = ids[0], ids[1]
    members = mine.shape[0]
    rows = width // members

    @pl.when(pl.program_id(0) == 0)
    def _():
        half = mine.shape[2]
        for own in range(2):

            @pl.when(core == own)
            def _():
                for side, part in ((own, mine), (1 - own, other)):
                    for place in range(members):
                        member = flip(place, members.bit_length() - 1) ^ me
                        at = pl.ds(pl.multiple_of(member * rows, rows), rows)
                        weight[at, side * half : (side + 1) * half] = part[place, :rows, :]

    z, _ = norm(images[...].astype(F32))
    gain = spread_line(lines, 0, rows, me)
    shift = spread_line(lines, 1, rows, me)
    attend_bias = spread_line(lines, 2, 3 * rows, me)
    low = (z * gain + shift).astype(BF16)
    normed[...] = low
    for part in range(3):
        cols = slice(part * width, (part + 1) * width)
        value = nn(low, weight[:, cols]) + attend_bias[:, cols]
        if part == 0:
            value = value * HEAD_DIM**-0.5
        flat[:, cols] = value.astype(BF16)
    merged[:16, :] = jnp.zeros((16, width), BF16)

    def one_image(image, carry):
        start = pl.multiple_of(image * STEP, 16)
        span = flat[pl.ds(start, SPAN), :]
        chosen = select[image]
        windows[image] = nn(chosen, span).astype(BF16)
        masks = head_masks()
        rows = []
        for w in range(4):
            at = slice(w * SLOT, (w + 1) * SLOT)
            parts = []
            for g in range(BLOCKS):
                q, k, v = (
                    windows[image, at, part * width + g * LANES : part * width + (g + 1) * LANES]
                    for part in range(3)
                )
                mixing = mix(k, spread_heads(q, masks), bias[w, g])
                parts.append(pick_heads(tn(pad_keys(mixing), v), masks).astype(BF16))
            rows.append(jnp.concatenate(parts, axis=1))
        context = jnp.concatenate(rows, axis=0)
        put_span(merged, start, nn(select_t[image], context).astype(BF16))
        return carry

    lax.fori_loop(0, GROUP, one_image, 0, unroll=2)


def gelu_parts(t):
    k = 1.0 / (1.0 + (0.3275911 * 0.5**0.5) * jnp.abs(t))
    bell = jnp.exp(-0.5 * (t * t))
    poly = 0.5 * 1.061405429 * k - 0.5 * 1.453152027
    poly = poly * k + 0.5 * 1.421413741
    poly = poly * k - 0.5 * 0.284496736
    poly = poly * k + 0.5 * 0.254829592
    tail = poly * k * bell
    below = jnp.where(t >= 0, 1.0 - tail, tail)
    return t * below, below + t * (bell * 0.3989422804014327)


def sum_tiles(left, right, columns, side):
    total = None
    for tile in range(left.shape[0]):
        cols = [slice(None), slice(None)]
        cols[side] = columns
        part = tn(left[tile, :, cols[0]], right[tile, :, cols[1]])
        total = part if total is None else total + part
    return total.astype(BF16)


def put_feed_grad(ids, step, act, grad_hid, cot, normed_two, kept, sent):
    me, core, second = ids[0], ids[1], ids[2]
    members, half = kept.shape[1], kept.shape[2]
    rows = half // 2
    width = cot.shape[2]
    columns = pl.ds(pl.multiple_of(step * width, width), width)
    grad_reduce = sum_tiles(act, cot, columns, 0)
    grad_expand = sum_tiles(normed_two, grad_hid, columns, 1)
    count = width // (2 * half)
    to = pl.ds(pl.multiple_of((step % 2) * rows, rows), rows)
    for own in range(2):

        @pl.when(core == own)
        def _():
            reduce_out, expand_out = (kept, sent) if own == 0 else (sent, kept)
            for i in range(count):
                for h in range(2):
                    at = (2 * i + h) * half
                    reduce_out[h ^ second, (step * count + i) ^ me] = grad_reduce[at : at + half]
            for member in range(members):
                expand_out[(step // 2) ^ second, member ^ me, to, :] = grad_expand[
                    member * rows : (member + 1) * rows
                ]


def feed_kernel(
    ids,
    images,
    merged,
    cot,
    lines,
    near,
    far,
    near_core,
    far_core,
    place,
    place_t,
    block_out,
    grad_mid,
    narrow,
    wide,
    out_w,
    feed_kept,
    feed_sent,
    exp_w,
    red_w,
    vectors,
    cot_all,
    normed_all,
    act_all,
    grad_all,
):
    me, core = ids[0], ids[1]
    step = pl.program_id(0)
    tiles = act_all.shape[0]
    width = images.shape[1]
    held = near.shape[0]
    rows = width // (2 * held)

    @pl.when(pl.program_id(0) == 0)
    def _():
        narrow[...] = jnp.zeros_like(narrow)
        wide[...] = jnp.zeros_like(wide)
        for i, index in enumerate((3, 4, 5, 7)):
            vectors[i : i + 1, :width] = spread_line(lines, index, rows, me)
        vectors[4:5, :] = spread_line(lines, 6, 4 * rows, me)
        for own in range(2):

            @pl.when(core == own)
            def _():
                for side, parts in ((own, (near, far)), (1 - own, (near_core, far_core))):
                    for odd, part in enumerate(parts):
                        for at in range(held):
                            member = ((flip(at, held.bit_length() - 1) << 1) | odd) ^ me
                            if side == 0:
                                to = pl.ds(pl.multiple_of(member * rows, rows), rows)
                                for i in range(4):
                                    exp_w[to, i * width : (i + 1) * width] = part[
                                        at, i * rows : (i + 1) * rows, :
                                    ]
                            else:
                                to = pl.ds(pl.multiple_of(member * 4 * rows, 4 * rows), 4 * rows)
                                red_w[to, :] = part[at, : 4 * rows, :]
                            half = rows // 2
                            to = pl.ds(pl.multiple_of(member * rows + side * half, half), half)
                            out_w[to, :] = part[at, 4 * rows :, :]

    @pl.when(step < tiles)
    def _():
        middle = images[...].astype(F32) + nn(merged[...], out_w[...]) + vectors[0:1, :width]
        z, scale = norm(middle)
        scaled = vectors[1:2, :width]
        low = (z * scaled + vectors[2:3, :width]).astype(BF16)
        normed_all[step] = low
        from_grid(cot, place_t, cot_all.at[step])
        grad = cot_all[step]
        result = middle + vectors[3:4, :width]
        grad_y = jnp.zeros_like(middle)
        for c in range(exp_w.shape[1] // CHUNK):
            at = slice(c * CHUNK, (c + 1) * CHUNK)
            hidden = nn(low, exp_w[:, at]) + vectors[4:5, at]
            grad_act = nt(grad, red_w[at, :])
            active, slope = gelu_parts(hidden)
            active = active.astype(BF16)
            act_all[step, :, at] = active
            grad_h = (grad_act * slope).astype(BF16)
            grad_all[step, :, at] = grad_h
            wide[:, at] += jnp.sum(grad_h.astype(F32), axis=0, keepdims=True)
            result = result + nn(active, red_w[at, :])
            grad_y = grad_y + nt(grad_h, exp_w[:, at])
        to_grid(result.astype(BF16), place, block_out)
        wide_cot = grad.astype(F32)
        grad_middle = wide_cot + norm_back(z, scale, scaled, grad_y)
        grad_mid[...] = grad_middle
        narrow[0:1] += jnp.sum(grad_y * z, axis=0, keepdims=True)
        narrow[1:2] += jnp.sum(grad_y, axis=0, keepdims=True)
        narrow[2:3] += jnp.sum(wide_cot, axis=0, keepdims=True)
        narrow[3:4] += jnp.sum(grad_middle.astype(BF16).astype(F32), axis=0, keepdims=True)

    @pl.when(step >= tiles)
    def _():
        put_feed_grad(
            ids, step - tiles, act_all, grad_all, cot_all, normed_all, feed_kept, feed_sent
        )


def unpack_kernel(ids, attend, feed_0, feed_1, arrived, attend_w, out_w, exp_w, red_w):
    core, second = ids[1], ids[2]
    size = attend.shape[0]
    rows = size // 2
    width = attend.shape[1]

    def place(side, attend_part, feeds):
        if side == 0:
            attend_w[:, :width] = attend_part[:rows].astype(F32)
            attend_w[:, width : 2 * width] = attend_part[rows:].astype(F32)
        else:
            attend_w[:, 2 * width :] = attend_part[:rows].astype(F32)
            out_w[...] = attend_part[rows:].astype(F32)
        for h, part in enumerate(feeds):
            if side == 0:
                red_w[h * size : (h + 1) * size] = part.astype(F32)
            else:
                at = 2 * h * width
                exp_w[:, at : at + width] = part[:rows].astype(F32)
                exp_w[:, at + width : at + 2 * width] = part[rows:].astype(F32)

    for own in range(2):
        for y in range(2):

            @pl.when((core == own) & (second == y))
            def _():
                place(own, attend[...], (feed_0[...], feed_1[...])[:: 1 - 2 * y])
                parts = [arrived[i * size : (i + 1) * size, :] for i in range(3)]
                place(1 - own, parts[2], parts[:2][:: 1 - 2 * y])


def attend_back_kernel(
    ids,
    grad_mid,
    out_w,
    windows,
    normed,
    merged,
    bias,
    select,
    select_t,
    triple,
    scores,
    sums,
    attend_kept,
    attend_sent,
    flat,
    tiles,
    total,
):
    width = grad_mid.shape[1]

    @pl.when(pl.program_id(0) == 0)
    def _():
        scores[...] = jnp.zeros_like(scores)
        sums[...] = jnp.zeros_like(sums)

    low = grad_mid[...].astype(BF16)
    flat[...] = nt(low, out_w[...]).astype(BF16)
    triple[:16, :] = jnp.zeros((16, 3 * width), BF16)

    def one_image(image, carry):
        start = pl.multiple_of(image * STEP, 16)
        context = nn(select[image], flat[pl.ds(start, SPAN), :]).astype(BF16)
        masks = head_masks()
        for w in range(4):
            at = slice(w * SLOT, (w + 1) * SLOT)
            for g in range(BLOCKS):
                cols = [
                    slice(part * width + g * LANES, part * width + (g + 1) * LANES)
                    for part in range(3)
                ]
                q, k, v = (windows[image, at, c] for c in cols)
                grad_c = context[at, g * LANES : (g + 1) * LANES]
                spread_q = spread_heads(q, masks)
                spread_g = spread_heads(grad_c, masks)
                mixing = mix(k, spread_q, bias[w, g])
                grad_v = nn(pad_keys(mixing), spread_g)
                grad_m = nt(v, spread_g)[:KEYS]
                inner = jnp.sum(grad_m * mixing, axis=0, keepdims=True)
                grad_s = pad_keys(mixing * (grad_m - inner))
                scores[g] += grad_s.astype(F32)[:KEYS]
                grad_k = nn(grad_s, spread_q)
                grad_q = pick_heads(tn(grad_s, k), masks) * HEAD_DIM**-0.5
                for c, value in zip(cols, (grad_q, grad_k, grad_v)):
                    tiles[at, c] = value.astype(BF16)
        sums[...] += jnp.sum(tiles[...].astype(F32), axis=0, keepdims=True)
        put_span(triple, start, nn(select_t[image], tiles[...]).astype(BF16))
        return carry

    lax.fori_loop(0, GROUP, one_image, 0, unroll=2)
    me, core = ids[0], ids[1]
    members = attend_kept.shape[0]
    rows = attend_kept.shape[1] // 2
    last = pl.num_programs(0) - 1
    for part in range(4):
        at = slice(part * width, (part + 1) * width)
        grad = tn(normed[...], triple[:, at]) if part < 3 else tn(merged[...], low)

        @pl.when(pl.program_id(0) == 0)
        def _():
            total[:, at] = grad

        @pl.when(pl.program_id(0) > 0)
        def _():
            total[:, at] += grad

    for own in range(2):

        @pl.when((pl.program_id(0) == last) & (core == own))
        def _():
            for part in range(4):
                to = slice((part % 2) * rows, (part % 2 + 1) * rows)
                out = attend_kept if part // 2 == own else attend_sent
                for member in range(members):
                    out[member ^ me, to, :] = total[
                        member * rows : (member + 1) * rows, part * width : (part + 1) * width
                    ].astype(BF16)


def input_back_kernel(
    ids, triple, weight, images, lines, grad_mid, place, images_grad, narrow
):
    @pl.when(pl.program_id(0) == 0)
    def _():
        narrow[...] = jnp.zeros_like(narrow)

    grad_n = nt(triple[...], weight[...])
    z, scale = norm(images[...].astype(F32))
    gain = spread_line(lines, 0, lines.shape[2] // 4, ids[0])
    back = norm_back(z, scale, gain, grad_n)
    to_grid((grad_mid[...] + back).astype(BF16), place, images_grad)
    narrow[0:1] += jnp.sum(grad_n * z, axis=0, keepdims=True)
    narrow[1:2] += jnp.sum(grad_n, axis=0, keepdims=True)


def grid_rows():
    place = np.zeros((PIECE // RES * 16, PIECE), np.float32)
    for token in range(PIECE):
        place[token // RES * 16 + token % RES, token] = 1.0
    return place


def from_grid(ref, place_t, rows):
    lines = PIECE // RES
    gap = jnp.zeros((lines, 16 - RES, rows.shape[1]), BF16)
    for i in range(rows.shape[0] // PIECE):
        padded = jnp.concatenate([ref[i * lines : (i + 1) * lines], gap], axis=1)
        padded = padded.reshape(lines * 16, rows.shape[1])
        rows[i * PIECE : (i + 1) * PIECE] = nn(place_t[...], padded).astype(BF16)


def to_grid(rows, place, ref):
    lines = PIECE // RES
    for i in range(rows.shape[0] // PIECE):
        padded = nn(place[...], rows[i * PIECE : (i + 1) * PIECE]).astype(BF16)
        ref[i * lines : (i + 1) * lines] = padded.reshape(lines, 16, rows.shape[1])[:, :RES]


def whole(array):
    return pl.BlockSpec(array.shape, lambda i, ids: (0,) * array.ndim)


def once(array):
    return pl.BlockSpec(
        array.shape, lambda i, ids: (0,) * array.ndim, pipeline_mode=pl.Buffered(1)
    )


def rows_of(count, width):
    return pl.BlockSpec((count, width), lambda i, ids: (i, 0))


def call(kernel, steps, ids, args, specs, outs, out_specs, scratch=(), flops=0):
    moved = sum(a.size * a.dtype.itemsize for a in args) + sum(
        o.size * o.dtype.itemsize for o in outs
    )
    return pl.pallas_call(
        kernel,
        grid_spec=pltpu.PrefetchScalarGridSpec(
            num_scalar_prefetch=1,
            grid=(steps,),
            in_specs=specs,
            out_specs=out_specs,
            scratch_shapes=list(scratch),
        ),
        out_shape=outs,
        compiler_params=pltpu.CompilerParams(vmem_limit_bytes=VMEM),
        cost_estimate=pl.CostEstimate(flops=flops, bytes_accessed=moved, transcendentals=0),
    )(ids, *args)


def pack(kernel, ids, args, outs):
    return call(kernel, 1, ids, args, [whole(a) for a in args], outs, [whole(a) for a in outs])


def shape(dims, kind):
    return jax.ShapeDtypeStruct(dims, kind)


def window_bias(region_labels, position_index, position_table):
    across = RES // WIN
    labels = (
        region_labels.reshape(across, WIN, across, WIN).transpose(0, 2, 1, 3).reshape(-1, WIN2)
    )
    masking = jnp.where(labels[:, :, None] == labels[:, None, :], 0.0, -100.0).astype(F32)
    index = jnp.pad(
        position_index.T, ((0, KEYS - WIN2), (0, SLOT - WIN2)), constant_values=-1
    ).reshape(-1)
    onehot = (jnp.arange(position_table.shape[0], dtype=jnp.int32)[:, None] == index[None]).astype(
        BF16
    )
    looked = dot(position_table, onehot, ((0,), (0,)))
    looked = looked.reshape(BLOCKS, 4, KEYS, SLOT).transpose(0, 2, 1, 3)
    masking = jnp.pad(masking, ((0, 0), (0, KEYS - WIN2), (0, SLOT - WIN2)))
    bias = looked[None] + masking[:, None, :, None, :]
    real = lax.broadcasted_iota(jnp.int32, bias.shape, 2) < WIN2
    bias = jnp.where(real, bias, -1e30).reshape(4, BLOCKS, KEYS, 4 * SLOT)
    return bias, onehot


def bits_of(size):
    return [1 << b for b in range(size.bit_length() - 1)]


def swap(value, axis, size, bit):
    return lax.ppermute(value, axis, [(i, i ^ bit) for i in range(size)])


def after(value, *others):
    return lax.optimization_barrier((value,) + others)[0]


def take(value, axis, side):
    return lax.index_in_dim(value, side, axis, keepdims=False)


def add_up(kept, arrived):
    total = kept.astype(F32)
    for value in arrived:
        total = total + value.astype(F32)
    return total.astype(BF16)


def stack_rows(*values):
    return jnp.concatenate([v.reshape(-1, v.shape[-1]).astype(BF16) for v in values], axis=0)


def split_rows(stacked, *like):
    out, at = [], 0
    for value in like:
        size = value.size // value.shape[-1]
        out.append(stacked[at : at + size].reshape(value.shape))
        at += size
    return out


def body(fsdp, dp, *args):
    (
        images,
        input_gain,
        input_shift,
        attend_weight,
        attend_bias,
        output_weight,
        output_bias,
        second_gain,
        second_shift,
        expand_weight,
        expand_bias,
        reduce_weight,
        reduce_bias,
        position_table,
        region_labels,
        position_index,
        cotangent,
    ) = args
    count = images.shape[0]
    width = images.shape[-1]
    rows = attend_weight.shape[0]
    hidden = expand_weight.shape[1]
    tokens = count * TOKENS
    me, dp_me = lax.axis_index("fsdp"), lax.axis_index("dp")
    linear = dp_me * fsdp + me
    ids = (linear // np.array([1, fsdp, 2 * fsdp], np.int32)) % np.array([fsdp, 2, 2], np.int32)
    bits = bits_of(fsdp)
    vectors = (
        input_gain,
        input_shift,
        attend_bias,
        output_bias,
        second_gain,
        second_shift,
        expand_bias,
        reduce_bias,
    )
    widest = expand_bias.shape[0]
    small = sum(
        jnp.pad(v[None], ((i, 15 - i), (0, widest - v.shape[0]))) for i, v in enumerate(vectors)
    )
    front = pack(
        pack_front_kernel,
        ids,
        (attend_weight, small),
        (shape((1, rows + 16, 3 * width // 2), BF16),),
    )[0]
    rest = pack(
        pack_rest_kernel,
        ids,
        (output_weight, expand_weight, reduce_weight),
        (shape((1, 4 * rows + rows // 2, width), BF16),),
    )[0]
    rest_stages = []
    for bit in reversed(bits):
        if len(rest_stages) > 1:
            front = after(front, rest_stages[-2])
        front = jnp.concatenate([front, swap(front, "fsdp", fsdp, bit)], axis=0)
        if bit != 1:
            rest = jnp.concatenate([rest, swap(rest, "fsdp", fsdp, bit)], axis=0)
            rest_stages.append(rest)
    front = after(front, rest)
    front_core = swap(front, "dp", dp, 1)
    lines = front[:, rows:, :widest].transpose(1, 0, 2)
    near = rest
    near_core = swap(near, "dp", dp, 1)
    far = swap(near, "fsdp", fsdp, 1)

    bias, onehot = window_bias(region_labels, position_index, position_table)
    order = window_order()
    select = jnp.asarray(order, BF16)
    select_t = jnp.asarray(order.transpose(0, 2, 1), BF16)
    flat_in = images.reshape(tokens, width)
    grid_cot = cotangent.reshape(tokens // RES, RES, width)
    place = jnp.asarray(grid_rows(), BF16)
    place_t = jnp.asarray(grid_rows().T, BF16)
    by_lines = pl.BlockSpec((ROWS // RES, RES, width), lambda i, ids: (i, 0, 0))

    group_rows = GROUP * TOKENS
    groups = count // GROUP
    by_group = rows_of(group_rows, width)
    win_spec = pl.BlockSpec((GROUP, 4 * SLOT, 3 * width), lambda i, ids: (i, 0, 0))
    fixed = (front, front_core, lines, bias, select, select_t)
    attend_w = shape((width, 3 * width), BF16)
    normed, windows, merged, attend_w = call(
        attend_kernel,
        groups,
        ids,
        (flat_in,) + fixed,
        [by_group] + [whole(a) for a in fixed],
        (
            shape((tokens, width), BF16),
            shape((count, 4 * SLOT, 3 * width), BF16),
            shape((tokens, width), BF16),
            attend_w,
        ),
        (by_group, win_spec, by_group, whole(attend_w)),
        (pltpu.VMEM((group_rows, 3 * width), BF16),),
        flops=12 * 10**9,
    )
    far = after(far, merged)
    far_core = swap(far, "dp", dp, 1)
    by_rows = rows_of(ROWS, width)
    tiles = tokens // ROWS
    tile_rows = pl.BlockSpec((ROWS, width), lambda i, ids: (jnp.minimum(i, tiles - 1), 0))
    tile_lines = pl.BlockSpec(
        (ROWS // RES, RES, width), lambda i, ids: (jnp.minimum(i, tiles - 1), 0, 0)
    )
    fixed = (lines, near, far, near_core, far_core, place, place_t)
    sums_out = (
        shape((8, width), F32),
        shape((1, hidden), F32),
        shape((width, width), BF16),
        shape((2, fsdp, 2 * rows, width), BF16),
        shape((2, fsdp, 2 * rows, width), BF16),
    )
    block_out, grad_mid, narrow_2, wide_2, out_w, feed, feed_sent = call(
        feed_kernel,
        tiles + hidden // width,
        ids,
        (flat_in, merged, grid_cot) + fixed,
        [tile_rows, tile_rows, tile_lines] + [once(a) for a in fixed],
        (shape(grid_cot.shape, BF16), shape((tokens, width), F32)) + sums_out,
        [tile_lines, tile_rows] + [whole(a) for a in sums_out],
        (
            pltpu.VMEM((width, hidden), BF16),
            pltpu.VMEM((hidden, width), BF16),
            pltpu.VMEM((8, hidden), F32),
            pltpu.VMEM((tiles, ROWS, width), BF16),
            pltpu.VMEM((tiles, ROWS, width), BF16),
            pltpu.VMEM((tiles, ROWS, hidden), BF16),
            pltpu.VMEM((tiles, ROWS, hidden), BF16),
        ),
        flops=27 * 10**9,
    )
    feed = add_up(feed, [swap(feed_sent, "dp", dp, 1)])
    sent = feed[1]
    grad_mid = after(grad_mid, sent)
    feed = feed[0]
    feed_new = swap(sent, "dp", dp, 2)
    fixed = (bias, select, select_t)
    score_out = (
        shape((BLOCKS, KEYS, 4 * SLOT), F32),
        shape((1, 3 * width), F32),
        shape((fsdp, 2 * rows, width), BF16),
        shape((fsdp, 2 * rows, width), BF16),
    )
    triple, scores, sums, attend, attend_sent = call(
        attend_back_kernel,
        groups,
        ids,
        (grad_mid, out_w, windows, normed, merged) + fixed,
        [by_group, whole(out_w), win_spec, by_group, by_group] + [whole(a) for a in fixed],
        (shape((tokens, 3 * width), BF16),) + score_out,
        [rows_of(group_rows, 3 * width)] + [whole(a) for a in score_out],
        (
            pltpu.VMEM((group_rows, width), BF16),
            pltpu.VMEM((4 * SLOT, 3 * width), BF16),
            pltpu.VMEM((width, 4 * width), F32),
        ),
        flops=19 * 10**9,
    )
    feed_new = after(feed_new, triple)
    feed = add_up(feed, [feed_new]).reshape((2,) * len(bits) + (2 * rows, width))
    first, second = len(bits) - 1, len(bits) - 2
    sent_1 = take(feed, first, 1).astype(BF16)
    feed = take(feed, first, 0)
    attend = add_up(attend, [swap(after(attend_sent, feed_new), "dp", dp, 1)])
    attend = attend.reshape((2,) * len(bits) + attend.shape[1:])
    sent_2 = take(attend, second, 1).astype(BF16)
    attend = take(attend, second, 0)
    feed_new = swap(sent_1, "fsdp", fsdp, 1)
    attend_new = swap(sent_2, "fsdp", fsdp, 2)
    triple = after(triple, sent_1, sent_2)
    score_rows = scores.reshape(BLOCKS, KEYS, 4, SLOT).transpose(0, 2, 1, 3).reshape(HEADS, -1)
    table_grad = lax.dot_general(
        onehot.astype(F32), score_rows, (((1,), (1,)), ((), ())), precision=lax.Precision.HIGHEST
    )
    images_grad, narrow_1 = call(
        input_back_kernel,
        tokens // ROWS,
        ids,
        (triple, attend_w, flat_in, lines, grad_mid, place),
        [rows_of(ROWS, 3 * width), whole(attend_w), by_rows, whole(lines), by_rows, whole(place)],
        (shape(grid_cot.shape, BF16), sums_out[0]),
        [by_lines, whole(sums_out[0])],
        flops=3 * 10**9,
    )
    feed = add_up(feed, [after(feed_new, images_grad)])
    attend = add_up(attend, [after(attend_new, images_grad)])
    table_rows = -(-table_grad.size // width)
    table_part = jnp.pad(table_grad.reshape(-1), (0, table_rows * width - table_grad.size))
    shared = jnp.concatenate(
        [
            narrow_1[:2],
            sums.reshape(3, width),
            narrow_2[3:4],
            narrow_2[:2],
            wide_2.reshape(4, width),
            narrow_2[2:3],
            table_part.reshape(table_rows, width),
        ],
        axis=0,
    )
    shared = jnp.pad(shared, ((0, 32 - shared.shape[0]), (0, 0))).astype(BF16)

    first, second = first - 1, len(bits) - 2
    sent_1 = take(feed, first, 1)
    feed = take(feed, first, 0)
    sent_2 = take(attend, second, 1)
    attend = take(attend, second, 0)
    attend_new, shared_new = split_rows(
        swap(stack_rows(sent_2, shared), "fsdp", fsdp, 1), sent_2, shared
    )
    feed = add_up(feed, [swap(sent_1.astype(BF16), "fsdp", fsdp, 2)])
    attend = add_up(attend, [attend_new])
    shared = add_up(shared, [shared_new])
    for bit in bits[2:]:
        last = feed.ndim - 3
        sent_1, feed = take(feed, last, 1), take(feed, last, 0)
        sent_2, attend = take(attend, last, 1), take(attend, last, 0)
        feed_new, attend_new, shared_new = split_rows(
            swap(stack_rows(sent_1, sent_2, shared), "fsdp", fsdp, bit), sent_1, sent_2, shared
        )
        feed = add_up(feed, [feed_new])
        attend = add_up(attend, [attend_new])
        shared = add_up(shared, [shared_new])
    feed, attend, shared = feed.astype(BF16), attend.astype(BF16), shared.astype(BF16)
    for bit in bits_of(dp)[:0:-1]:
        feed_new, attend_new, shared_new = split_rows(
            swap(stack_rows(feed, attend, shared), "dp", dp, bit), feed, attend, shared
        )
        attend = add_up(attend, [attend_new]).astype(BF16)
        shared = add_up(shared, [shared_new]).astype(BF16)
        if bit != 2:
            feed = add_up(feed, [feed_new]).astype(BF16)
    arrived = swap(stack_rows(feed, feed_new, attend, shared), "dp", dp, 1)
    across = lax.ppermute(
        shared,
        ("dp", "fsdp"),
        [(d * fsdp + f, (d ^ 1) * fsdp + (f ^ 2)) for d in range(dp) for f in range(fsdp)],
    )
    near = swap(shared, "fsdp", fsdp, 2)
    shared = sum(v.astype(F32) for v in (shared, arrived[6 * rows :], near, across))
    grads = (
        shape((rows, 3 * width), F32),
        shape((rows, width), F32),
        shape((rows, hidden), F32),
        shape((4 * rows, width), F32),
    )
    operands = (attend, feed, feed_new, arrived)
    attend_grad, out_grad, exp_grad, red_grad = pack(unpack_kernel, ids, operands, grads)
    vector_grads = []
    at = 0
    for vector in vectors:
        size = vector.shape[0]
        count_rows = size * fsdp // width
        line = shared[at : at + count_rows].reshape(-1)
        vector_grads.append(lax.dynamic_slice_in_dim(line, me * size, size, 0))
        at += count_rows
    table_grad = shared[at : at + table_rows].reshape(-1)[: table_grad.size].reshape(
        table_grad.shape
    )
    return (
        block_out.reshape(images.shape),
        images_grad.reshape(images.shape),
        vector_grads[0],
        vector_grads[1],
        attend_grad,
        vector_grads[2],
        out_grad,
        vector_grads[3],
        vector_grads[4],
        vector_grads[5],
        exp_grad,
        vector_grads[6],
        red_grad,
        vector_grads[7],
        table_grad,
    )


def solution(mesh):
    tokens = P(("dp", "fsdp"), None, None, None)
    line, matrix = P("fsdp"), P("fsdp", None)
    weights = (line, line, matrix, line, matrix, line, line, line, matrix, line, matrix, line)
    return jax.shard_map(
        functools.partial(body, mesh.shape["fsdp"], mesh.shape["dp"]),
        mesh=mesh,
        in_specs=(tokens,) + weights + (P(), P(), P(), tokens),
        out_specs=(tokens, tokens) + weights + (P(),),
        check_vma=False,
    )
```

```python
import functools

import jax
import jax.numpy as jnp
import numpy as np
from jax import lax
from jax.experimental import pallas as pl
from jax.experimental.pallas import tpu as pltpu
from jax.sharding import PartitionSpec as P

HEADS = 16
HEAD_DIM = 32
WIN = 7
RES = 14
SHIFT = 3
WIN2 = 49
TOKENS = RES * RES
EPSILON = 1e-05
GROUP = 4
SLOT = 64
KEYS = 56
SPAN = 208
STEP = 192
BLOCKS = 4
LANES = 128
ROWS = 784
PIECE = 112
CHUNK = 1024
VMEM = 60 * 1024 * 1024
F32 = jnp.float32
BF16 = jnp.bfloat16


def window_order():
    select = np.zeros((GROUP, 4 * SLOT, SPAN), np.float32)
    for image in range(GROUP):
        for wi in range(2):
            for wj in range(2):
                for ti in range(WIN):
                    for tj in range(WIN):
                        row = (wi * 2 + wj) * SLOT + ti * WIN + tj
                        si = (wi * WIN + ti + SHIFT) % RES
                        sj = (wj * WIN + tj + SHIFT) % RES
                        select[image, row, si * RES + sj + image * (TOKENS - STEP)] = 1.0
    return select


def dot(left, right, contract):
    return lax.dot_general(left, right, (contract, ((), ())), preferred_element_type=F32)


def nn(left, right):
    return dot(left, right, ((1,), (0,)))


def nt(left, right):
    return dot(left, right, ((1,), (1,)))


def tn(left, right):
    return dot(left, right, ((0,), (0,)))


def norm(rows):
    center = rows - jnp.mean(rows, axis=-1, keepdims=True)
    spread = jnp.mean(center * center, axis=-1, keepdims=True)
    scale = lax.rsqrt(spread + EPSILON)
    return center * scale, scale


def norm_back(z, scale, gain, grad):
    g = grad * gain
    return scale * (
        g - jnp.mean(g, axis=-1, keepdims=True) - z * jnp.mean(g * z, axis=-1, keepdims=True)
    )


def head_masks():
    lane = lax.broadcasted_iota(jnp.int32, (SLOT, LANES), 1)
    return [(lane // HEAD_DIM) == j for j in range(4)]


def spread_heads(rows, masks):
    zero = jnp.zeros_like(rows)
    return jnp.concatenate([jnp.where(mask, rows, zero) for mask in masks], axis=0)


def pick_heads(wide, masks):
    total = jnp.where(masks[0], wide[:SLOT], 0.0)
    for j in range(1, 4):
        total = jnp.where(masks[j], wide[j * SLOT : (j + 1) * SLOT], total)
    return total


def pad_keys(rows):
    return jnp.concatenate([rows, jnp.zeros((SLOT - KEYS, rows.shape[1]), F32)], axis=0).astype(
        BF16
    )


def mix(keys, spread_q, bias):
    scores = nt(keys, spread_q)[:KEYS] + bias
    top = jnp.max(scores, axis=0, keepdims=True)
    raised = jnp.exp(scores - top)
    return raised * (1.0 / jnp.sum(raised, axis=0, keepdims=True))


def put_span(ref, start, value, columns=slice(None)):
    head = pl.ds(start, 16)
    tail = pl.ds(pl.multiple_of(start + 16, 16), SPAN - 16)
    ref[head, columns] = ref[head, columns] + value[:16]
    ref[tail, columns] = value[16:]


def pack_front_kernel(ids, attend, vectors, front):
    rows = attend.shape[0]
    half = attend.shape[1] // 2
    front[rows:, :] = jnp.zeros((16, half), BF16)
    front[rows:, : vectors.shape[1]] = vectors[...]
    for core in range(2):

        @pl.when(ids[1] == core)
        def _():
            front[:rows, :] = attend[:, core * half : (core + 1) * half]


def pack_rest_kernel(ids, output, expand, reduce, rest):
    rows, width = output.shape
    for core in range(2):

        @pl.when(ids[1] == core)
        def _():
            if core == 0:
                for i in range(4):
                    rest[i * rows : (i + 1) * rows] = expand[:, i * width : (i + 1) * width]
            else:
                rest[: 4 * rows] = reduce[...]
            rest[4 * rows :] = output[core * (rows // 2) : (core + 1) * (rows // 2)]


def spread_line(lines, index, size, me):
    members = lines.shape[1]
    bits = members.bit_length() - 1
    piece = lines[index][:, :size]
    column = lax.broadcasted_iota(jnp.int32, (size, members * size), 1)
    inside = lax.broadcasted_iota(jnp.int32, (size, members * size), 0)
    wide = nn(piece, (column % size == inside).astype(BF16))
    place = lax.broadcasted_iota(jnp.int32, wide.shape, 0)
    flipped = sum(((place >> b) & 1) << (bits - 1 - b) for b in range(bits))
    owner = lax.broadcasted_iota(jnp.int32, wide.shape, 1) // size
    return jnp.sum(jnp.where(owner == (flipped ^ me), wide, 0.0), axis=0, keepdims=True)


def flip(place, bits):
    return sum(((place >> b) & 1) << (bits - 1 - b) for b in range(bits))


def attend_kernel(
    ids, images, mine, other, lines, bias, select, select_t, normed, windows, merged, weight, flat
):
    width = images.shape[1]
    me, core = ids[0], ids[1]
    members = mine.shape[0]
    rows = width // members

    @pl.when(pl.program_id(0) == 0)
    def _():
        half = mine.shape[2]
        for own in range(2):

            @pl.when(core == own)
            def _():
                for side, part in ((own, mine), (1 - own, other)):
                    for place in range(members):
                        member = flip(place, members.bit_length() - 1) ^ me
                        at = pl.ds(pl.multiple_of(member * rows, rows), rows)
                        weight[at, side * half : (side + 1) * half] = part[place, :rows, :]

    z, _ = norm(images[...].astype(F32))
    gain = spread_line(lines, 0, rows, me)
    shift = spread_line(lines, 1, rows, me)
    attend_bias = spread_line(lines, 2, 3 * rows, me)
    low = (z * gain + shift).astype(BF16)
    normed[...] = low
    for part in range(3):
        cols = slice(part * width, (part + 1) * width)
        value = nn(low, weight[:, cols]) + attend_bias[:, cols]
        if part == 0:
            value = value * HEAD_DIM**-0.5
        flat[:, cols] = value.astype(BF16)
    merged[:16, :] = jnp.zeros((16, width), BF16)

    def one_image(image, carry):
        start = pl.multiple_of(image * STEP, 16)
        span = flat[pl.ds(start, SPAN), :]
        chosen = select[image]
        windows[image] = nn(chosen, span).astype(BF16)
        masks = head_masks()
        rows = []
        for w in range(4):
            at = slice(w * SLOT, (w + 1) * SLOT)
            parts = []
            for g in range(BLOCKS):
                q, k, v = (
                    windows[image, at, part * width + g * LANES : part * width + (g + 1) * LANES]
                    for part in range(3)
                )
                mixing = mix(k, spread_heads(q, masks), bias[w, g])
                parts.append(pick_heads(tn(pad_keys(mixing), v), masks).astype(BF16))
            rows.append(jnp.concatenate(parts, axis=1))
        context = jnp.concatenate(rows, axis=0)
        put_span(merged, start, nn(select_t[image], context).astype(BF16))
        return carry

    lax.fori_loop(0, GROUP, one_image, 0, unroll=4)


def gelu_parts(t):
    k = 1.0 / (1.0 + (0.3275911 * 0.5**0.5) * jnp.abs(t))
    bell = jnp.exp(-0.5 * (t * t))
    poly = 0.5 * 1.061405429 * k - 0.5 * 1.453152027
    poly = poly * k + 0.5 * 1.421413741
    poly = poly * k - 0.5 * 0.284496736
    poly = poly * k + 0.5 * 0.254829592
    tail = poly * k * bell
    below = jnp.where(t >= 0, 1.0 - tail, tail)
    return t * below, below + t * (bell * 0.3989422804014327)


def sum_tiles(left, right, columns, side):
    total = None
    for tile in range(left.shape[0]):
        cols = [slice(None), slice(None)]
        cols[side] = columns
        part = tn(left[tile, :, cols[0]], right[tile, :, cols[1]])
        total = part if total is None else total + part
    return total.astype(BF16)


def put_feed_grad(ids, step, act, grad_hid, cot, normed_two, kept, sent):
    me, core, second = ids[0], ids[1], ids[2]
    members, half = kept.shape[1], kept.shape[2]
    rows = half // 2
    width = cot.shape[2]
    columns = pl.ds(pl.multiple_of(step * width, width), width)
    grad_reduce = sum_tiles(act, cot, columns, 0)
    grad_expand = sum_tiles(normed_two, grad_hid, columns, 1)
    count = width // (2 * half)
    to = pl.ds(pl.multiple_of((step % 2) * rows, rows), rows)
    for own in range(2):

        @pl.when(core == own)
        def _():
            reduce_out, expand_out = (kept, sent) if own == 0 else (sent, kept)
            for i in range(count):
                for h in range(2):
                    at = (2 * i + h) * half
                    reduce_out[h ^ second, (step * count + i) ^ me] = grad_reduce[at : at + half]
            for member in range(members):
                expand_out[(step // 2) ^ second, member ^ me, to, :] = grad_expand[
                    member * rows : (member + 1) * rows
                ]


def feed_kernel(
    ids,
    images,
    merged,
    cot,
    lines,
    near,
    far,
    near_core,
    far_core,
    place,
    place_t,
    block_out,
    grad_mid,
    narrow,
    wide,
    out_w,
    feed_kept,
    feed_sent,
    exp_w,
    red_w,
    vectors,
    cot_all,
    normed_all,
    act_all,
    grad_all,
):
    me, core = ids[0], ids[1]
    step = pl.program_id(0)
    tiles = act_all.shape[0]
    width = images.shape[1]
    held = near.shape[0]
    rows = width // (2 * held)

    @pl.when(pl.program_id(0) == 0)
    def _():
        narrow[...] = jnp.zeros_like(narrow)
        wide[...] = jnp.zeros_like(wide)
        for i, index in enumerate((3, 4, 5, 7)):
            vectors[i : i + 1, :width] = spread_line(lines, index, rows, me)
        vectors[4:5, :] = spread_line(lines, 6, 4 * rows, me)
        for own in range(2):

            @pl.when(core == own)
            def _():
                for side, parts in ((own, (near, far)), (1 - own, (near_core, far_core))):
                    for odd, part in enumerate(parts):
                        for at in range(held):
                            member = ((flip(at, held.bit_length() - 1) << 1) | odd) ^ me
                            if side == 0:
                                to = pl.ds(pl.multiple_of(member * rows, rows), rows)
                                for i in range(4):
                                    exp_w[to, i * width : (i + 1) * width] = part[
                                        at, i * rows : (i + 1) * rows, :
                                    ]
                            else:
                                to = pl.ds(pl.multiple_of(member * 4 * rows, 4 * rows), 4 * rows)
                                red_w[to, :] = part[at, : 4 * rows, :]
                            half = rows // 2
                            to = pl.ds(pl.multiple_of(member * rows + side * half, half), half)
                            out_w[to, :] = part[at, 4 * rows :, :]

    @pl.when(step < tiles)
    def _():
        middle = images[...].astype(F32) + nn(merged[...], out_w[...]) + vectors[0:1, :width]
        z, scale = norm(middle)
        scaled = vectors[1:2, :width]
        low = (z * scaled + vectors[2:3, :width]).astype(BF16)
        normed_all[step] = low
        from_grid(cot, place_t, cot_all.at[step])
        grad = cot_all[step]
        result = middle + vectors[3:4, :width]
        grad_y = jnp.zeros_like(middle)
        for c in range(exp_w.shape[1] // CHUNK):
            at = slice(c * CHUNK, (c + 1) * CHUNK)
            hidden = nn(low, exp_w[:, at]) + vectors[4:5, at]
            grad_act = nt(grad, red_w[at, :])
            active, slope = gelu_parts(hidden)
            active = active.astype(BF16)
            act_all[step, :, at] = active
            grad_h = (grad_act * slope).astype(BF16)
            grad_all[step, :, at] = grad_h
            wide[:, at] += jnp.sum(grad_h.astype(F32), axis=0, keepdims=True)
            result = result + nn(active, red_w[at, :])
            grad_y = grad_y + nt(grad_h, exp_w[:, at])
        to_grid(result.astype(BF16), place, block_out)
        wide_cot = grad.astype(F32)
        grad_middle = wide_cot + norm_back(z, scale, scaled, grad_y)
        grad_mid[...] = grad_middle
        narrow[0:1] += jnp.sum(grad_y * z, axis=0, keepdims=True)
        narrow[1:2] += jnp.sum(grad_y, axis=0, keepdims=True)
        narrow[2:3] += jnp.sum(wide_cot, axis=0, keepdims=True)
        narrow[3:4] += jnp.sum(grad_middle.astype(BF16).astype(F32), axis=0, keepdims=True)

    @pl.when(step >= tiles)
    def _():
        put_feed_grad(
            ids, step - tiles, act_all, grad_all, cot_all, normed_all, feed_kept, feed_sent
        )


def unpack_kernel(ids, attend, feed_0, feed_1, arrived, attend_w, out_w, exp_w, red_w):
    core, second = ids[1], ids[2]
    size = attend.shape[0]
    rows = size // 2
    width = attend.shape[1]

    def place(side, attend_part, feeds):
        if side == 0:
            attend_w[:, :width] = attend_part[:rows].astype(F32)
            attend_w[:, width : 2 * width] = attend_part[rows:].astype(F32)
        else:
            attend_w[:, 2 * width :] = attend_part[:rows].astype(F32)
            out_w[...] = attend_part[rows:].astype(F32)
        for h, part in enumerate(feeds):
            if side == 0:
                red_w[h * size : (h + 1) * size] = part.astype(F32)
            else:
                at = 2 * h * width
                exp_w[:, at : at + width] = part[:rows].astype(F32)
                exp_w[:, at + width : at + 2 * width] = part[rows:].astype(F32)

    for own in range(2):
        for y in range(2):

            @pl.when((core == own) & (second == y))
            def _():
                place(own, attend[...], (feed_0[...], feed_1[...])[:: 1 - 2 * y])
                parts = [arrived[i * size : (i + 1) * size, :] for i in range(3)]
                place(1 - own, parts[2], parts[:2][:: 1 - 2 * y])


def attend_back_kernel(
    ids,
    grad_mid,
    out_w,
    windows,
    normed,
    merged,
    bias,
    select,
    select_t,
    triple,
    scores,
    sums,
    attend_kept,
    attend_sent,
    flat,
    tiles,
    total,
):
    width = grad_mid.shape[1]

    @pl.when(pl.program_id(0) == 0)
    def _():
        scores[...] = jnp.zeros_like(scores)
        sums[...] = jnp.zeros_like(sums)

    low = grad_mid[...].astype(BF16)
    flat[...] = nt(low, out_w[...]).astype(BF16)
    triple[:16, :] = jnp.zeros((16, 3 * width), BF16)

    def one_image(image, carry):
        start = pl.multiple_of(image * STEP, 16)
        context = nn(select[image], flat[pl.ds(start, SPAN), :]).astype(BF16)
        masks = head_masks()
        for w in range(4):
            at = slice(w * SLOT, (w + 1) * SLOT)
            for g in range(BLOCKS):
                cols = [
                    slice(part * width + g * LANES, part * width + (g + 1) * LANES)
                    for part in range(3)
                ]
                q, k, v = (windows[image, at, c] for c in cols)
                grad_c = context[at, g * LANES : (g + 1) * LANES]
                spread_q = spread_heads(q, masks)
                spread_g = spread_heads(grad_c, masks)
                mixing = mix(k, spread_q, bias[w, g])
                grad_v = nn(pad_keys(mixing), spread_g)
                grad_m = nt(v, spread_g)[:KEYS]
                inner = jnp.sum(grad_m * mixing, axis=0, keepdims=True)
                grad_s = pad_keys(mixing * (grad_m - inner))
                scores[g] += grad_s.astype(F32)[:KEYS]
                grad_k = nn(grad_s, spread_q)
                grad_q = pick_heads(tn(grad_s, k), masks) * HEAD_DIM**-0.5
                for c, value in zip(cols, (grad_q, grad_k, grad_v)):
                    tiles[at, c] = value.astype(BF16)
        sums[...] += jnp.sum(tiles[...].astype(F32), axis=0, keepdims=True)
        put_span(triple, start, nn(select_t[image], tiles[...]).astype(BF16))
        return carry

    lax.fori_loop(0, GROUP, one_image, 0, unroll=4)
    me, core = ids[0], ids[1]
    members = attend_kept.shape[0]
    rows = attend_kept.shape[1] // 2
    last = pl.num_programs(0) - 1
    for part in range(4):
        at = slice(part * width, (part + 1) * width)
        grad = tn(normed[...], triple[:, at]) if part < 3 else tn(merged[...], low)

        @pl.when(pl.program_id(0) == 0)
        def _():
            total[:, at] = grad

        @pl.when(pl.program_id(0) > 0)
        def _():
            total[:, at] += grad

    for own in range(2):

        @pl.when((pl.program_id(0) == last) & (core == own))
        def _():
            for part in range(4):
                to = slice((part % 2) * rows, (part % 2 + 1) * rows)
                out = attend_kept if part // 2 == own else attend_sent
                for member in range(members):
                    out[member ^ me, to, :] = total[
                        member * rows : (member + 1) * rows, part * width : (part + 1) * width
                    ].astype(BF16)


def input_back_kernel(
    ids, triple, weight, images, lines, grad_mid, place, images_grad, narrow
):
    @pl.when(pl.program_id(0) == 0)
    def _():
        narrow[...] = jnp.zeros_like(narrow)

    grad_n = nt(triple[...], weight[...])
    z, scale = norm(images[...].astype(F32))
    gain = spread_line(lines, 0, lines.shape[2] // 4, ids[0])
    back = norm_back(z, scale, gain, grad_n)
    to_grid((grad_mid[...] + back).astype(BF16), place, images_grad)
    narrow[0:1] += jnp.sum(grad_n * z, axis=0, keepdims=True)
    narrow[1:2] += jnp.sum(grad_n, axis=0, keepdims=True)


def grid_rows():
    place = np.zeros((PIECE // RES * 16, PIECE), np.float32)
    for token in range(PIECE):
        place[token // RES * 16 + token % RES, token] = 1.0
    return place


def from_grid(ref, place_t, rows):
    lines = PIECE // RES
    gap = jnp.zeros((lines, 16 - RES, rows.shape[1]), BF16)
    for i in range(rows.shape[0] // PIECE):
        padded = jnp.concatenate([ref[i * lines : (i + 1) * lines], gap], axis=1)
        padded = padded.reshape(lines * 16, rows.shape[1])
        rows[i * PIECE : (i + 1) * PIECE] = nn(place_t[...], padded).astype(BF16)


def to_grid(rows, place, ref):
    lines = PIECE // RES
    for i in range(rows.shape[0] // PIECE):
        padded = nn(place[...], rows[i * PIECE : (i + 1) * PIECE]).astype(BF16)
        ref[i * lines : (i + 1) * lines] = padded.reshape(lines, 16, rows.shape[1])[:, :RES]


def whole(array):
    return pl.BlockSpec(array.shape, lambda i, ids: (0,) * array.ndim)


def once(array):
    return pl.BlockSpec(
        array.shape, lambda i, ids: (0,) * array.ndim, pipeline_mode=pl.Buffered(1)
    )


def rows_of(count, width):
    return pl.BlockSpec((count, width), lambda i, ids: (i, 0))


def call(kernel, steps, ids, args, specs, outs, out_specs, scratch=(), flops=0):
    moved = sum(a.size * a.dtype.itemsize for a in args) + sum(
        o.size * o.dtype.itemsize for o in outs
    )
    return pl.pallas_call(
        kernel,
        grid_spec=pltpu.PrefetchScalarGridSpec(
            num_scalar_prefetch=1,
            grid=(steps,),
            in_specs=specs,
            out_specs=out_specs,
            scratch_shapes=list(scratch),
        ),
        out_shape=outs,
        compiler_params=pltpu.CompilerParams(vmem_limit_bytes=VMEM),
        cost_estimate=pl.CostEstimate(flops=flops, bytes_accessed=moved, transcendentals=0),
    )(ids, *args)


def pack(kernel, ids, args, outs):
    return call(kernel, 1, ids, args, [whole(a) for a in args], outs, [whole(a) for a in outs])


def shape(dims, kind):
    return jax.ShapeDtypeStruct(dims, kind)


def window_bias(region_labels, position_index, position_table):
    across = RES // WIN
    labels = (
        region_labels.reshape(across, WIN, across, WIN).transpose(0, 2, 1, 3).reshape(-1, WIN2)
    )
    masking = jnp.where(labels[:, :, None] == labels[:, None, :], 0.0, -100.0).astype(F32)
    index = jnp.pad(
        position_index.T, ((0, KEYS - WIN2), (0, SLOT - WIN2)), constant_values=-1
    ).reshape(-1)
    onehot = (jnp.arange(position_table.shape[0], dtype=jnp.int32)[:, None] == index[None]).astype(
        BF16
    )
    looked = dot(position_table, onehot, ((0,), (0,)))
    looked = looked.reshape(BLOCKS, 4, KEYS, SLOT).transpose(0, 2, 1, 3)
    masking = jnp.pad(masking, ((0, 0), (0, KEYS - WIN2), (0, SLOT - WIN2)))
    bias = looked[None] + masking[:, None, :, None, :]
    real = lax.broadcasted_iota(jnp.int32, bias.shape, 2) < WIN2
    bias = jnp.where(real, bias, -1e30).reshape(4, BLOCKS, KEYS, 4 * SLOT)
    return bias, onehot


def bits_of(size):
    return [1 << b for b in range(size.bit_length() - 1)]


def swap(value, axis, size, bit):
    return lax.ppermute(value, axis, [(i, i ^ bit) for i in range(size)])


def after(value, *others):
    return lax.optimization_barrier((value,) + others)[0]


def take(value, axis, side):
    return lax.index_in_dim(value, side, axis, keepdims=False)


def add_up(kept, arrived):
    total = kept.astype(F32)
    for value in arrived:
        total = total + value.astype(F32)
    return total.astype(BF16)


def stack_rows(*values):
    return jnp.concatenate([v.reshape(-1, v.shape[-1]).astype(BF16) for v in values], axis=0)


def split_rows(stacked, *like):
    out, at = [], 0
    for value in like:
        size = value.size // value.shape[-1]
        out.append(stacked[at : at + size].reshape(value.shape))
        at += size
    return out


def body(fsdp, dp, *args):
    (
        images,
        input_gain,
        input_shift,
        attend_weight,
        attend_bias,
        output_weight,
        output_bias,
        second_gain,
        second_shift,
        expand_weight,
        expand_bias,
        reduce_weight,
        reduce_bias,
        position_table,
        region_labels,
        position_index,
        cotangent,
    ) = args
    count = images.shape[0]
    width = images.shape[-1]
    rows = attend_weight.shape[0]
    hidden = expand_weight.shape[1]
    tokens = count * TOKENS
    me, dp_me = lax.axis_index("fsdp"), lax.axis_index("dp")
    linear = dp_me * fsdp + me
    ids = (linear // np.array([1, fsdp, 2 * fsdp], np.int32)) % np.array([fsdp, 2, 2], np.int32)
    bits = bits_of(fsdp)
    vectors = (
        input_gain,
        input_shift,
        attend_bias,
        output_bias,
        second_gain,
        second_shift,
        expand_bias,
        reduce_bias,
    )
    widest = expand_bias.shape[0]
    small = sum(
        jnp.pad(v[None], ((i, 15 - i), (0, widest - v.shape[0]))) for i, v in enumerate(vectors)
    )
    front = pack(
        pack_front_kernel,
        ids,
        (attend_weight, small),
        (shape((rows + 16, 3 * width // 2), BF16),),
    )[0]
    rest = pack(
        pack_rest_kernel,
        ids,
        (output_weight, expand_weight, reduce_weight),
        (shape((4 * rows + rows // 2, width), BF16),),
    )[0]
    rest_stages = []
    for bit in reversed(bits):
        if len(rest_stages) > 1:
            front = after(front, rest_stages[-2])
        front = jnp.concatenate([front, swap(front, "fsdp", fsdp, bit)], axis=0)
        if bit != 1:
            rest = jnp.concatenate([rest, swap(rest, "fsdp", fsdp, bit)], axis=0)
            rest_stages.append(rest)
    grid_cot = cotangent.reshape(tokens // RES, RES, width)
    front, _, grid_cot = lax.optimization_barrier((front, rest, grid_cot))
    front_core = swap(front, "dp", dp, 1)
    near = rest
    near_core = swap(near, "dp", dp, 1)
    far = swap(near, "fsdp", fsdp, 1)
    front, front_core = (v.reshape(fsdp, rows + 16, -1) for v in (front, front_core))
    lines = front[:, rows:, :widest].transpose(1, 0, 2)

    bias, onehot = window_bias(region_labels, position_index, position_table)
    order = window_order()
    select = jnp.asarray(order, BF16)
    select_t = jnp.asarray(order.transpose(0, 2, 1), BF16)
    flat_in = images.reshape(tokens, width)
    place = jnp.asarray(grid_rows(), BF16)
    place_t = jnp.asarray(grid_rows().T, BF16)
    by_lines = pl.BlockSpec((ROWS // RES, RES, width), lambda i, ids: (i, 0, 0))

    group_rows = GROUP * TOKENS
    groups = count // GROUP
    by_group = rows_of(group_rows, width)
    win_spec = pl.BlockSpec((GROUP, 4 * SLOT, 3 * width), lambda i, ids: (i, 0, 0))
    fixed = (front, front_core, lines, bias, select, select_t)
    attend_w = shape((width, 3 * width), BF16)
    normed, windows, merged, attend_w = call(
        attend_kernel,
        groups,
        ids,
        (flat_in,) + fixed,
        [by_group] + [whole(a) for a in fixed],
        (
            shape((tokens, width), BF16),
            shape((count, 4 * SLOT, 3 * width), BF16),
            shape((tokens, width), BF16),
            attend_w,
        ),
        (by_group, win_spec, by_group, whole(attend_w)),
        (pltpu.VMEM((group_rows, 3 * width), BF16),),
        flops=12 * 10**9,
    )
    far = after(far, merged)
    far_core = swap(far, "dp", dp, 1)
    near, far, near_core, far_core = (
        v.reshape(fsdp // 2, -1, width) for v in (near, far, near_core, far_core)
    )
    by_rows = rows_of(ROWS, width)
    tiles = tokens // ROWS
    tile_rows = pl.BlockSpec((ROWS, width), lambda i, ids: (jnp.minimum(i, tiles - 1), 0))
    tile_lines = pl.BlockSpec(
        (ROWS // RES, RES, width), lambda i, ids: (jnp.minimum(i, tiles - 1), 0, 0)
    )
    fixed = (lines, near, far, near_core, far_core, place, place_t)
    sums_out = (
        shape((8, width), F32),
        shape((1, hidden), F32),
        shape((width, width), BF16),
        shape((2, fsdp, 2 * rows, width), BF16),
        shape((2, fsdp, 2 * rows, width), BF16),
    )
    block_out, grad_mid, narrow_2, wide_2, out_w, feed, feed_sent = call(
        feed_kernel,
        tiles + hidden // width,
        ids,
        (flat_in, merged, grid_cot) + fixed,
        [tile_rows, tile_rows, tile_lines] + [once(a) for a in fixed],
        (shape(grid_cot.shape, BF16), shape((tokens, width), F32)) + sums_out,
        [tile_lines, tile_rows] + [whole(a) for a in sums_out],
        (
            pltpu.VMEM((width, hidden), BF16),
            pltpu.VMEM((hidden, width), BF16),
            pltpu.VMEM((8, hidden), F32),
            pltpu.VMEM((tiles, ROWS, width), BF16),
            pltpu.VMEM((tiles, ROWS, width), BF16),
            pltpu.VMEM((tiles, ROWS, hidden), BF16),
            pltpu.VMEM((tiles, ROWS, hidden), BF16),
        ),
        flops=27 * 10**9,
    )
    feed = add_up(feed, [swap(feed_sent, "dp", dp, 1)])
    sent = feed[1]
    grad_mid = after(grad_mid, sent)
    feed = feed[0]
    feed_new = swap(sent, "dp", dp, 2)
    fixed = (bias, select, select_t)
    score_out = (
        shape((BLOCKS, KEYS, 4 * SLOT), F32),
        shape((1, 3 * width), F32),
        shape((fsdp, 2 * rows, width), BF16),
        shape((fsdp, 2 * rows, width), BF16),
    )
    triple, scores, sums, attend, attend_sent = call(
        attend_back_kernel,
        groups,
        ids,
        (grad_mid, out_w, windows, normed, merged) + fixed,
        [by_group, whole(out_w), win_spec, by_group, by_group] + [whole(a) for a in fixed],
        (shape((tokens, 3 * width), BF16),) + score_out,
        [rows_of(group_rows, 3 * width)] + [whole(a) for a in score_out],
        (
            pltpu.VMEM((group_rows, width), BF16),
            pltpu.VMEM((4 * SLOT, 3 * width), BF16),
            pltpu.VMEM((width, 4 * width), F32),
        ),
        flops=19 * 10**9,
    )
    feed_new = after(feed_new, triple)
    feed = add_up(feed, [feed_new]).reshape((2,) * len(bits) + (2 * rows, width))
    first, second = len(bits) - 1, len(bits) - 2
    sent_1 = take(feed, first, 1).astype(BF16)
    feed = take(feed, first, 0)
    attend = add_up(attend, [swap(after(attend_sent, feed_new), "dp", dp, 1)])
    attend = attend.reshape((2,) * len(bits) + attend.shape[1:])
    sent_2 = take(attend, second, 1).astype(BF16)
    attend = take(attend, second, 0)
    feed_new = swap(sent_1, "fsdp", fsdp, 1)
    attend_new = swap(sent_2, "fsdp", fsdp, 2)
    triple = after(triple, sent_1, sent_2)
    score_rows = scores.reshape(BLOCKS, KEYS, 4, SLOT).transpose(0, 2, 1, 3).reshape(HEADS, -1)
    table_grad = lax.dot_general(
        onehot.astype(F32), score_rows, (((1,), (1,)), ((), ())), precision=lax.Precision.HIGHEST
    )
    images_grad, narrow_1 = call(
        input_back_kernel,
        tokens // ROWS,
        ids,
        (triple, attend_w, flat_in, lines, grad_mid, place),
        [rows_of(ROWS, 3 * width), whole(attend_w), by_rows, whole(lines), by_rows, whole(place)],
        (shape(grid_cot.shape, BF16), sums_out[0]),
        [by_lines, whole(sums_out[0])],
        flops=3 * 10**9,
    )
    feed = add_up(feed, [after(feed_new, images_grad)])
    attend = add_up(attend, [after(attend_new, images_grad)])
    table_rows = -(-table_grad.size // width)
    table_part = jnp.pad(table_grad.reshape(-1), (0, table_rows * width - table_grad.size))
    shared = jnp.concatenate(
        [
            narrow_1[:2],
            sums.reshape(3, width),
            narrow_2[3:4],
            narrow_2[:2],
            wide_2.reshape(4, width),
            narrow_2[2:3],
            table_part.reshape(table_rows, width),
        ],
        axis=0,
    )
    shared = jnp.pad(shared, ((0, 32 - shared.shape[0]), (0, 0))).astype(BF16)

    first, second = first - 1, len(bits) - 2
    sent_1 = take(feed, first, 1)
    feed = take(feed, first, 0)
    sent_2 = take(attend, second, 1)
    attend = take(attend, second, 0)
    attend_new, shared_new = split_rows(
        swap(stack_rows(sent_2, shared), "fsdp", fsdp, 1), sent_2, shared
    )
    feed = add_up(feed, [swap(sent_1.astype(BF16), "fsdp", fsdp, 2)])
    attend = add_up(attend, [attend_new])
    shared = add_up(shared, [shared_new])
    for bit in bits[2:]:
        last = feed.ndim - 3
        sent_1, feed = take(feed, last, 1), take(feed, last, 0)
        sent_2, attend = take(attend, last, 1), take(attend, last, 0)
        feed_new, attend_new, shared_new = split_rows(
            swap(stack_rows(sent_1, sent_2, shared), "fsdp", fsdp, bit), sent_1, sent_2, shared
        )
        feed = add_up(feed, [feed_new])
        attend = add_up(attend, [attend_new])
        shared = add_up(shared, [shared_new])
    feed, attend, shared = feed.astype(BF16), attend.astype(BF16), shared.astype(BF16)
    for bit in bits_of(dp)[:0:-1]:
        feed_new, attend_new, shared_new = split_rows(
            swap(stack_rows(feed, attend, shared), "dp", dp, bit), feed, attend, shared
        )
        attend = add_up(attend, [attend_new]).astype(BF16)
        shared = add_up(shared, [shared_new]).astype(BF16)
        if bit != 2:
            feed = add_up(feed, [feed_new]).astype(BF16)
    arrived = swap(stack_rows(feed, feed_new, attend, shared), "dp", dp, 1)
    across = lax.ppermute(
        shared,
        ("dp", "fsdp"),
        [(d * fsdp + f, (d ^ 1) * fsdp + (f ^ 2)) for d in range(dp) for f in range(fsdp)],
    )
    near = swap(shared, "fsdp", fsdp, 2)
    shared = sum(v.astype(F32) for v in (shared, arrived[6 * rows :], near, across))
    grads = (
        shape((rows, 3 * width), F32),
        shape((rows, width), F32),
        shape((rows, hidden), F32),
        shape((4 * rows, width), F32),
    )
    operands = (attend, feed, feed_new, arrived)
    attend_grad, out_grad, exp_grad, red_grad = pack(unpack_kernel, ids, operands, grads)
    vector_grads = []
    at = 0
    for vector in vectors:
        size = vector.shape[0]
        count_rows = size * fsdp // width
        line = shared[at : at + count_rows].reshape(-1)
        vector_grads.append(lax.dynamic_slice_in_dim(line, me * size, size, 0))
        at += count_rows
    table_grad = shared[at : at + table_rows].reshape(-1)[: table_grad.size].reshape(
        table_grad.shape
    )
    return (
        block_out.reshape(images.shape),
        images_grad.reshape(images.shape),
        vector_grads[0],
        vector_grads[1],
        attend_grad,
        vector_grads[2],
        out_grad,
        vector_grads[3],
        vector_grads[4],
        vector_grads[5],
        exp_grad,
        vector_grads[6],
        red_grad,
        vector_grads[7],
        table_grad,
    )


def solution(mesh):
    tokens = P(("dp", "fsdp"), None, None, None)
    line, matrix = P("fsdp"), P("fsdp", None)
    weights = (line, line, matrix, line, matrix, line, line, line, matrix, line, matrix, line)
    return jax.shard_map(
        functools.partial(body, mesh.shape["fsdp"], mesh.shape["dp"]),
        mesh=mesh,
        in_specs=(tokens,) + weights + (P(), P(), P(), tokens),
        out_specs=(tokens, tokens) + weights + (P(),),
        check_vma=False,
    )
```

```python
import functools

import jax
import jax.numpy as jnp
import numpy as np
from jax import lax
from jax.experimental import pallas as pl
from jax.experimental.pallas import tpu as pltpu
from jax.sharding import PartitionSpec as P

HEADS = 16
HEAD_DIM = 32
WIN = 7
RES = 14
SHIFT = 3
WIN2 = 49
TOKENS = RES * RES
EPSILON = 1e-05
GROUP = 4
SLOT = 64
KEYS = 56
SPAN = 208
STEP = 192
BLOCKS = 4
LANES = 128
ROWS = 784
PIECE = 112
CHUNK = 1024
VMEM = 60 * 1024 * 1024
F32 = jnp.float32
BF16 = jnp.bfloat16


def window_order():
    select = np.zeros((GROUP, 4 * SLOT, SPAN), np.float32)
    for image in range(GROUP):
        for wi in range(2):
            for wj in range(2):
                for ti in range(WIN):
                    for tj in range(WIN):
                        row = (wi * 2 + wj) * SLOT + ti * WIN + tj
                        si = (wi * WIN + ti + SHIFT) % RES
                        sj = (wj * WIN + tj + SHIFT) % RES
                        select[image, row, si * RES + sj + image * (TOKENS - STEP)] = 1.0
    return select


def dot(left, right, contract):
    return lax.dot_general(left, right, (contract, ((), ())), preferred_element_type=F32)


def nn(left, right):
    return dot(left, right, ((1,), (0,)))


def nt(left, right):
    return dot(left, right, ((1,), (1,)))


def tn(left, right):
    return dot(left, right, ((0,), (0,)))


def norm(rows):
    center = rows - jnp.mean(rows, axis=-1, keepdims=True)
    spread = jnp.mean(center * center, axis=-1, keepdims=True)
    scale = lax.rsqrt(spread + EPSILON)
    return center * scale, scale


def norm_back(z, scale, gain, grad):
    g = grad * gain
    return scale * (
        g - jnp.mean(g, axis=-1, keepdims=True) - z * jnp.mean(g * z, axis=-1, keepdims=True)
    )


def head_masks():
    lane = lax.broadcasted_iota(jnp.int32, (SLOT, LANES), 1)
    return [(lane // HEAD_DIM) == j for j in range(4)]


def spread_heads(rows, masks):
    zero = jnp.zeros_like(rows)
    return jnp.concatenate([jnp.where(mask, rows, zero) for mask in masks], axis=0)


def pick_heads(wide, masks):
    total = jnp.where(masks[0], wide[:SLOT], 0.0)
    for j in range(1, 4):
        total = jnp.where(masks[j], wide[j * SLOT : (j + 1) * SLOT], total)
    return total


def pad_keys(rows):
    return jnp.concatenate([rows, jnp.zeros((SLOT - KEYS, rows.shape[1]), F32)], axis=0).astype(
        BF16
    )


def mix(keys, spread_q, bias):
    scores = nt(keys, spread_q)[:KEYS] + bias
    top = jnp.max(scores, axis=0, keepdims=True)
    raised = jnp.exp(scores - top)
    return raised * (1.0 / jnp.sum(raised, axis=0, keepdims=True))


def put_span(ref, start, value, columns=slice(None)):
    head = pl.ds(start, 16)
    tail = pl.ds(pl.multiple_of(start + 16, 16), SPAN - 16)
    ref[head, columns] = ref[head, columns] + value[:16]
    ref[tail, columns] = value[16:]


def pack_front_kernel(ids, attend, vectors, front):
    rows = attend.shape[0]
    half = attend.shape[1] // 2
    front[rows:, :] = jnp.zeros((16, half), BF16)
    front[rows:, : vectors.shape[1]] = vectors[...]
    for core in range(2):

        @pl.when(ids[1] == core)
        def _():
            front[:rows, :] = attend[:, core * half : (core + 1) * half]


def pack_rest_kernel(ids, output, expand, reduce, rest):
    rows, width = output.shape
    for core in range(2):

        @pl.when(ids[1] == core)
        def _():
            if core == 0:
                for i in range(4):
                    rest[i * rows : (i + 1) * rows] = expand[:, i * width : (i + 1) * width]
            else:
                rest[: 4 * rows] = reduce[...]
            rest[4 * rows :] = output[core * (rows // 2) : (core + 1) * (rows // 2)]


def spread_line(lines, index, size, me):
    members = lines.shape[1]
    bits = members.bit_length() - 1
    piece = lines[index][:, :size]
    column = lax.broadcasted_iota(jnp.int32, (size, members * size), 1)
    inside = lax.broadcasted_iota(jnp.int32, (size, members * size), 0)
    wide = nn(piece, (column % size == inside).astype(BF16))
    place = lax.broadcasted_iota(jnp.int32, wide.shape, 0)
    flipped = sum(((place >> b) & 1) << (bits - 1 - b) for b in range(bits))
    owner = lax.broadcasted_iota(jnp.int32, wide.shape, 1) // size
    return jnp.sum(jnp.where(owner == (flipped ^ me), wide, 0.0), axis=0, keepdims=True)


def flip(place, bits):
    return sum(((place >> b) & 1) << (bits - 1 - b) for b in range(bits))


def attend_kernel(
    ids, images, mine, other, lines, bias, select, select_t, normed, windows, merged, weight, flat
):
    width = images.shape[1]
    me, core = ids[0], ids[1]
    members = mine.shape[0]
    rows = width // members

    @pl.when(pl.program_id(0) == 0)
    def _():
        half = mine.shape[2]
        for own in range(2):

            @pl.when(core == own)
            def _():
                for side, part in ((own, mine), (1 - own, other)):
                    for place in range(members):
                        member = flip(place, members.bit_length() - 1) ^ me
                        at = pl.ds(pl.multiple_of(member * rows, rows), rows)
                        weight[at, side * half : (side + 1) * half] = part[place, :rows, :]

    z, _ = norm(images[...].astype(F32))
    gain = spread_line(lines, 0, rows, me)
    shift = spread_line(lines, 1, rows, me)
    attend_bias = spread_line(lines, 2, 3 * rows, me)
    low = (z * gain + shift).astype(BF16)
    normed[...] = low
    for part in range(3):
        cols = slice(part * width, (part + 1) * width)
        value = nn(low, weight[:, cols]) + attend_bias[:, cols]
        if part == 0:
            value = value * HEAD_DIM**-0.5
        flat[:, cols] = value.astype(BF16)
    merged[:16, :] = jnp.zeros((16, width), BF16)

    def one_image(image, carry):
        start = pl.multiple_of(image * STEP, 16)
        span = flat[pl.ds(start, SPAN), :]
        chosen = select[image]
        windows[image] = nn(chosen, span).astype(BF16)
        masks = head_masks()
        rows = []
        for w in range(4):
            at = slice(w * SLOT, (w + 1) * SLOT)
            parts = []
            for g in range(BLOCKS):
                q, k, v = (
                    windows[image, at, part * width + g * LANES : part * width + (g + 1) * LANES]
                    for part in range(3)
                )
                mixing = mix(k, spread_heads(q, masks), bias[w, g])
                parts.append(pick_heads(tn(pad_keys(mixing), v), masks).astype(BF16))
            rows.append(jnp.concatenate(parts, axis=1))
        context = jnp.concatenate(rows, axis=0)
        put_span(merged, start, nn(select_t[image], context).astype(BF16))
        return carry

    lax.fori_loop(0, GROUP, one_image, 0, unroll=4)


def gelu_parts(t):
    k = 1.0 / (1.0 + (0.3275911 * 0.5**0.5) * jnp.abs(t))
    bell = jnp.exp(-0.5 * (t * t))
    poly = 0.5 * 1.061405429 * k - 0.5 * 1.453152027
    poly = poly * k + 0.5 * 1.421413741
    poly = poly * k - 0.5 * 0.284496736
    poly = poly * k + 0.5 * 0.254829592
    tail = poly * k * bell
    below = jnp.where(t >= 0, 1.0 - tail, tail)
    return t * below, below + t * (bell * 0.3989422804014327)


def sum_tiles(left, right, columns, side):
    total = None
    for tile in range(left.shape[0]):
        cols = [slice(None), slice(None)]
        cols[side] = columns
        part = tn(left[tile, :, cols[0]], right[tile, :, cols[1]])
        total = part if total is None else total + part
    return total.astype(BF16)


def put_feed_grad(ids, step, act, grad_hid, cot, normed_two, kept, sent):
    me, core, second = ids[0], ids[1], ids[2]
    members, half = kept.shape[1], kept.shape[2]
    rows = half // 2
    width = cot.shape[2]
    columns = pl.ds(pl.multiple_of(step * width, width), width)
    grad_reduce = sum_tiles(act, cot, columns, 0)
    grad_expand = sum_tiles(normed_two, grad_hid, columns, 1)
    count = width // (2 * half)
    to = pl.ds(pl.multiple_of((step % 2) * rows, rows), rows)
    for own in range(2):

        @pl.when(core == own)
        def _():
            reduce_out, expand_out = (kept, sent) if own == 0 else (sent, kept)
            for i in range(count):
                for h in range(2):
                    at = (2 * i + h) * half
                    reduce_out[h ^ second, (step * count + i) ^ me] = grad_reduce[at : at + half]
            for member in range(members):
                expand_out[(step // 2) ^ second, member ^ me, to, :] = grad_expand[
                    member * rows : (member + 1) * rows
                ]


def feed_kernel(
    ids,
    images,
    merged,
    cot,
    lines,
    near,
    far,
    near_core,
    far_core,
    place,
    place_t,
    block_out,
    grad_mid,
    narrow,
    wide,
    out_w,
    feed_kept,
    feed_sent,
    exp_w,
    red_w,
    vectors,
    cot_all,
    normed_all,
    act_all,
    grad_all,
):
    me, core = ids[0], ids[1]
    step = pl.program_id(0)
    tiles = act_all.shape[0]
    width = images.shape[1]
    held = near.shape[0]
    rows = width // (2 * held)

    @pl.when(pl.program_id(0) == 0)
    def _():
        narrow[...] = jnp.zeros_like(narrow)
        wide[...] = jnp.zeros_like(wide)
        for i, index in enumerate((3, 4, 5, 7)):
            vectors[i : i + 1, :width] = spread_line(lines, index, rows, me)
        vectors[4:5, :] = spread_line(lines, 6, 4 * rows, me)
        for own in range(2):

            @pl.when(core == own)
            def _():
                for side, parts in ((own, (near, far)), (1 - own, (near_core, far_core))):
                    for odd, part in enumerate(parts):
                        for at in range(held):
                            member = ((flip(at, held.bit_length() - 1) << 1) | odd) ^ me
                            if side == 0:
                                to = pl.ds(pl.multiple_of(member * rows, rows), rows)
                                for i in range(4):
                                    exp_w[to, i * width : (i + 1) * width] = part[
                                        at, i * rows : (i + 1) * rows, :
                                    ]
                            else:
                                to = pl.ds(pl.multiple_of(member * 4 * rows, 4 * rows), 4 * rows)
                                red_w[to, :] = part[at, : 4 * rows, :]
                            half = rows // 2
                            to = pl.ds(pl.multiple_of(member * rows + side * half, half), half)
                            out_w[to, :] = part[at, 4 * rows :, :]

    @pl.when(step < tiles)
    def _():
        middle = images[...].astype(F32) + nn(merged[...], out_w[...]) + vectors[0:1, :width]
        z, scale = norm(middle)
        scaled = vectors[1:2, :width]
        low = (z * scaled + vectors[2:3, :width]).astype(BF16)
        normed_all[step] = low
        from_grid(cot, place_t, cot_all.at[step])
        grad = cot_all[step]
        result = middle + vectors[3:4, :width]
        grad_y = jnp.zeros_like(middle)
        for c in range(exp_w.shape[1] // CHUNK):
            at = slice(c * CHUNK, (c + 1) * CHUNK)
            hidden = nn(low, exp_w[:, at]) + vectors[4:5, at]
            grad_act = nt(grad, red_w[at, :])
            active, slope = gelu_parts(hidden)
            active = active.astype(BF16)
            act_all[step, :, at] = active
            grad_h = (grad_act * slope).astype(BF16)
            grad_all[step, :, at] = grad_h
            wide[:, at] += jnp.sum(grad_h.astype(F32), axis=0, keepdims=True)
            result = result + nn(active, red_w[at, :])
            grad_y = grad_y + nt(grad_h, exp_w[:, at])
        to_grid(result.astype(BF16), place, block_out)
        wide_cot = grad.astype(F32)
        grad_middle = wide_cot + norm_back(z, scale, scaled, grad_y)
        grad_mid[...] = grad_middle
        narrow[0:1] += jnp.sum(grad_y * z, axis=0, keepdims=True)
        narrow[1:2] += jnp.sum(grad_y, axis=0, keepdims=True)
        narrow[2:3] += jnp.sum(wide_cot, axis=0, keepdims=True)
        narrow[3:4] += jnp.sum(grad_middle.astype(BF16).astype(F32), axis=0, keepdims=True)

    @pl.when(step >= tiles)
    def _():
        put_feed_grad(
            ids, step - tiles, act_all, grad_all, cot_all, normed_all, feed_kept, feed_sent
        )


def unpack_kernel(ids, attend, feed_0, feed_1, arrived, attend_w, out_w, exp_w, red_w):
    core, second = ids[1], ids[2]
    size = attend.shape[0]
    rows = size // 2
    width = attend.shape[1]

    def place(side, attend_part, feeds):
        if side == 0:
            attend_w[:, :width] = attend_part[:rows].astype(F32)
            attend_w[:, width : 2 * width] = attend_part[rows:].astype(F32)
        else:
            attend_w[:, 2 * width :] = attend_part[:rows].astype(F32)
            out_w[...] = attend_part[rows:].astype(F32)
        for h, part in enumerate(feeds):
            if side == 0:
                red_w[h * size : (h + 1) * size] = part.astype(F32)
            else:
                at = 2 * h * width
                exp_w[:, at : at + width] = part[:rows].astype(F32)
                exp_w[:, at + width : at + 2 * width] = part[rows:].astype(F32)

    for own in range(2):
        for y in range(2):

            @pl.when((core == own) & (second == y))
            def _():
                place(own, attend[...], (feed_0[...], feed_1[...])[:: 1 - 2 * y])
                parts = [arrived[i * size : (i + 1) * size, :] for i in range(3)]
                place(1 - own, parts[2], parts[:2][:: 1 - 2 * y])


def attend_back_kernel(
    ids,
    grad_mid,
    out_w,
    windows,
    normed,
    merged,
    bias,
    select,
    select_t,
    triple,
    scores,
    sums,
    attend_kept,
    attend_sent,
    flat,
    tiles,
    total,
):
    width = grad_mid.shape[1]

    @pl.when(pl.program_id(0) == 0)
    def _():
        scores[...] = jnp.zeros_like(scores)
        sums[...] = jnp.zeros_like(sums)

    low = grad_mid[...].astype(BF16)
    flat[...] = nt(low, out_w[...]).astype(BF16)
    triple[:16, :] = jnp.zeros((16, 3 * width), BF16)

    def one_image(image, carry):
        start = pl.multiple_of(image * STEP, 16)
        context = nn(select[image], flat[pl.ds(start, SPAN), :]).astype(BF16)
        masks = head_masks()
        for w in range(4):
            at = slice(w * SLOT, (w + 1) * SLOT)
            for g in range(BLOCKS):
                cols = [
                    slice(part * width + g * LANES, part * width + (g + 1) * LANES)
                    for part in range(3)
                ]
                q, k, v = (windows[image, at, c] for c in cols)
                grad_c = context[at, g * LANES : (g + 1) * LANES]
                spread_q = spread_heads(q, masks)
                spread_g = spread_heads(grad_c, masks)
                mixing = mix(k, spread_q, bias[w, g])
                grad_v = nn(pad_keys(mixing), spread_g)
                grad_m = nt(v, spread_g)[:KEYS]
                inner = jnp.sum(grad_m * mixing, axis=0, keepdims=True)
                grad_s = pad_keys(mixing * (grad_m - inner))
                scores[g] += grad_s.astype(F32)[:KEYS]
                grad_k = nn(grad_s, spread_q)
                grad_q = pick_heads(tn(grad_s, k), masks) * HEAD_DIM**-0.5
                for c, value in zip(cols, (grad_q, grad_k, grad_v)):
                    tiles[at, c] = value.astype(BF16)
        sums[...] += jnp.sum(tiles[...].astype(F32), axis=0, keepdims=True)
        put_span(triple, start, nn(select_t[image], tiles[...]).astype(BF16))
        return carry

    lax.fori_loop(0, GROUP, one_image, 0, unroll=4)
    me, core = ids[0], ids[1]
    members = attend_kept.shape[0]
    rows = attend_kept.shape[1] // 2
    last = pl.num_programs(0) - 1
    for part in range(4):
        at = slice(part * width, (part + 1) * width)
        grad = tn(normed[...], triple[:, at]) if part < 3 else tn(merged[...], low)

        @pl.when(pl.program_id(0) == 0)
        def _():
            total[:, at] = grad

        @pl.when(pl.program_id(0) > 0)
        def _():
            total[:, at] += grad

    for own in range(2):

        @pl.when((pl.program_id(0) == last) & (core == own))
        def _():
            for part in range(4):
                to = slice((part % 2) * rows, (part % 2 + 1) * rows)
                out = attend_kept if part // 2 == own else attend_sent
                for member in range(members):
                    out[member ^ me, to, :] = total[
                        member * rows : (member + 1) * rows, part * width : (part + 1) * width
                    ].astype(BF16)


def input_back_kernel(
    ids, triple, weight, images, lines, grad_mid, place, images_grad, narrow
):
    @pl.when(pl.program_id(0) == 0)
    def _():
        narrow[...] = jnp.zeros_like(narrow)

    grad_n = nt(triple[...], weight[...])
    z, scale = norm(images[...].astype(F32))
    gain = spread_line(lines, 0, lines.shape[2] // 4, ids[0])
    back = norm_back(z, scale, gain, grad_n)
    to_grid((grad_mid[...] + back).astype(BF16), place, images_grad)
    narrow[0:1] += jnp.sum(grad_n * z, axis=0, keepdims=True)
    narrow[1:2] += jnp.sum(grad_n, axis=0, keepdims=True)


def grid_rows():
    place = np.zeros((PIECE // RES * 16, PIECE), np.float32)
    for token in range(PIECE):
        place[token // RES * 16 + token % RES, token] = 1.0
    return place


def from_grid(ref, place_t, rows):
    lines = PIECE // RES
    gap = jnp.zeros((lines, 16 - RES, rows.shape[1]), BF16)
    for i in range(rows.shape[0] // PIECE):
        padded = jnp.concatenate([ref[i * lines : (i + 1) * lines], gap], axis=1)
        padded = padded.reshape(lines * 16, rows.shape[1])
        rows[i * PIECE : (i + 1) * PIECE] = nn(place_t[...], padded).astype(BF16)


def to_grid(rows, place, ref):
    lines = PIECE // RES
    for i in range(rows.shape[0] // PIECE):
        padded = nn(place[...], rows[i * PIECE : (i + 1) * PIECE]).astype(BF16)
        ref[i * lines : (i + 1) * lines] = padded.reshape(lines, 16, rows.shape[1])[:, :RES]


def whole(array):
    return pl.BlockSpec(array.shape, lambda i, ids: (0,) * array.ndim)


def once(array):
    return pl.BlockSpec(
        array.shape, lambda i, ids: (0,) * array.ndim, pipeline_mode=pl.Buffered(1)
    )


def rows_of(count, width):
    return pl.BlockSpec((count, width), lambda i, ids: (i, 0))


def call(kernel, steps, ids, args, specs, outs, out_specs, scratch=(), flops=0):
    moved = sum(a.size * a.dtype.itemsize for a in args) + sum(
        o.size * o.dtype.itemsize for o in outs
    )
    return pl.pallas_call(
        kernel,
        grid_spec=pltpu.PrefetchScalarGridSpec(
            num_scalar_prefetch=1,
            grid=(steps,),
            in_specs=specs,
            out_specs=out_specs,
            scratch_shapes=list(scratch),
        ),
        out_shape=outs,
        compiler_params=pltpu.CompilerParams(vmem_limit_bytes=VMEM),
        cost_estimate=pl.CostEstimate(flops=flops, bytes_accessed=moved, transcendentals=0),
    )(ids, *args)


def pack(kernel, ids, args, outs):
    return call(kernel, 1, ids, args, [whole(a) for a in args], outs, [whole(a) for a in outs])


def shape(dims, kind):
    return jax.ShapeDtypeStruct(dims, kind)


def window_bias(region_labels, position_index, position_table):
    across = RES // WIN
    labels = (
        region_labels.reshape(across, WIN, across, WIN).transpose(0, 2, 1, 3).reshape(-1, WIN2)
    )
    masking = jnp.where(labels[:, :, None] == labels[:, None, :], 0.0, -100.0).astype(F32)
    index = jnp.pad(
        position_index.T, ((0, KEYS - WIN2), (0, SLOT - WIN2)), constant_values=-1
    ).reshape(-1)
    onehot = (jnp.arange(position_table.shape[0], dtype=jnp.int32)[:, None] == index[None]).astype(
        BF16
    )
    looked = dot(position_table, onehot, ((0,), (0,)))
    looked = looked.reshape(BLOCKS, 4, KEYS, SLOT).transpose(0, 2, 1, 3)
    masking = jnp.pad(masking, ((0, 0), (0, KEYS - WIN2), (0, SLOT - WIN2)))
    bias = looked[None] + masking[:, None, :, None, :]
    real = lax.broadcasted_iota(jnp.int32, bias.shape, 2) < WIN2
    bias = jnp.where(real, bias, -1e30).reshape(4, BLOCKS, KEYS, 4 * SLOT)
    return bias, onehot


def bits_of(size):
    return [1 << b for b in range(size.bit_length() - 1)]


def swap(value, axis, size, bit):
    return lax.ppermute(value, axis, [(i, i ^ bit) for i in range(size)])


def after(value, *others):
    return lax.optimization_barrier((value,) + others)[0]


def take(value, axis, side):
    return lax.index_in_dim(value, side, axis, keepdims=False)


def add_up(kept, arrived):
    total = kept.astype(F32)
    for value in arrived:
        total = total + value.astype(F32)
    return total.astype(BF16)


def stack_rows(*values):
    return jnp.concatenate([v.reshape(-1, v.shape[-1]).astype(BF16) for v in values], axis=0)


def split_rows(stacked, *like):
    out, at = [], 0
    for value in like:
        size = value.size // value.shape[-1]
        out.append(stacked[at : at + size].reshape(value.shape))
        at += size
    return out


def body(fsdp, dp, *args):
    (
        images,
        input_gain,
        input_shift,
        attend_weight,
        attend_bias,
        output_weight,
        output_bias,
        second_gain,
        second_shift,
        expand_weight,
        expand_bias,
        reduce_weight,
        reduce_bias,
        position_table,
        region_labels,
        position_index,
        cotangent,
    ) = args
    count = images.shape[0]
    width = images.shape[-1]
    rows = attend_weight.shape[0]
    hidden = expand_weight.shape[1]
    tokens = count * TOKENS
    me, dp_me = lax.axis_index("fsdp"), lax.axis_index("dp")
    linear = dp_me * fsdp + me
    ids = (linear // np.array([1, fsdp, 2 * fsdp], np.int32)) % np.array([fsdp, 2, 2], np.int32)
    bits = bits_of(fsdp)
    vectors = (
        input_gain,
        input_shift,
        attend_bias,
        output_bias,
        second_gain,
        second_shift,
        expand_bias,
        reduce_bias,
    )
    widest = expand_bias.shape[0]
    small = sum(
        jnp.pad(v[None], ((i, 15 - i), (0, widest - v.shape[0]))) for i, v in enumerate(vectors)
    )
    front = pack(
        pack_front_kernel,
        ids,
        (attend_weight, small),
        (shape((rows + 16, 3 * width // 2), BF16),),
    )[0]
    rest = pack(
        pack_rest_kernel,
        ids,
        (output_weight, expand_weight, reduce_weight),
        (shape((4 * rows + rows // 2, width), BF16),),
    )[0]
    rest_stages = []
    for bit in reversed(bits):
        if len(rest_stages) > 1:
            front = after(front, rest_stages[-2])
        front = jnp.concatenate([front, swap(front, "fsdp", fsdp, bit)], axis=0)
        if bit != 1:
            rest = jnp.concatenate([rest, swap(rest, "fsdp", fsdp, bit)], axis=0)
            rest_stages.append(rest)
    grid_cot = cotangent.reshape(tokens // RES, RES, width)
    front, _, grid_cot = lax.optimization_barrier((front, rest, grid_cot))
    front_core = swap(front, "dp", dp, 1)
    near = rest
    near_core = swap(near, "dp", dp, 1)
    far = swap(near, "fsdp", fsdp, 1)
    front, front_core = (v.reshape(fsdp, rows + 16, -1) for v in (front, front_core))
    lines = front[:, rows:, :widest].transpose(1, 0, 2)

    bias, onehot = window_bias(region_labels, position_index, position_table)
    order = window_order()
    select = jnp.asarray(order, BF16)
    select_t = jnp.asarray(order.transpose(0, 2, 1), BF16)
    flat_in = images.reshape(tokens, width)
    place = jnp.asarray(grid_rows(), BF16)
    place_t = jnp.asarray(grid_rows().T, BF16)
    by_lines = pl.BlockSpec((ROWS // RES, RES, width), lambda i, ids: (i, 0, 0))

    group_rows = GROUP * TOKENS
    groups = count // GROUP
    by_group = rows_of(group_rows, width)
    win_spec = pl.BlockSpec((GROUP, 4 * SLOT, 3 * width), lambda i, ids: (i, 0, 0))
    fixed = (front, front_core, lines, bias, select, select_t)
    attend_w = shape((width, 3 * width), BF16)
    normed, windows, merged, attend_w = call(
        attend_kernel,
        groups,
        ids,
        (flat_in,) + fixed,
        [by_group] + [whole(a) for a in fixed],
        (
            shape((tokens, width), BF16),
            shape((count, 4 * SLOT, 3 * width), BF16),
            shape((tokens, width), BF16),
            attend_w,
        ),
        (by_group, win_spec, by_group, whole(attend_w)),
        (pltpu.VMEM((group_rows, 3 * width), BF16),),
        flops=12 * 10**9,
    )
    far = after(far, merged)
    far_core = swap(far, "dp", dp, 1)
    near, far, near_core, far_core = (
        v.reshape(fsdp // 2, -1, width) for v in (near, far, near_core, far_core)
    )
    by_rows = rows_of(ROWS, width)
    tiles = tokens // ROWS
    tile_rows = pl.BlockSpec((ROWS, width), lambda i, ids: (jnp.minimum(i, tiles - 1), 0))
    tile_lines = pl.BlockSpec(
        (ROWS // RES, RES, width), lambda i, ids: (jnp.minimum(i, tiles - 1), 0, 0)
    )
    fixed = (lines, near, far, near_core, far_core, place, place_t)
    sums_out = (
        shape((8, width), F32),
        shape((1, hidden), F32),
        shape((width, width), BF16),
        shape((2, fsdp, 2 * rows, width), BF16),
        shape((2, fsdp, 2 * rows, width), BF16),
    )
    block_out, grad_mid, narrow_2, wide_2, out_w, feed, feed_sent = call(
        feed_kernel,
        tiles + hidden // width,
        ids,
        (flat_in, merged, grid_cot) + fixed,
        [tile_rows, tile_rows, tile_lines] + [once(a) for a in fixed],
        (shape(grid_cot.shape, BF16), shape((tokens, width), F32)) + sums_out,
        [tile_lines, tile_rows] + [whole(a) for a in sums_out],
        (
            pltpu.VMEM((width, hidden), BF16),
            pltpu.VMEM((hidden, width), BF16),
            pltpu.VMEM((8, hidden), F32),
            pltpu.VMEM((tiles, ROWS, width), BF16),
            pltpu.VMEM((tiles, ROWS, width), BF16),
            pltpu.VMEM((tiles, ROWS, hidden), BF16),
            pltpu.VMEM((tiles, ROWS, hidden), BF16),
        ),
        flops=27 * 10**9,
    )
    arrived = swap(feed_sent, "dp", dp, 1)
    sent = add_up(feed[1], [arrived[1]])
    feed = add_up(feed[0], [arrived[0]])
    grad_mid = after(grad_mid, sent)
    feed_new = swap(sent, "dp", dp, 2)
    fixed = (bias, select, select_t)
    score_out = (
        shape((BLOCKS, KEYS, 4 * SLOT), F32),
        shape((1, 3 * width), F32),
        shape((fsdp, 2 * rows, width), BF16),
        shape((fsdp, 2 * rows, width), BF16),
    )
    triple, scores, sums, attend, attend_sent = call(
        attend_back_kernel,
        groups,
        ids,
        (grad_mid, out_w, windows, normed, merged) + fixed,
        [by_group, whole(out_w), win_spec, by_group, by_group] + [whole(a) for a in fixed],
        (shape((tokens, 3 * width), BF16),) + score_out,
        [rows_of(group_rows, 3 * width)] + [whole(a) for a in score_out],
        (
            pltpu.VMEM((group_rows, width), BF16),
            pltpu.VMEM((4 * SLOT, 3 * width), BF16),
            pltpu.VMEM((width, 4 * width), F32),
        ),
        flops=19 * 10**9,
    )
    feed_new = after(feed_new, triple)
    feed = add_up(feed, [feed_new]).reshape((2,) * len(bits) + (2 * rows, width))
    first, second = len(bits) - 1, len(bits) - 2
    sent_1 = take(feed, first, 1).astype(BF16)
    feed = take(feed, first, 0)
    attend = add_up(attend, [swap(after(attend_sent, feed_new), "dp", dp, 1)])
    attend = attend.reshape((2,) * len(bits) + attend.shape[1:])
    sent_2 = take(attend, second, 1).astype(BF16)
    attend = take(attend, second, 0)
    feed_new = swap(sent_1, "fsdp", fsdp, 1)
    attend_new = swap(sent_2, "fsdp", fsdp, 2)
    triple = after(triple, sent_1, sent_2)
    score_rows = scores.reshape(BLOCKS, KEYS, 4, SLOT).transpose(0, 2, 1, 3).reshape(HEADS, -1)
    table_grad = lax.dot_general(
        onehot.astype(F32), score_rows, (((1,), (1,)), ((), ())), precision=lax.Precision.HIGHEST
    )
    images_grad, narrow_1 = call(
        input_back_kernel,
        tokens // ROWS,
        ids,
        (triple, attend_w, flat_in, lines, grad_mid, place),
        [rows_of(ROWS, 3 * width), whole(attend_w), by_rows, whole(lines), by_rows, whole(place)],
        (shape(grid_cot.shape, BF16), sums_out[0]),
        [by_lines, whole(sums_out[0])],
        flops=3 * 10**9,
    )
    feed = add_up(feed, [after(feed_new, images_grad)])
    attend = add_up(attend, [after(attend_new, images_grad)])
    table_rows = -(-table_grad.size // width)
    table_part = jnp.pad(table_grad.reshape(-1), (0, table_rows * width - table_grad.size))
    shared = jnp.concatenate(
        [
            narrow_1[:2],
            sums.reshape(3, width),
            narrow_2[3:4],
            narrow_2[:2],
            wide_2.reshape(4, width),
            narrow_2[2:3],
            table_part.reshape(table_rows, width),
        ],
        axis=0,
    )
    shared = jnp.pad(shared, ((0, 32 - shared.shape[0]), (0, 0))).astype(BF16)

    first, second = first - 1, len(bits) - 2
    sent_1 = take(feed, first, 1)
    feed = take(feed, first, 0)
    sent_2 = take(attend, second, 1)
    attend = take(attend, second, 0)
    attend_new, shared_new = split_rows(
        swap(stack_rows(sent_2, shared), "fsdp", fsdp, 1), sent_2, shared
    )
    feed = add_up(feed, [swap(sent_1.astype(BF16), "fsdp", fsdp, 2)])
    attend = add_up(attend, [attend_new])
    shared = add_up(shared, [shared_new])
    for bit in bits[2:]:
        last = feed.ndim - 3
        sent_1, feed = take(feed, last, 1), take(feed, last, 0)
        sent_2, attend = take(attend, last, 1), take(attend, last, 0)
        feed_new, attend_new, shared_new = split_rows(
            swap(stack_rows(sent_1, sent_2, shared), "fsdp", fsdp, bit), sent_1, sent_2, shared
        )
        feed = add_up(feed, [feed_new])
        attend = add_up(attend, [attend_new])
        shared = add_up(shared, [shared_new])
    feed, attend, shared = feed.astype(BF16), attend.astype(BF16), shared.astype(BF16)
    for bit in bits_of(dp)[:0:-1]:
        feed_new, attend_new, shared_new = split_rows(
            swap(stack_rows(feed, attend, shared), "dp", dp, bit), feed, attend, shared
        )
        attend = add_up(attend, [attend_new]).astype(BF16)
        shared = add_up(shared, [shared_new]).astype(BF16)
        if bit != 2:
            feed = add_up(feed, [feed_new]).astype(BF16)
    arrived = swap(stack_rows(feed, feed_new, attend, shared), "dp", dp, 1)
    across = lax.ppermute(
        shared,
        ("dp", "fsdp"),
        [(d * fsdp + f, (d ^ 1) * fsdp + (f ^ 2)) for d in range(dp) for f in range(fsdp)],
    )
    near = swap(shared, "fsdp", fsdp, 2)
    shared = sum(v.astype(F32) for v in (shared, arrived[6 * rows :], near, across))
    grads = (
        shape((rows, 3 * width), F32),
        shape((rows, width), F32),
        shape((rows, hidden), F32),
        shape((4 * rows, width), F32),
    )
    operands = (attend, feed, feed_new, arrived)
    attend_grad, out_grad, exp_grad, red_grad = pack(unpack_kernel, ids, operands, grads)
    vector_grads = []
    at = 0
    for vector in vectors:
        size = vector.shape[0]
        count_rows = size * fsdp // width
        line = shared[at : at + count_rows].reshape(-1)
        vector_grads.append(lax.dynamic_slice_in_dim(line, me * size, size, 0))
        at += count_rows
    table_grad = shared[at : at + table_rows].reshape(-1)[: table_grad.size].reshape(
        table_grad.shape
    )
    return (
        block_out.reshape(images.shape),
        images_grad.reshape(images.shape),
        vector_grads[0],
        vector_grads[1],
        attend_grad,
        vector_grads[2],
        out_grad,
        vector_grads[3],
        vector_grads[4],
        vector_grads[5],
        exp_grad,
        vector_grads[6],
        red_grad,
        vector_grads[7],
        table_grad,
    )


def solution(mesh):
    tokens = P(("dp", "fsdp"), None, None, None)
    line, matrix = P("fsdp"), P("fsdp", None)
    weights = (line, line, matrix, line, matrix, line, line, line, matrix, line, matrix, line)
    return jax.shard_map(
        functools.partial(body, mesh.shape["fsdp"], mesh.shape["dp"]),
        mesh=mesh,
        in_specs=(tokens,) + weights + (P(), P(), P(), tokens),
        out_specs=(tokens, tokens) + weights + (P(),),
        check_vma=False,
    )
```
